32 devices in a mesh: rows: 8 (over z, y), heads: 4 (over x, core).
Axes of the slice: x: 2, y: 2, z: 4, core: 2. Of those that a mesh axis runs over, the one named last changes fastest.
Arguments:
- atom_states: float32 [4096, 768], P('rows'), may hold values from -6 to 6
- time_steps: int32 [4096], P('rows'), may hold values from 0 to 999
- coords: float32 [3, 4096], P(None, 'rows'), may hold values from -4.75 to 4.75
- item_ids: int32 [8, 512], P('rows'), may hold values from 0 to 15, never falling along the last dimension, each value on 1 to 384 neighbouring positions
- w_time: bfloat16 [256, 768], replicated, may hold values from -0.375 to 0.375
- ln1_gain: float32 [768], replicated, may hold values from 0.5 to 1.5
- ln1_bias: float32 [768], replicated, may hold values from -1 to 1
- w_qkv: bfloat16 [768, 32, 3, 24], P(None, 'heads'), may hold values from -0.21875 to 0.21875
- w_kernel: bfloat16 [128, 32], P(None, 'heads'), may hold values from -1.5 to 1.5
- kernel_means: float32 [128], replicated, may hold values from 0 to 8
- kernel_widths: float32 [128], replicated, may hold values from 0.12 to 0.5
- w_out: bfloat16 [32, 24, 768], P('heads'), may hold values from -1 to 1
- ln2_gain: float32 [768], replicated, may hold values from 0.5 to 1.5
- ln2_bias: float32 [768], replicated, may hold values from -1 to 1
- w_up: bfloat16 [768, 3072], P(None, 'heads'), may hold values from -0.21875 to 0.21875
- w_down: bfloat16 [3072, 768], P('heads'), may hold values from -0.109375 to 0.109375
- w_force: bfloat16 [3, 768], replicated, may hold values from -0.21875 to 0.21875
- cot_states: float32 [4096, 768], P('rows'), may hold values from -6 to 6
- cot_forces: float32 [3, 4096], P(None, 'rows'), may hold values from -6 to 6
Outputs:
- states_out: float32 [4096, 768], P('rows')
- forces: float32 [3, 4096], P(None, 'rows')
- grad_states: float32 [4096, 768], P('rows')
- grad_w_time: float32 [256, 768], replicated
- grad_ln1_gain: float32 [768], replicated
- grad_ln1_bias: float32 [768], replicated
- grad_w_qkv: float32 [768, 32, 3, 24], P(None, 'heads')
- grad_w_kernel: float32 [128, 32], P(None, 'heads')
- grad_kernel_means: float32 [128], replicated
- grad_kernel_widths: float32 [128], replicated
- grad_w_out: float32 [32, 24, 768], P('heads')
- grad_ln2_gain: float32 [768], replicated
- grad_ln2_bias: float32 [768], replicated
- grad_w_up: float32 [768, 3072], P(None, 'heads')
- grad_w_down: float32 [3072, 768], P('heads')
- grad_w_force: float32 [3, 768], replicated
The draws below stay inside these ranges and needn't reach their ends.
Inputs may be any that keep to these rules, and one draw needn't show every extreme that they name: `item_ids`: item numbers start at 0 and never fall along a pack; items never cross packs; an item has 1 to 384 atoms and some item has exactly 384.
All inputs are finite; a program needn't handle non-finite values.
Results may differ from the reference program's by a relative error of at most 0.02.
Values may be sent and summed in bfloat16 or wider, within the bound.
A program may use at most 128 MiB of HBM per device.

```python
import math
import jax
import jax.numpy as jnp
import numpy as np
from jax import lax

D = 768
HEADS = 32
HEAD_DIM = 24
FF = 3072
KERNELS = 128
TFREQ = 256
BLOCK_ROWS = 64
ITEMS = 16
TOK_DEV = 512
LONGEST = 384
PACKS = 8
ATOMS = 4096
N_ROWS = 8


def draw_coords(key, part):
    key = jax.random.fold_in(key, 17)
    site_key, shift_key = jax.random.split(key)
    lattice = jax.random.randint(site_key, (3, ATOMS), -3, 4).astype(jnp.float32)
    jitter = jnp.clip(0.08 * jax.random.normal(shift_key, (3, ATOMS), jnp.float32), -0.25, 0.25)
    return (1.5 * lattice + jitter).astype(jnp.float32)


def with_ends(array, stream_key, least, top_value):
    dims = array.shape
    spot = [jax.random.randint(jax.random.fold_in(stream_key, axis), (), 0, dims[axis]) for axis in range(len(dims))]
    array = array.at[tuple(spot)].set(least)
    longest = dims.index(max(dims))
    spot[longest] = (spot[longest] + 1) % dims[longest]
    return array.at[tuple(spot)].set(top_value)


def shard_levels(own_key, dims, cuts, low, largest):
    level = 1.0
    for dim, parts in cuts:
        steps = jax.random.uniform(jax.random.fold_in(jax.random.fold_in(own_key, 6), dim), (parts,), jnp.float32, low / len(cuts), largest / len(cuts))
        level = level * jnp.repeat(jnp.exp(steps), dims[dim] // parts).reshape((-1,) + (1,) * (len(dims) - 1 - dim))
    return level


def profile(amount, total, limit, skew):
    portions = [(1 << 20) // math.isqrt(rank ** skew) + 1 for rank in range(2, amount + 1)]
    spare, counts = total - limit - (amount - 1), [1] * (amount - 1)
    while spare > 0:
        free = [i for i in range(amount - 1) if counts[i] < limit]
        mass, remaining = sum([portions[i] for i in free]), spare
        for i in free:
            extra = min(limit - counts[i], max(1, remaining * portions[i] // mass), spare)
            counts[i] = counts[i] + extra
            spare = spare - extra
    return np.array([limit] + counts)


def ragged(rng, count, total, most, slope):
    if count == 2:
        one = jax.random.randint(rng, (), max(1, total - most), min(most, total - 1) + 1)
        return jnp.stack([one, total - one])
    sizes = jnp.asarray(profile(count, total, most, slope), jnp.int32)
    twos = (count - 1) // 2
    donor, sink = sizes[1:1 + 2 * twos:2], sizes[2:2 + 2 * twos:2]
    room = jnp.minimum(donor - 1, most - sink)
    passed = jax.random.randint(jax.random.fold_in(rng, 1), (twos,), 0, 1 << 20) % (room + 1)
    sizes = sizes.at[1:1 + 2 * twos:2].set(donor - passed).at[2:2 + 2 * twos:2].set(sink + passed)
    return sizes[jax.random.permutation(jax.random.fold_in(rng, 2), count)]


def gaussian(key, shape, width, bound, pieces=(), kind=jnp.bfloat16):
    level = shard_levels(key, shape, pieces, -0.22, 0.18) if pieces else 1.0
    entries = jax.random.normal(key, shape, jnp.float32) * width * level
    return jnp.minimum(jnp.maximum(entries, -bound), bound).astype(kind)


def setup_inputs(seed: int = 0) -> dict:
    keys = jax.random.split(jax.random.key(seed), 20)
    atom_states = gaussian(keys[0], (ATOMS, D), 1.0, 6.0, ((0, 8),), jnp.float32)
    time_steps = with_ends(jax.random.randint(keys[1], (ATOMS,), 0, 1000), jax.random.fold_in(keys[1], 1), 0, 999).astype(jnp.int32)
    coords = draw_coords(jax.random.fold_in(keys[19], 71), 0)
    item_ids = jax.vmap(lambda own: jnp.searchsorted(jnp.cumsum(ragged(own, ITEMS, TOK_DEV, LONGEST, 2)), jnp.arange(TOK_DEV), side="right"))(jax.random.split(keys[3], PACKS)).reshape((PACKS, TOK_DEV)).astype(jnp.int32)
    w_time = gaussian(keys[4], (TFREQ, D), TFREQ ** -0.5, 0.375)
    ln1_gain = jnp.clip(1.0 + 0.1 * jax.random.normal(keys[5], (D,), jnp.float32), 0.5, 1.5)
    ln1_bias = gaussian(keys[6], (D,), 0.2, 1.0, (), jnp.float32)
    w_qkv = gaussian(keys[7], (D, HEADS, 3, HEAD_DIM), D ** -0.5, 0.21875, ((1, 4),))
    w_kernel = gaussian(keys[8], (KERNELS, HEADS), (KERNELS // 8) ** -0.5, 1.5, ((1, 4),))
    kernel_means = jnp.clip(jax.random.uniform(keys[9], (KERNELS,), jnp.float32, 0.0, 8.0), 0.0, 8.0)
    kernel_widths = jnp.clip(jnp.exp(jax.random.uniform(keys[10], (KERNELS,), jnp.float32, math.log(0.12), math.log(0.5))), 0.12, 0.5)
    w_out = gaussian(keys[11], (HEADS, HEAD_DIM, D), (D // 24) ** -0.5, 1.0, ((0, 4),))
    ln2_gain = jnp.clip(1.0 + 0.1 * jax.random.normal(keys[12], (D,), jnp.float32), 0.5, 1.5)
    ln2_bias = gaussian(keys[13], (D,), 0.2, 1.0, (), jnp.float32)
    w_up = gaussian(keys[14], (D, FF), D ** -0.5, 0.21875, ((1, 4),))
    w_down = gaussian(keys[15], (FF, D), FF ** -0.5, 0.109375, ((0, 4),))
    w_force = gaussian(keys[16], (3, D), D ** -0.5, 0.21875)
    cot_states = gaussian(keys[17], (ATOMS, D), 1.0, 6.0, ((0, 8),), jnp.float32)
    cot_forces = gaussian(keys[18], (3, ATOMS), 1.0, 6.0, ((1, 8),), jnp.float32)
    return dict(atom_states=atom_states, time_steps=time_steps, coords=coords, item_ids=item_ids, w_time=w_time, ln1_gain=ln1_gain, ln1_bias=ln1_bias, w_qkv=w_qkv, w_kernel=w_kernel, kernel_means=kernel_means, kernel_widths=kernel_widths, w_out=w_out, ln2_gain=ln2_gain, ln2_bias=ln2_bias, w_up=w_up, w_down=w_down, w_force=w_force, cot_states=cot_states, cot_forces=cot_forces)


@jax.custom_vjp
def low(v):
    return lax.optimization_barrier(v.astype(jnp.bfloat16)).astype(jnp.float32)

@jax.custom_vjp
def low_back(v):
    return v

def low_keep(v):
    return (low(v), None)

def low_pass(kept, grad):
    return (grad,)

def back_keep(v):
    return (v, None)

def back_low(kept, grad):
    return (low(grad),)
low.defvjp(low_keep, low_pass)
low_back.defvjp(back_keep, back_low)
epsilon = 1e-05
highest = lax.Precision.HIGHEST

def matmul(left_side, right_side):
    return jnp.dot(left_side, right_side, precision=highest)

def layer_norm(values, scale_gain, shift_bias):
    center = lax.optimization_barrier(jnp.mean(values, axis=-1, keepdims=True))
    centered = values - center
    spread = lax.optimization_barrier(jnp.mean(centered * centered, axis=-1, keepdims=True))
    return centered * lax.rsqrt(spread + epsilon) * scale_gain + shift_bias

def time_features(time_index):
    half_width = TFREQ // 2
    frequency = jnp.exp(-math.log(10000.0) * jnp.arange(half_width, dtype=jnp.float32) / half_width)
    angles = time_index.astype(jnp.float32)[:, None] * frequency[None, :]
    return jnp.concatenate([jnp.sin(angles), jnp.cos(angles)], axis=1)

def slot_order(values):
    columns = values.shape[-1]
    shaped = values.reshape(N_ROWS, TOK_DEV // N_ROWS, N_ROWS, columns)
    return jnp.transpose(shaped, (2, 1, 0, 3)).reshape(ATOMS, columns)

def bias_block(query_xyz, coords_pack, centres, widths, kernel_weight):
    deltas = query_xyz[:, :, None] - coords_pack[:, None, :]
    distance = jnp.sqrt(lax.optimization_barrier(jnp.sum(deltas * deltas, axis=0)))
    scaled = (distance[:, :, None] - centres) / widths
    kernels = jnp.exp(-0.5 * scaled * scaled) / (widths * math.sqrt(2.0 * math.pi))
    mixed = jnp.einsum('qkc,ch->hqk', low(kernels), kernel_weight, precision=highest)
    return low_back(mixed)

def pair_bias(coords_pack, centres, widths, kernel_weight):
    width_atoms = coords_pack.shape[1]
    blocks = width_atoms // BLOCK_ROWS
    queries = jnp.transpose(coords_pack.reshape(3, blocks, BLOCK_ROWS), (1, 0, 2))

    def one_block(query_xyz):
        return bias_block(query_xyz, coords_pack, centres, widths, kernel_weight)
    stacked = lax.map(jax.checkpoint(one_block), queries)
    heads_here = kernel_weight.shape[1]
    return jnp.transpose(stacked, (1, 0, 2, 3)).reshape(heads_here, width_atoms, width_atoms)

def attend_given(qkv_flat, pair_terms, item_row):
    heads_here = pair_terms.shape[0]
    width_atoms = qkv_flat.shape[0]
    head_width = qkv_flat.shape[1] // (3 * heads_here)
    shaped = qkv_flat.reshape(width_atoms, heads_here, 3, head_width)
    query_part = shaped[:, :, 0, :]
    key_part = shaped[:, :, 1, :]
    value_part = shaped[:, :, 2, :]
    raw_scores = jnp.einsum('qhd,khd->hqk', query_part, key_part, precision=highest)
    logits = low_back(raw_scores) / math.sqrt(head_width) + pair_terms
    same_item = item_row[:, None] == item_row[None, :]
    logits = jnp.where(same_item[None, :, :], logits, -1e+30)
    row_top = lax.optimization_barrier(jnp.max(logits, axis=2, keepdims=True))
    weights = jnp.exp(logits - row_top)
    attention = weights / lax.optimization_barrier(jnp.sum(weights, axis=2, keepdims=True))
    context = jnp.einsum('hqk,khd->qhd', low(attention), value_part, precision=highest)
    return low_back(low(context)).reshape(width_atoms, heads_here * head_width)

def reference(atom_states, time_steps, coords, item_ids, w_time, ln1_gain, ln1_bias, w_qkv, w_kernel, kernel_means, kernel_widths, w_out, ln2_gain, ln2_bias, w_up, w_down, w_force, cot_states, cot_forces):
    time_terms = low(time_features(time_steps))
    coord_packs = jnp.transpose(coords.reshape(3, PACKS, TOK_DEV), (1, 0, 2))

    def layer_forward(states_in, weight_time, gain_one, shift_one, weight_qkv, weight_kernel, centres, widths, weight_out, gain_two, shift_two, weight_up, weight_down, weight_force):
        state_zero = states_in + low_back(matmul(time_terms, weight_time))
        normed_one = low(layer_norm(state_zero, gain_one, shift_one))
        qkv_values = low_back(low(matmul(normed_one, weight_qkv.reshape(D, 3 * D))))
        qkv_packs = slot_order(qkv_values).reshape(PACKS, TOK_DEV, 3 * D)

        def one_pack(pack_inputs):
            qkv_pack, item_row, coords_pack = pack_inputs
            return attend_given(qkv_pack, pair_bias(coords_pack, centres, widths, weight_kernel), item_row)
        context = lax.map(jax.checkpoint(one_pack), (qkv_packs, item_ids, coord_packs))
        context = slot_order(context.reshape(ATOMS, D))
        state_one = state_zero + low_back(matmul(context, weight_out.reshape(D, D)))
        normed_two = low(layer_norm(state_one, gain_two, shift_two))
        pre_act = low_back(matmul(normed_two, weight_up))
        hidden = low(jax.nn.gelu(pre_act, approximate=False))
        state_two = state_one + low_back(matmul(hidden, weight_down))
        forces = low_back(matmul(weight_force, low(state_two).T))
        return (state_two, forces)
    outputs, backward = jax.vjp(layer_forward, atom_states, w_time.astype(jnp.float32), ln1_gain, ln1_bias, w_qkv.astype(jnp.float32), w_kernel.astype(jnp.float32), kernel_means, kernel_widths, w_out.astype(jnp.float32), ln2_gain, ln2_bias, w_up.astype(jnp.float32), w_down.astype(jnp.float32), w_force.astype(jnp.float32))
    grads = backward((cot_states, cot_forces))
    return (outputs[0], outputs[1], grads[0], grads[1], grads[2], grads[3], grads[4], grads[5], grads[6], grads[7], grads[8], grads[9], grads[10], grads[11], grads[12], grads[13])
```

```python
import math

import jax
import jax.numpy as jnp
from jax import lax
from jax.experimental import pallas as pl
from jax.experimental.pallas import tpu as pltpu
from jax.sharding import PartitionSpec as P

LOG2E = math.log2(math.e)
CENTRE = 4.0
LANES = 128
PAD = 32
bf16, f32 = jnp.bfloat16, jnp.float32
UNROLL_F = (2, 2, 4, 8)
UNROLL_B = (2, 2, 4, 8)


def dot(a, b):
    return lax.dot_general(a, b, (((1,), (0,)), ((), ())), preferred_element_type=f32)


def dot_nt(a, b):
    return lax.dot_general(a, b, (((1,), (1,)), ((), ())), preferred_element_type=f32)


def head_mask(h, width):
    lane = lax.broadcasted_iota(jnp.int32, (1, width), 1)
    return jnp.where(lane // PAD == h, 1.0, 0.0).astype(bf16)


def gauss_coefs(means, widths, coef):
    inv = 1.0 / (widths * widths)
    shift = means - CENTRE
    half = 0.5 * LOG2E * inv
    coef[0] = jnp.broadcast_to(-half, coef.shape[1:])
    coef[1] = jnp.broadcast_to(2.0 * half * shift, coef.shape[1:])
    norm = -jnp.log(widths * math.sqrt(2.0 * math.pi)) * LOG2E
    coef[2] = jnp.broadcast_to(norm - half * shift * shift, coef.shape[1:])


def distances(row0, aux, coords, first, width):
    total = None
    for axis in range(3):
        delta = aux[pl.ds(row0, 8), axis : axis + 1] - coords[axis : axis + 1, first : first + width]
        total = delta * delta if total is None else total + delta * delta
    return jnp.sqrt(total) - CENTRE


def gauss_value(dist, coef, row, cols):
    kernels = coef.shape[1]
    rows = []
    for piece in range(kernels // 16):
        ks = slice(piece * 16, piece * 16 + 16)
        c0, c1, c2 = coef[0, ks, :], coef[1, ks, :], coef[2, ks, :]
        line = []
        for lane in range(cols.start, cols.stop, LANES):
            d = dist[row : row + 1, lane : lane + LANES]
            line.append(jnp.exp2((d * c0 + c1) * d + c2).astype(bf16))
        rows.append(jnp.concatenate(line, axis=1) if len(line) > 1 else line[0])
    return jnp.concatenate(rows, axis=0)


def chunks(width, step):
    return [slice(at, min(at + step, width)) for at in range(0, width, step)]


def spread_weights(wk_t):
    zero = jnp.zeros_like(wk_t)
    return jnp.concatenate([jnp.concatenate([wk_t, zero], 1), jnp.concatenate([zero, wk_t], 1)], 0).astype(bf16)


def pair_phase(aux, coords, ids, coef, dist, pair, spread, heads, atoms):
    tiles = atoms // LANES
    for tile in range(tiles):
        first, width = tile * LANES, atoms - tile * LANES

        def unit(group, carry):
            row0 = pl.multiple_of(first + group * 8, 8)
            dist[:, :width] = distances(row0, aux, coords, first, width)
            same = aux[pl.ds(row0, 8), 3:4] == ids[0:1, first:]
            mask = jnp.where(same, 0.0, -1e30)
            for two in range(4):
                at = pl.ds(pl.multiple_of((row0 + 2 * two) * heads, 2 * heads), 2 * heads)
                for cols in chunks(width, 2 * LANES):
                    g = jnp.concatenate([gauss_value(dist, coef, 2 * two + i, cols) for i in range(2)], 0)
                    terms = dot(spread[...], g) * LOG2E
                    for lane in range(cols.start, cols.stop, LANES):
                        bar = jnp.concatenate([jnp.broadcast_to(mask[2 * two + i : 2 * two + i + 1, lane : lane + LANES], (heads, LANES)) for i in range(2)], 0)
                        pair[tile + lane // LANES, at, :] = terms[:, lane - cols.start : lane - cols.start + LANES] + bar
            return carry

        lax.fori_loop(0, LANES // 8, unit, 0, unroll=UNROLL_F[tile % 4])


def mirror(ref, h, heads, tiles, add):
    for lo in range(tiles):
        for hi in range(lo + 1, tiles):
            near = pl.ds(lo * LANES * heads + h, LANES, stride=heads)
            far = pl.ds(hi * LANES * heads + h, LANES, stride=heads)
            if add:
                ref[hi, near, :] = ref[hi, near, :] + jnp.transpose(ref[lo, far, :])
            else:
                ref[lo, far, :] = jnp.transpose(ref[hi, near, :])


def soft_phase(pair, qt, k, vt, att_out, ctx_out, buf0, buf1, heads, atoms):
    tiles = atoms // LANES
    scale = LOG2E / math.sqrt(24)

    def raw(h, buf):
        buf[...] = dot(k[...] * head_mask(h, k.shape[1]), qt[...])

    def soften(h, buf):
        rows = pl.ds(pl.multiple_of(h * PAD, PAD), PAD)
        for tile in range(tiles):
            cols = slice(tile * LANES, (tile + 1) * LANES)
            logits = buf[:, cols] * scale + pair[tile, pl.ds(h, atoms, stride=heads), :]
            weights = jnp.exp2(logits - jnp.max(logits, axis=0, keepdims=True))
            soft = weights * (1.0 / jnp.sum(weights, axis=0, keepdims=True))
            att_out[h, :, cols] = soft.astype(bf16)
        ctx_out[rows, :] = dot(vt[rows, :], att_out[h]).astype(bf16)

    raw(0, buf0)

    def step(i, carry):
        h = 2 * i
        mirror(pair, h, heads, tiles, False)
        raw(h + 1, buf1)
        soften(h, buf0)
        mirror(pair, h + 1, heads, tiles, False)
        raw(jnp.minimum(h + 2, heads - 1), buf0)
        soften(h + 1, buf1)
        return carry

    lax.fori_loop(0, heads // 2, step, 0)


def attend_kernel(aux, coords, ids, wk_t, means, widths, qt, k, vt, att_out, ctx_out, coef, dist, pair, spread, buf0, buf1):
    heads, atoms = att_out.shape[0], att_out.shape[1]
    gauss_coefs(means[...], widths[...], coef)
    spread[...] = spread_weights(wk_t[...].astype(f32))
    pair_phase(aux, coords, ids, coef, dist, pair, spread, heads, atoms)
    soft_phase(pair, qt, k, vt, att_out, ctx_out, buf0, buf1, heads, atoms)


def pieces_of(x):
    a = x.astype(bf16).astype(f32)
    r = x - a
    b = r.astype(bf16).astype(f32)
    return a, b, r - b


def score_phase(att, q, kt, v, dc, dct, term, score0, score1, buf0, buf1, dqt_out, dk_sum, dv_sum, heads, atoms):
    tiles = atoms // LANES
    scale = 1.0 / math.sqrt(24)
    dk_sum[...] = jnp.zeros_like(dk_sum)
    dv_sum[...] = jnp.zeros_like(dv_sum)

    def raw(h, buf):
        buf[...] = dot(v[...] * head_mask(h, v.shape[1]), dct[...])

    def grads(h, buf, score):
        mask = head_mask(h, v.shape[1])
        rows = pl.ds(pl.multiple_of(h * PAD, PAD), PAD)
        for tile in range(tiles):
            cols = slice(tile * LANES, (tile + 1) * LANES)
            soft = att[h, :, cols].astype(f32)
            part = soft * buf[:, cols]
            grad = part - soft * jnp.sum(part, axis=0, keepdims=True)
            score[:, cols] = (grad * scale).astype(bf16)
            term[tile, pl.ds(h, atoms, stride=heads), :] = grad.astype(bf16).astype(f32)
        dqt_out[rows, :] = dot(kt[rows, :], score[...]).astype(bf16)
        dv_sum[...] += dot(att[h], dc[...] * mask)
        dk_sum[...] += dot(score[...], q[...] * mask)
        mirror(term, h, heads, tiles, True)

    raw(0, buf0)

    def step(i, carry):
        h = 2 * i
        raw(h + 1, buf1)
        grads(h, buf0, score0)
        raw(jnp.minimum(h + 2, heads - 1), buf0)
        grads(h + 1, buf1, score1)
        return carry

    lax.fori_loop(0, heads // 2, step, 0)


def moment_phase(aux, coords, coef, dist, term, moments, heads, atoms):
    tiles = atoms // LANES
    moments[...] = jnp.zeros_like(moments)
    for tile in range(tiles):
        first, width = tile * LANES, atoms - tile * LANES

        def unit(group, carry):
            row0 = pl.multiple_of(first + group * 8, 8)
            dist[:, :width] = distances(row0, aux, coords, first, width)
            total = None
            for row in range(8):
                at = pl.ds(pl.multiple_of((row0 + row) * heads, heads), heads)
                for cols in chunks(width, 2 * LANES):
                    lhs = []
                    for lane in range(cols.start, cols.stop, LANES):
                        t = term[tile + lane // LANES, at, :].astype(bf16).astype(f32)
                        d = dist[row : row + 1, lane : lane + LANES]
                        x1 = t * d
                        parts = (t,) + pieces_of(x1) + pieces_of(x1 * d) + (jnp.zeros_like(t),)
                        lhs.append(jnp.concatenate(parts, axis=0).astype(bf16))
                    lhs = jnp.concatenate(lhs, axis=1) if len(lhs) > 1 else lhs[0]
                    out = dot_nt(gauss_value(dist, coef, row, cols), lhs)
                    total = out if total is None else total + out
            moments[...] += total
            return carry

        lax.fori_loop(0, LANES // 8, unit, 0, unroll=UNROLL_B[tile % 4])


def kernel_grads(moments, means, widths, wk_t, dwk_out, dmean_out, dwidth_out, heads):
    kernels = wk_t.shape[1]
    flat = jnp.transpose(jnp.concatenate([moments[...], jnp.zeros((kernels, LANES - moments.shape[1]), f32)], axis=1)) if moments.shape[1] < LANES else jnp.transpose(moments[...])
    m = [flat[i * heads : (i + 1) * heads] for i in range(7)]
    m0, m1, m2 = m[0], m[1] + m[2] + m[3], m[4] + m[5] + m[6]
    shift, sigma = means[...] - CENTRE, widths[...]
    m_t, s_t = jnp.transpose(jnp.broadcast_to(shift, (kernels, LANES)))[:1], jnp.transpose(jnp.broadcast_to(sigma, (kernels, LANES)))[:1]
    w = wk_t[...].astype(f32)
    s1 = m1 - m_t * m0
    s2 = m2 - 2.0 * m_t * m1 + m_t * m_t * m0
    dwk_out[...] = m0
    dmean_out[...] = jnp.sum(w * s1, axis=0, keepdims=True) / (s_t * s_t)
    dwidth_out[...] = jnp.sum(w * (s2 / (s_t * s_t) - m0), axis=0, keepdims=True) / s_t


def attend_back_kernel(aux, coords, wk_t, means, widths, att, q, kt, v, dc, dct,
                       dqt_out, dk_out, dv_out, dwk_out, dmean_out, dwidth_out,
                       coef, dist, term, score0, score1, buf0, buf1, moments, dk_sum, dv_sum):
    heads, atoms = att.shape[0], att.shape[1]
    score_phase(att, q, kt, v, dc, dct, term, score0, score1, buf0, buf1, dqt_out, dk_sum, dv_sum, heads, atoms)
    dk_out[...] = dk_sum[...].astype(bf16)
    dv_out[...] = dv_sum[...].astype(bf16)
    gauss_coefs(means[...], widths[...], coef)
    moment_phase(aux, coords, coef, dist, term, moments, heads, atoms)
    kernel_grads(moments, means, widths, wk_t, dwk_out, dmean_out, dwidth_out, heads)


VM = pl.BlockSpec(memory_space=pltpu.VMEM)


def attend(aux, coords, ids, wk_t, means, widths, qt, k, vt):
    atoms, heads, kernels = aux.shape[0], wk_t.shape[0], wk_t.shape[1]
    return pl.pallas_call(
        attend_kernel,
        out_shape=(jax.ShapeDtypeStruct((heads, atoms, atoms), bf16), jax.ShapeDtypeStruct((heads * PAD, atoms), bf16)),
        in_specs=[VM] * 9, out_specs=(VM, VM),
        scratch_shapes=[pltpu.VMEM((3, kernels, LANES), f32), pltpu.VMEM((8, atoms), f32),
                        pltpu.VMEM((atoms // LANES, atoms * heads, LANES), f32),
                        pltpu.VMEM((heads * 2, 2 * kernels), bf16), pltpu.VMEM((atoms, atoms), f32), pltpu.VMEM((atoms, atoms), f32)],
        name="attend",
        compiler_params=pltpu.CompilerParams(vmem_limit_bytes=50 << 20),
    )(aux, coords, ids, wk_t, means, widths, qt, k, vt)


def attend_back(aux, coords, wk_t, means, widths, att, q, kt, v, dc, dct):
    atoms, heads, kernels = aux.shape[0], wk_t.shape[0], wk_t.shape[1]
    wide = heads * PAD
    S = jax.ShapeDtypeStruct
    return pl.pallas_call(
        attend_back_kernel,
        out_shape=(S((wide, atoms), bf16), S((atoms, wide), bf16), S((atoms, wide), bf16),
                   S((heads, kernels), f32), S((1, kernels), f32), S((1, kernels), f32)),
        in_specs=[VM] * 11, out_specs=(VM,) * 6,
        scratch_shapes=[pltpu.VMEM((3, kernels, LANES), f32), pltpu.VMEM((8, atoms), f32),
                        pltpu.VMEM((atoms // LANES, atoms * heads, LANES), f32),
                        pltpu.VMEM((atoms, atoms), bf16), pltpu.VMEM((atoms, atoms), bf16),
                        pltpu.VMEM((atoms, atoms), f32), pltpu.VMEM((atoms, atoms), f32),
                        pltpu.VMEM((kernels, 8 * heads), f32),
                        pltpu.VMEM((atoms, wide), f32), pltpu.VMEM((atoms, wide), f32)],
        name="attend_back",
        compiler_params=pltpu.CompilerParams(vmem_limit_bytes=50 << 20),
    )(aux, coords, wk_t, means, widths, att, q, kt, v, dc, dct)

TFREQ = 256
BLOCK_ROWS = 64


epsilon = 1e-05


def as_sent(value):

    def short(part):
        return part.astype(jnp.bfloat16) if part.dtype == jnp.float32 else part

    return jax.tree.map(short, value)


def round_value(v):
    return lax.optimization_barrier(v.astype(jnp.bfloat16)).astype(jnp.float32)


def round_keep(v):
    return (round_value(v), None)


def round_pass(kept, grad):
    return (grad,)


def pass_value(v):
    return v


def back_keep(v):
    return (v, None)


def back_round(kept, grad):
    return (round_value(grad),)


def low(v):
    rounder = jax.custom_vjp(round_value)
    rounder.defvjp(round_keep, round_pass)
    return rounder(v)


def low_back(v):
    passer = jax.custom_vjp(pass_value)
    passer.defvjp(back_keep, back_round)
    return passer(v)


def layer_norm(values, scale_gain, shift_bias):
    center = jnp.mean(values, axis=-1, keepdims=True)
    centered = values - center
    spread = jnp.mean(centered * centered, axis=-1, keepdims=True)
    return centered * lax.rsqrt(spread + epsilon) * scale_gain + shift_bias


def norm_round(values, scale_gain, shift_bias):
    return low(layer_norm(values, scale_gain, shift_bias))


def time_features(time_index):
    half_width = TFREQ // 2
    frequency = jnp.exp(-math.log(10000.0) * jnp.arange(half_width, dtype=jnp.float32) / half_width)
    angles = time_index.astype(jnp.float32)[:, None] * frequency[None, :]
    return jnp.concatenate([jnp.sin(angles), jnp.cos(angles)], axis=1)


def project_out(context, weight_out):
    flat_weight = weight_out.reshape(-1, weight_out.shape[-1])
    return low_back(jnp.dot(context, flat_weight))


def feed_forward(normed, weight_up, weight_down):
    pre_act = low_back(jnp.dot(normed, weight_up))
    hidden = low(jax.nn.gelu(pre_act, approximate=False))
    return low_back(jnp.dot(hidden, weight_down))


def force_head(states, weight_force):
    return low_back(jnp.dot(weight_force, low(states).T))


def split_rows(values, peer_count):
    return values.reshape(values.shape[0] // peer_count, peer_count, values.shape[1])


def join_rows(values):
    return values.reshape(values.shape[0] * values.shape[1], values.shape[2])


def body(
    atom_states,
    time_steps,
    coords,
    item_ids,
    w_time,
    ln1_gain,
    ln1_bias,
    w_qkv,
    w_kernel,
    kernel_means,
    kernel_widths,
    w_out,
    ln2_gain,
    ln2_bias,
    w_up,
    w_down,
    w_force,
    cot_states,
    cot_forces,
):
    peer_count = lax.axis_size("rows")
    item_row = item_ids[0]
    time_terms = low(time_features(time_steps))
    weight_time = w_time.astype(jnp.float32)
    heads = w_kernel.shape[1]
    head_dim = w_qkv.shape[3]
    width = w_qkv.shape[0]
    padded = jnp.pad(jnp.transpose(w_qkv, (2, 1, 3, 0)), ((0, 0), (0, 0), (0, PAD - head_dim), (0, 0)))
    weight_q, weight_k, weight_v = padded.reshape(3, heads * PAD, width)
    aux = jnp.concatenate([coords.T, item_ids.astype(jnp.float32).T], axis=1)
    ids = item_ids.astype(jnp.float32)
    wk_t, centres, spreads = w_kernel.T, kernel_means[:, None], kernel_widths[:, None]
    weight_out = w_out.astype(jnp.float32)
    weight_up = w_up.astype(jnp.float32)
    weight_down = w_down.astype(jnp.float32)
    weight_force = w_force.astype(jnp.float32)

    def time_branch(states_in, weight):
        return states_in + low_back(jnp.dot(time_terms, weight))

    state_zero, time_backward = jax.vjp(time_branch, atom_states, weight_time)
    normed_one, norm_one_backward = jax.vjp(norm_round, state_zero, ln1_gain, ln1_bias)
    normed_rows = join_rows(
        lax.all_to_all(
            as_sent(split_rows(normed_one.astype(jnp.bfloat16), peer_count)),
            "rows",
            split_axis=1,
            concat_axis=1,
            tiled=True,
        )
    )
    q_t, k_t, v_t = [dot_nt(weight, normed_rows).astype(bf16) for weight in (weight_q, weight_k, weight_v)]
    q_r, k_r, v_r = [dot_nt(normed_rows, weight).astype(bf16) for weight in (weight_q, weight_k, weight_v)]
    soft, context_t = attend(aux, coords, ids, wk_t, centres, spreads, q_t, k_r, v_t)
    atoms = normed_rows.shape[0]
    context = context_t.T.reshape(atoms, heads, PAD)[:, :, :head_dim].reshape(atoms, heads * head_dim).astype(f32)
    partial_rows, out_backward = jax.vjp(project_out, context, weight_out)
    attn_partial = join_rows(
        lax.all_to_all(
            split_rows(partial_rows, peer_count), "rows", split_axis=1, concat_axis=1, tiled=True
        )
    )
    state_one = state_zero + lax.psum(attn_partial, "heads")
    normed_two, norm_two_backward = jax.vjp(norm_round, state_one, ln2_gain, ln2_bias)
    ffn_partial, ffn_backward = jax.vjp(feed_forward, normed_two, weight_up, weight_down)
    state_two = state_one + jax.tree.map(
        lambda part: part.astype(jnp.float32), lax.psum(as_sent(ffn_partial), "heads")
    )
    forces, force_backward = jax.vjp(force_head, state_two, weight_force)
    force_state_grad, dweight_force = force_backward(cot_forces)
    grad_two = cot_states + force_state_grad
    normed_two_part, dweight_up, dweight_down = ffn_backward(grad_two)
    normed_two_grad = lax.psum(normed_two_part, "heads")
    norm_two_state_grad, dgain_two, dshift_two = norm_two_backward(normed_two_grad)
    grad_one = grad_two + norm_two_state_grad
    gain_part = jnp.zeros_like(ln2_gain)
    shift_part = jnp.zeros_like(ln2_bias)
    grad_rows = join_rows(
        lax.all_to_all(
            split_rows(grad_one.astype(jnp.bfloat16), peer_count),
            "rows",
            split_axis=1,
            concat_axis=1,
            tiled=True,
        )
    ).astype(jnp.float32)
    context_grad, dweight_out = out_backward(grad_rows)
    context_grad = jnp.pad(
        context_grad.astype(bf16).reshape(atoms, heads, head_dim), ((0, 0), (0, 0), (0, PAD - head_dim))
    ).reshape(atoms, heads * PAD)
    dq_t, dk, dv, dwk_t, centre_grad, width_grad = attend_back(
        aux, coords, wk_t, centres, spreads, soft, q_r, k_t, v_r, context_grad, context_grad.T
    )
    dq = dq_t.T
    normed_rows_grad = dot(dq, weight_q) + dot(dk, weight_k) + dot(dv, weight_v)
    dweight_qkv = jnp.stack([dot(grad.T, normed_rows).reshape(heads, PAD, width)[:, :head_dim] for grad in (dq, dk, dv)], axis=1)
    dweight_qkv = jnp.transpose(dweight_qkv, (3, 0, 1, 2))
    dweight_kernel, centre_grad, width_grad = dwk_t.T, centre_grad[0], width_grad[0]
    normed_one_part = join_rows(
        lax.all_to_all(
            as_sent(split_rows(normed_rows_grad, peer_count)),
            "rows",
            split_axis=1,
            concat_axis=1,
            tiled=True,
        )
    )
    normed_one_grad, centre_grad, width_grad, gain_total, shift_total = (
        lax.psum(normed_one_part.astype(jnp.bfloat16), "heads").astype(jnp.float32),
        lax.psum(centre_grad.astype(jnp.bfloat16), "heads").astype(jnp.float32),
        lax.psum(width_grad.astype(jnp.bfloat16), "heads").astype(jnp.float32),
        lax.psum(gain_part.astype(jnp.bfloat16), "heads").astype(jnp.float32),
        lax.psum(shift_part.astype(jnp.bfloat16), "heads").astype(jnp.float32),
    )
    dgain_two = dgain_two + gain_total
    dshift_two = dshift_two + shift_total
    norm_one_state_grad, dgain_one, dshift_one = norm_one_backward(normed_one_grad)
    grad_zero = grad_one + norm_one_state_grad
    grad_states, dweight_time = time_backward(grad_zero)
    summed = (
        lax.psum(dweight_time.astype(jnp.bfloat16), "rows").astype(jnp.float32),
        lax.psum(dgain_one.astype(jnp.bfloat16), "rows").astype(jnp.float32),
        lax.psum(dshift_one.astype(jnp.bfloat16), "rows").astype(jnp.float32),
        lax.psum(dweight_qkv.astype(jnp.bfloat16), "rows").astype(jnp.float32),
        lax.psum(dweight_kernel.astype(jnp.bfloat16), "rows").astype(jnp.float32),
        lax.psum(centre_grad.astype(jnp.bfloat16), "rows").astype(jnp.float32),
        lax.psum(width_grad.astype(jnp.bfloat16), "rows").astype(jnp.float32),
        lax.psum(dweight_out.astype(jnp.bfloat16), "rows").astype(jnp.float32),
        lax.psum(dgain_two.astype(jnp.bfloat16), "rows").astype(jnp.float32),
        lax.psum(dshift_two.astype(jnp.bfloat16), "rows").astype(jnp.float32),
        lax.psum(dweight_up.astype(jnp.bfloat16), "rows").astype(jnp.float32),
        lax.psum(dweight_down.astype(jnp.bfloat16), "rows").astype(jnp.float32),
        lax.psum(dweight_force.astype(jnp.bfloat16), "rows").astype(jnp.float32),
    )
    return (
        state_two,
        forces,
        grad_states,
        summed[0],
        summed[1],
        summed[2],
        summed[3],
        summed[4],
        summed[5],
        summed[6],
        summed[7],
        summed[8],
        summed[9],
        summed[10],
        summed[11],
        summed[12],
    )


def solution(mesh):
    in_specs = (
        P("rows", None),
        P("rows"),
        P(None, "rows"),
        P("rows", None),
        P(),
        P(),
        P(),
        P(None, "heads", None, None),
        P(None, "heads"),
        P(),
        P(),
        P("heads", None, None),
        P(),
        P(),
        P(None, "heads"),
        P("heads", None),
        P(),
        P("rows", None),
        P(None, "rows"),
    )
    out_specs = (
        P("rows", None),
        P(None, "rows"),
        P("rows", None),
        P(),
        P(),
        P(),
        P(None, "heads", None, None),
        P(None, "heads"),
        P(),
        P(),
        P("heads", None, None),
        P(),
        P(),
        P(None, "heads"),
        P("heads", None),
        P(),
    )
    return jax.shard_map(body, mesh=mesh, in_specs=in_specs, out_specs=out_specs, check_vma=False)
```

```python
import functools
import math

import jax
import jax.numpy as jnp
from jax import lax
from jax.experimental import pallas as pl
from jax.experimental.pallas import tpu as pltpu
from jax.sharding import PartitionSpec as P

LOG2E = math.log2(math.e)
CENTRE = 4.0
LANES = 128
PAD = 32
bf16, f32 = jnp.bfloat16, jnp.float32
UNROLL_F = (2, 2, 4, 8)
UNROLL_B = (2, 2, 4, 8)


def dot(a, b):
    return lax.dot_general(a, b, (((1,), (0,)), ((), ())), preferred_element_type=f32)


def dot_nt(a, b):
    return lax.dot_general(a, b, (((1,), (1,)), ((), ())), preferred_element_type=f32)


def head_mask(h, width):
    lane = lax.broadcasted_iota(jnp.int32, (1, width), 1)
    return jnp.where(lane // PAD == h, 1.0, 0.0).astype(bf16)


def gauss_coefs(means, widths, coef):
    inv = 1.0 / (widths * widths)
    shift = means - CENTRE
    half = 0.5 * LOG2E * inv
    coef[0] = jnp.broadcast_to(-half, coef.shape[1:])
    coef[1] = jnp.broadcast_to(2.0 * half * shift, coef.shape[1:])
    norm = -jnp.log(widths * math.sqrt(2.0 * math.pi)) * LOG2E
    coef[2] = jnp.broadcast_to(norm - half * shift * shift, coef.shape[1:])


def distances(row0, aux, coords, first, width):
    total = None
    for axis in range(3):
        delta = aux[pl.ds(row0, 8), axis : axis + 1] - coords[axis : axis + 1, first : first + width]
        total = delta * delta if total is None else total + delta * delta
    return jnp.sqrt(total) - CENTRE


def gauss_value(dist, coef, row, cols):
    kernels = coef.shape[1]
    rows = []
    for piece in range(kernels // 16):
        ks = slice(piece * 16, piece * 16 + 16)
        c0, c1, c2 = coef[0, ks, :], coef[1, ks, :], coef[2, ks, :]
        line = []
        for lane in range(cols.start, cols.stop, LANES):
            d = dist[row : row + 1, lane : lane + LANES]
            line.append(jnp.exp2((d * c0 + c1) * d + c2).astype(bf16))
        rows.append(jnp.concatenate(line, axis=1) if len(line) > 1 else line[0])
    return jnp.concatenate(rows, axis=0)


def chunks(width, step):
    return [slice(at, min(at + step, width)) for at in range(0, width, step)]


def spread_weights(wk_t):
    zero = jnp.zeros_like(wk_t)
    return jnp.concatenate([jnp.concatenate([wk_t, zero], 1), jnp.concatenate([zero, wk_t], 1)], 0).astype(bf16)


def pair_tile(tile, aux, coords, ids, coef, dist, pair, spread, heads, atoms):
    first, width = tile * LANES, atoms - tile * LANES

    def unit(group, carry):
        row0 = pl.multiple_of(first + group * 8, 8)
        dist[:, :width] = distances(row0, aux, coords, first, width)
        same = aux[pl.ds(row0, 8), 3:4] == ids[0:1, first:]
        mask = jnp.where(same, 0.0, -1e30)
        for two in range(4):
            at = pl.ds(pl.multiple_of((row0 + 2 * two) * heads, 2 * heads), 2 * heads)
            for cols in chunks(width, 2 * LANES):
                g = jnp.concatenate([gauss_value(dist, coef, 2 * two + i, cols) for i in range(2)], 0)
                terms = dot(spread[...], g) * LOG2E
                for lane in range(cols.start, cols.stop, LANES):
                    bar = jnp.concatenate([jnp.broadcast_to(mask[2 * two + i : 2 * two + i + 1, lane : lane + LANES], (heads, LANES)) for i in range(2)], 0)
                    pair[tile + lane // LANES, at, :] = terms[:, lane - cols.start : lane - cols.start + LANES] + bar
        return carry

    lax.fori_loop(0, LANES // 8, unit, 0, unroll=UNROLL_F[tile % 4])


def mirror(ref, h, heads, tiles, add):
    for lo in range(tiles):
        for hi in range(lo + 1, tiles):
            near = pl.ds(lo * LANES * heads + h, LANES, stride=heads)
            far = pl.ds(hi * LANES * heads + h, LANES, stride=heads)
            if add:
                ref[hi, near, :] = ref[hi, near, :] + jnp.transpose(ref[lo, far, :])
            else:
                ref[lo, far, :] = jnp.transpose(ref[hi, near, :])


def soft_phase(pair, qt, k, vt, att_out, ctx_out, buf0, buf1, heads, atoms):
    tiles = atoms // LANES
    scale = LOG2E / math.sqrt(24)

    def raw(h, buf):
        buf[...] = dot(k[...] * head_mask(h, k.shape[1]), qt[...])

    def soften(h, buf):
        rows = pl.ds(pl.multiple_of(h * PAD, PAD), PAD)
        for tile in range(tiles):
            cols = slice(tile * LANES, (tile + 1) * LANES)
            logits = buf[:, cols] * scale + pair[tile, pl.ds(h, atoms, stride=heads), :]
            weights = jnp.exp2(logits - jnp.max(logits, axis=0, keepdims=True))
            soft = weights * (1.0 / jnp.sum(weights, axis=0, keepdims=True))
            att_out[h, :, cols] = soft.astype(bf16)
        ctx_out[rows, :] = dot(vt[rows, :], att_out[h]).astype(bf16)

    raw(0, buf0)

    def step(i, carry):
        h = 2 * i
        mirror(pair, h, heads, tiles, False)
        raw(h + 1, buf1)
        soften(h, buf0)
        mirror(pair, h + 1, heads, tiles, False)
        raw(jnp.minimum(h + 2, heads - 1), buf0)
        soften(h + 1, buf1)
        return carry

    lax.fori_loop(0, heads // 2, step, 0)


def pieces_of(x):
    a = x.astype(bf16).astype(f32)
    r = x - a
    b = r.astype(bf16).astype(f32)
    return a, b, r - b


def score_phase(att, q, kt, v, dc, dct, term, score0, score1, buf0, buf1, dqt_out, dk_sum, dv_sum, heads, atoms):
    tiles = atoms // LANES
    scale = 1.0 / math.sqrt(24)
    dk_sum[...] = jnp.zeros_like(dk_sum)
    dv_sum[...] = jnp.zeros_like(dv_sum)

    def raw(h, buf):
        buf[...] = dot(v[...] * head_mask(h, v.shape[1]), dct[...])

    def grads(h, buf, score):
        mask = head_mask(h, v.shape[1])
        rows = pl.ds(pl.multiple_of(h * PAD, PAD), PAD)
        for tile in range(tiles):
            cols = slice(tile * LANES, (tile + 1) * LANES)
            soft = att[h, :, cols].astype(f32)
            part = soft * buf[:, cols]
            grad = part - soft * jnp.sum(part, axis=0, keepdims=True)
            score[:, cols] = (grad * scale).astype(bf16)
            term[tile, pl.ds(h, atoms, stride=heads), :] = grad.astype(bf16).astype(f32)
        dqt_out[rows, :] = dot(kt[rows, :], score[...]).astype(bf16)
        dv_sum[...] += dot(att[h], dc[...] * mask)
        dk_sum[...] += dot(score[...], q[...] * mask)
        mirror(term, h, heads, tiles, True)

    raw(0, buf0)

    def step(i, carry):
        h = 2 * i
        raw(h + 1, buf1)
        grads(h, buf0, score0)
        raw(jnp.minimum(h + 2, heads - 1), buf0)
        grads(h + 1, buf1, score1)
        return carry

    lax.fori_loop(0, heads // 2, step, 0)


def moment_tile(tile, aux, coords, coef, dist, term, moments, heads, atoms):
    first, width = tile * LANES, atoms - tile * LANES

    def unit(group, carry):
        row0 = pl.multiple_of(first + group * 8, 8)
        dist[:, :width] = distances(row0, aux, coords, first, width)
        total = None
        for row in range(8):
            at = pl.ds(pl.multiple_of((row0 + row) * heads, heads), heads)
            for cols in chunks(width, 2 * LANES):
                lhs = []
                for lane in range(cols.start, cols.stop, LANES):
                    t = term[tile + lane // LANES, at, :].astype(bf16).astype(f32)
                    d = dist[row : row + 1, lane : lane + LANES]
                    x1 = t * d
                    parts = (t,) + pieces_of(x1) + pieces_of(x1 * d) + (jnp.zeros_like(t),)
                    lhs.append(jnp.concatenate(parts, axis=0).astype(bf16))
                lhs = jnp.concatenate(lhs, axis=1) if len(lhs) > 1 else lhs[0]
                out = dot_nt(gauss_value(dist, coef, row, cols), lhs)
                total = out if total is None else total + out
        moments[...] += total
        return carry

    lax.fori_loop(0, LANES // 8, unit, 0, unroll=UNROLL_B[tile % 4])


def kernel_grads(moments, means, widths, w, heads):
    kernels = means.shape[1]
    sums = moments[...]
    if sums.shape[1] < LANES:
        sums = jnp.concatenate([sums, jnp.zeros((kernels, LANES - sums.shape[1]), f32)], axis=1)
    flat = jnp.transpose(sums)
    m = [flat[i * heads : (i + 1) * heads] for i in range(7)]
    m0, m1, m2 = m[0], m[1] + m[2] + m[3], m[4] + m[5] + m[6]
    shift = means - CENTRE
    s1 = m1 - shift * m0
    s2 = m2 - 2.0 * shift * m1 + shift * shift * m0
    inv = 1.0 / widths
    mean_grad = jnp.sum(w * s1, axis=0, keepdims=True) * inv * inv
    width_grad = jnp.sum(w * (s2 * inv * inv - m0), axis=0, keepdims=True) * inv
    return m0, mean_grad, width_grad


MESH = pl.DeviceIdType.MESH
epsilon = 1e-05


def remote(src, dst, send, recv, device):
    return pltpu.make_async_remote_copy(
        src_ref=src, dst_ref=dst, send_sem=send, recv_sem=recv, device_id=device, device_id_type=MESH
    )


class Place:
    def __init__(self, nr, nh):
        self.nr, self.nh, self.chips = nr, nh, nh // 2
        self.r, self.h = lax.axis_index("rows"), lax.axis_index("heads")
        self.x, self.c = self.h // 2, lax.rem(self.h, 2)
        self.mate = self.h + 1 - 2 * self.c

    def chip(self, k):
        return lax.rem(self.x + k + self.chips, self.chips)

    def enter(self):
        barrier = pltpu.get_barrier_semaphore()
        for k in range(1, self.nr):
            pl.semaphore_signal(barrier, inc=1, device_id=(lax.rem(self.r + k, self.nr), self.h), device_id_type=MESH)
        for k in range(1, self.nh):
            pl.semaphore_signal(barrier, inc=1, device_id=(self.r, lax.rem(self.h + k, self.nh)), device_id_type=MESH)
        pl.semaphore_wait(barrier, self.nr + self.nh - 2)


class Gather:
    def __init__(self, place, full, send, recv):
        self.place, self.full, self.send, self.recv = place, full, send, recv

    def copy(self, block, to, slot):
        ref = self.full.at[block]
        made = remote(ref, ref, self.send.at[slot], self.recv.at[slot], (self.place.r, to))
        made.start()
        return made

    def start(self):
        p = self.place
        self.along = [self.copy(p.h, p.chip(k) * 2 + p.c, k) for k in range(1, p.chips)]
        self.across = [self.copy(p.h, p.mate, 0)]

    def forward(self):
        p = self.place
        for k in range(1, p.chips):
            self.along[k - 1].wait_recv()
            self.across.append(self.copy(p.chip(-k) * 2 + p.c, p.mate, p.chips - 1 + k))

    def near(self):
        self.across[0].wait_recv()

    def far(self):
        for made in self.across[1:]:
            made.wait_recv()

    def done(self):
        for made in self.along + self.across:
            made.wait_send()


class Scatter:
    def __init__(self, place, out1, in1, out2, in2, send, recv):
        self.place, self.out1, self.in1, self.out2, self.in2 = place, out1, in1, out2, in2
        self.send, self.recv = send, recv

    def start(self, block):
        p = self.place
        self.block = block
        self.pair, self.line = {}, []
        for k in list(range(1, p.chips)) + [0]:
            self.out1[k] = block(p.chip(k) * 2 + 1 - p.c).astype(bf16)
            self.pair[k] = remote(self.out1.at[k], self.in1.at[k], self.send.at[k], self.recv.at[k], (p.r, p.mate))
            self.pair[k].start()

    def middle(self):
        p = self.place
        for k in range(1, p.chips):
            mine = self.block(p.chip(k) * 2 + p.c)
            self.pair[k].wait_recv()
            self.out2[k - 1] = (mine + self.in1[k].astype(f32)).astype(bf16)
            slot = p.chips + k - 1
            made = remote(self.out2.at[k - 1], self.in2.at[k - 1], self.send.at[slot], self.recv.at[slot], (p.r, p.chip(k) * 2 + p.c))
            made.start()
            self.line.append(made)
        self.own = self.block(p.h)

    def finish(self):
        total = self.own
        self.pair[0].wait_recv()
        total = total + self.in1[0].astype(f32)
        for k, made in enumerate(self.line):
            made.wait_recv()
            total = total + self.in2[k].astype(f32)
        for made in list(self.pair.values()) + self.line:
            made.wait_send()
        return total


class Swap:
    def __init__(self, place, stage, land, send, recv):
        self.place, self.stage, self.land, self.send, self.recv = place, stage, land, send, recv

    def start(self):
        p = self.place
        self.made = []
        for k in range(1, p.nr):
            to = lax.rem(p.r + k, p.nr)
            made = remote(self.stage.at[to], self.land.at[p.r], self.send.at[k], self.recv.at[k], (to, p.h))
            made.start()
            self.made.append(made)
        self.land[p.r] = self.stage[p.r]

    def finish(self):
        for made in self.made:
            made.wait_recv()
        for made in self.made:
            made.wait_send()


def put_blocks(ref, value):
    count, size = ref.shape[0], ref.shape[1]
    for i in range(count):
        ref[i] = value[i * size : (i + 1) * size].astype(ref.dtype)


def take_blocks(ref):
    return jnp.concatenate([ref[i].astype(f32) for i in range(ref.shape[0])], axis=0)


def turn(value, inner):
    rows = value.shape[0]
    outer = rows // inner
    to = lax.broadcasted_iota(jnp.int32, (rows, rows), 0)
    at = lax.broadcasted_iota(jnp.int32, (rows, rows), 1)
    matrix = jnp.where(at == lax.rem(to, outer) * inner + to // outer, 1.0, 0.0).astype(bf16)
    return dot(matrix, value.astype(bf16))


def norm_parts(x):
    centred = x - jnp.mean(x, axis=1, keepdims=True)
    rstd = lax.rsqrt(jnp.mean(centred * centred, axis=1, keepdims=True) + epsilon)
    return centred * rstd, rstd


def norm_back(grad, xhat, rstd, gain):
    dy = grad * gain
    mean1 = jnp.mean(dy, axis=1, keepdims=True)
    mean2 = jnp.mean(dy * xhat, axis=1, keepdims=True)
    return rstd * (dy - mean1 - xhat * mean2)


def column_sum(x):
    return jnp.sum(x, axis=0, keepdims=True)


def flip(x):
    return jnp.transpose(x.astype(f32)).astype(x.dtype)


def pad_heads(parts):
    padded = []
    for part in parts:
        part = part.astype(f32)
        padded += [part, jnp.zeros((PAD - part.shape[0], part.shape[1]), f32)]
    return jnp.concatenate(padded, axis=0).astype(bf16)


def first_kernel(
    nr, nh, states, cots, steps, cot_forces, w_time, w_force, gain, bias, w_qkv, coords, ids, wk_t, means, widths,
    att_out, ctx_out, q_out, kt_out, v_out, n1_out, x0_out, gt_out, tt_out,
    x_in, c_in, stage_x, land_x, stage_g, land_g, weight, qt, k_rows, vt, aux, coef, dist, pair, spread, buf0, buf1,
    copy_sem, sx, rx, sg, rg, sn, rn, st, rt,
):
    place = Place(nr, nh)
    shard, width = x_in.shape
    heads, atoms = att_out.shape[0], att_out.shape[1]
    at = pl.ds(pl.multiple_of(place.h * shard, shard), shard)
    loads = [pltpu.make_async_copy(states.at[at], x_in, copy_sem.at[0]), pltpu.make_async_copy(cots.at[at], c_in, copy_sem.at[1])]
    for load in loads:
        load.start()
    place.enter()

    half = w_time.shape[0] // 2
    row = steps[pl.ds(place.h, 1), :].astype(f32)
    row = jnp.concatenate([row, jnp.zeros((1, LANES - shard), f32)], axis=1) if shard < LANES else row
    frequency = jnp.exp(lax.broadcasted_iota(jnp.int32, (half, 1), 0).astype(f32) * (-math.log(10000.0) / half))
    angles = frequency * row
    terms = jnp.transpose(jnp.concatenate([jnp.sin(angles), jnp.cos(angles)], axis=0))[:shard].astype(bf16)
    for load in loads:
        load.wait()
    zero = x_in[...] + dot(terms, w_time[...])
    put_blocks(stage_x, turn(zero, nr))
    swap_x = Swap(place, stage_x, land_x, sx, rx)
    swap_x.start()

    force = [cot_forces[pl.ds(j * nh + place.h, 1), :].astype(bf16).astype(f32) for j in range(3)]
    force = jnp.concatenate(force + [jnp.zeros((LANES - 3, shard), f32)], axis=0)
    force = jnp.concatenate([force, jnp.zeros((LANES, LANES - shard), f32)], axis=1) if shard < LANES else force
    force = jnp.transpose(force)[:shard]
    grad_two = c_in[...]
    for j in range(3):
        grad_two = grad_two + force[:, j : j + 1] * w_force[j : j + 1, :].astype(f32)
    put_blocks(stage_g, turn(jnp.concatenate([grad_two.astype(bf16), terms], axis=1), nr))
    swap_g = Swap(place, stage_g, land_g, sg, rg)
    swap_g.start()

    table = jnp.concatenate([coords[...], ids[...], jnp.zeros((LANES - 4, atoms), f32)], axis=0)
    aux[...] = jnp.transpose(table)
    kernels = wk_t.shape[1]
    columns = [jnp.transpose(jnp.broadcast_to(ref[...], (LANES, kernels))) for ref in (means, widths)]
    gauss_coefs(columns[0], columns[1], coef)
    spread[...] = spread_weights(wk_t[...].astype(f32))
    for part in range(3):
        weight[part] = pad_heads([w_qkv[h, part] for h in range(heads)])

    tiles = atoms // LANES
    pair_tile(0, aux, coords, ids, coef, dist, pair, spread, heads, atoms)

    swap_x.finish()
    x0 = turn(take_blocks(land_x), shard // nr)
    x0_out[...] = x0
    xhat, _ = norm_parts(x0)
    n1_out[place.h] = (xhat * gain[...] + bias[...]).astype(bf16)
    gather_n = Gather(place, n1_out, sn, rn)
    gather_n.start()
    swap_g.finish()
    both = turn(take_blocks(land_g), shard // nr).astype(bf16)
    gt_out[place.h] = both[:, :width]
    tt_out[...] = both[:, width:]

    pair_tile(1, aux, coords, ids, coef, dist, pair, spread, heads, atoms)
    gather_n.forward()
    gather_t = Gather(place, gt_out, st, rt)
    gather_t.start()
    for tile in range(2, tiles):
        pair_tile(tile, aux, coords, ids, coef, dist, pair, spread, heads, atoms)
    gather_n.near()
    gather_n.far()
    gather_n.done()

    normed = n1_out[...].reshape(atoms, width)
    qt[...] = dot_nt(weight[0], normed).astype(bf16)
    kt_out[...] = dot_nt(weight[1], normed).astype(bf16)
    vt[...] = dot_nt(weight[2], normed).astype(bf16)
    q_out[...] = dot_nt(normed, weight[0]).astype(bf16)
    k_rows[...] = dot_nt(normed, weight[1]).astype(bf16)
    v_out[...] = dot_nt(normed, weight[2]).astype(bf16)
    soft_phase(pair, qt, k_rows, vt, att_out, ctx_out, buf0, buf1, heads, atoms)
    gather_t.forward()
    gather_t.near()
    gather_t.far()
    gather_t.done()


def gelu_parts(x):
    below = 0.5 * (1.0 + lax.erf(x * math.sqrt(0.5)))
    return x * below, below + x * (jnp.exp(-0.5 * x * x) * (1.0 / math.sqrt(2.0 * math.pi)))


def second_kernel(
    nr, nh, ctx_t, x0, gt, w_out, w_up, w_down, gain, bias,
    dc_out, dct_out, up_out, down_out, wout_out, one_out, sums_out, two_out,
    ctx, weight, back, n2, hidden, pre_grad, og,
    o1a, i1a, o2a, i2a, o1b, i1b, o2b, i2b, o1c, i1c, o2c, i2c,
    s1, r1, s2, r2, s3, r3, s4, r4, s5, r5,
):
    place = Place(nr, nh)
    shard, width = x0.shape
    heads = w_out.shape[0]
    atoms = shard * nh
    place.enter()
    weight[...] = pad_heads([w_out[h] for h in range(heads)])
    for s in range(nh):
        ctx[s] = flip(ctx_t[:, s * shard : (s + 1) * shard]) if shard % LANES == 0 else flip(ctx_t[...])[s * shard : (s + 1) * shard]

    sum_a = Scatter(place, o1a, i1a, o2a, i2a, s1, r1)
    sum_a.start(lambda s: dot(ctx[s], weight[...]))
    sum_a.middle()
    for s in range(nh):
        back[s] = dot_nt(gt[s], w_down[...])
    one = x0[...] + sum_a.finish()
    xhat, rstd = norm_parts(one)
    n2[place.h] = (xhat * gain[...] + bias[...]).astype(bf16)
    gather_n = Gather(place, n2, s2, r2)
    gather_n.start()

    def forward(s):
        act, slope = gelu_parts(dot(n2[s], w_up[...]))
        hidden[s] = act.astype(bf16)
        pre_grad[s] = (back[s] * slope).astype(bf16)

    forward(place.h)
    gather_n.near()
    forward(place.mate)
    gather_n.forward()
    for k in range(1, place.chips):
        forward(place.chip(-k) * 2 + place.c)
    gather_n.far()
    for k in range(1, place.chips):
        forward(place.chip(-k) * 2 + 1 - place.c)
    gather_n.done()

    sum_b = Scatter(place, o1b, i1b, o2b, i2b, s3, r3)
    sum_b.start(lambda s: dot_nt(pre_grad[s], w_up[...]))
    sum_b.middle()
    hid = hidden[...].reshape(atoms, hidden.shape[2])
    down_out[...] = dot(flip(hid), gt[...].reshape(atoms, width)).astype(bf16).reshape(down_out.shape)
    normed_grad = sum_b.finish()
    one_grad = gt[place.h].astype(f32) + norm_back(normed_grad, xhat, rstd, gain[...])
    one_out[...] = one_grad
    og[place.h] = one_grad.astype(bf16)
    gather_o = Gather(place, og, s4, r4)
    gather_o.start()
    sums_out[0:1, :] = column_sum(normed_grad * xhat)
    sums_out[1:2, :] = column_sum(normed_grad)
    sum_c = Scatter(place, o1c, i1c, o2c, i2c, s5, r5)
    sum_c.start(lambda s: dot(hidden[s], w_down[...]))
    gather_o.forward()
    sum_c.middle()
    up_out[...] = dot(flip(n2[...].reshape(atoms, width)), pre_grad[...].reshape(atoms, pre_grad.shape[2])).astype(bf16).reshape(up_out.shape)
    gather_o.near()
    gather_o.far()
    gather_o.done()
    grads = og[...].reshape(atoms, width)
    dc_out[...] = dot_nt(grads, weight[...]).astype(bf16)
    dct_out[...] = dot_nt(weight[...], grads).astype(bf16)
    wout_out[...] = dot(ctx_t[...], grads).astype(bf16)
    two_out[...] = (one + sum_c.finish()).astype(bf16)


class Total:
    def __init__(self, place, data, full, got, part, line, send, recv):
        self.place, self.data, self.full, self.got, self.part, self.line = place, data, full, got, part, line
        self.send, self.recv = send, recv
        self.a, self.b = place.r // 2, lax.rem(place.r, 2)
        self.count = place.nr // 2

    def peer(self, k):
        return lax.rem(self.a + k + self.count, self.count)

    def pair(self):
        p = self.place
        self.first = remote(self.data.at[1 - self.b], self.got, self.send.at[0], self.recv.at[0], (p.r + 1 - 2 * self.b, p.h))
        self.first.start()

    def spread(self):
        p = self.place
        self.first.wait_recv()
        self.first.wait_send()
        for j in range(self.count):
            self.part[j] = (self.data[self.b, j].astype(f32) + self.got[j].astype(f32)).astype(bf16)
        self.second = []
        for k in range(1, self.count):
            to = self.peer(k)
            made = remote(self.part.at[to], self.line.at[k], self.send.at[k], self.recv.at[k], (to * 2 + self.b, p.h))
            made.start()
            self.second.append(made)

    def collect(self):
        p = self.place
        total = self.part[self.a].astype(f32)
        for k in range(1, self.count):
            self.second[k - 1].wait_recv()
            total = total + self.line[k].astype(f32)
        for made in self.second:
            made.wait_send()
        self.full[self.b, self.a] = total.astype(bf16)
        self.third, self.fourth = [], []
        for k in range(1, self.count):
            ref = self.full.at[self.b, self.a]
            slot = self.count - 1 + k
            made = remote(ref, ref, self.send.at[slot], self.recv.at[slot], (self.peer(k) * 2 + self.b, p.h))
            made.start()
            self.third.append(made)
        self.cross(self.a, 0)

    def cross(self, a, k):
        p = self.place
        ref = self.full.at[self.b, a]
        slot = 2 * self.count - 1 + k
        made = remote(ref, ref, self.send.at[slot], self.recv.at[slot], (p.r + 1 - 2 * self.b, p.h))
        made.start()
        self.fourth.append(made)

    def back(self):
        for k in range(1, self.count):
            self.third[k - 1].wait_recv()
            self.cross(self.peer(-k), k)

    def finish(self):
        for made in self.fourth:
            made.wait_recv()
        for made in self.third + self.fourth:
            made.wait_send()


def third_kernel(
    nr, nh, att, q, kt, v, dc, dct, n1, x0, tt, one, two, up, down, wout, sums, gain, w_qkv, w_force, cot_forces,
    coords, ids, wk_t, means, widths,
    up_out, down_out, qo_out, states_out, forces_out, gs_out, time_out, small_out, wk_out,
    weight, dq_t, dq, dk, dv, flat, aux, coef, dist, term, score0, score1, buf0, buf1, moments, dk_sum, dv_sum,
    o1, i1, o2, i2, stage_s, land_s, stage_g, land_g, full_s, full_g,
    time_mine, time_part, time_land, time_full, row_mine, row_all, one_mine, one_all,
    up_got, up_part, up_line, down_got, down_part, down_line, qo_got, qo_part, qo_line,
    qo_data, s_up, r_up, s_dn, r_dn, s_qo, r_qo, s_n, r_n, s_sw, r_sw, s_sg, r_sg, s_gw, r_gw, s_gg, r_gg,
    s_t1, r_t1, s_t2, r_t2, s_t3, r_t3, s_t4, r_t4, s_m1, r_m1, s_m2, r_m2,
):
    place = Place(nr, nh)
    shard, width = x0.shape
    heads, atoms = att.shape[0], att.shape[1]
    tiles = atoms // LANES
    kernels = wk_t.shape[1]
    place.enter()
    total_up = Total(place, up, up_out, up_got, up_part, up_line, s_up, r_up)
    total_down = Total(place, down, down_out, down_got, down_part, down_line, s_dn, r_dn)
    total_up.pair()
    total_down.pair()
    put_blocks(stage_s, turn(two[...], nr))
    swap_s = Swap(place, stage_s, land_s, s_sw, r_sw)
    swap_s.start()

    table = jnp.concatenate([coords[...], ids[...], jnp.zeros((LANES - 4, atoms), f32)], axis=0)
    aux[...] = jnp.transpose(table)
    columns = [jnp.transpose(jnp.broadcast_to(ref[...], (LANES, kernels))) for ref in (means, widths)]
    gauss_coefs(columns[0], columns[1], coef)
    for part in range(3):
        weight[part] = pad_heads([w_qkv[h, part] for h in range(heads)])

    score_phase(att, q, kt, v, dc, dct, term, score0, score1, buf0, buf1, dq_t, dk_sum, dv_sum, heads, atoms)

    total_up.spread()
    swap_s.finish()
    full_s[place.h] = turn(take_blocks(land_s), shard // nr).astype(bf16)
    gather_s = Gather(place, full_s, s_gw, r_gw)
    gather_s.start()

    for s in range(nh):
        rows = slice(s * shard, (s + 1) * shard)
        dq[s] = flip(dq_t[...])[rows] if shard % LANES else flip(dq_t[:, rows])
        dk[s] = dk_sum[rows, :].astype(bf16)
        dv[s] = dv_sum[rows, :].astype(bf16)
    sum_n = Scatter(place, o1, i1, o2, i2, s_n, r_n)
    sum_n.start(lambda s: dot(dq[s], weight[0]) + dot(dk[s], weight[1]) + dot(dv[s], weight[2]))
    sum_n.middle()

    normed = n1[...].reshape(atoms, width)
    parts = [dot(dq_t[...], normed), dot(flip(dk[...].reshape(atoms, -1)), normed), dot(flip(dv[...].reshape(atoms, -1)), normed)]
    size = w_qkv.shape[2]
    for h in range(heads):
        for i in range(3):
            flat[(h * 3 + i) * size : (h * 3 + i + 1) * size, :] = parts[i][h * PAD : h * PAD + size]
        base = heads * 3 * size + h * size
        flat[base : base + size, :] = wout[h * PAD : (h + 1) * PAD, :].astype(f32)[:size]
    slab = qo_out.shape[2]
    for b in range(2):
        for a in range(nr // 2):
            f = b * (nr // 2) + a
            qo_data[b, a] = flat[f * slab : (f + 1) * slab, :].astype(bf16)
    total_qo = Total(place, qo_data, qo_out, qo_got, qo_part, qo_line, s_qo, r_qo)
    total_qo.pair()
    total_down.spread()

    moments[...] = jnp.zeros_like(moments)
    moment_tile(0, aux, coords, coef, dist, term, moments, heads, atoms)

    grad_n = sum_n.finish()
    xhat, rstd = norm_parts(x0[...])
    gs = one[...] + norm_back(grad_n, xhat, rstd, gain[...])
    gs16 = gs.astype(bf16)
    put_blocks(stage_g, turn(gs16, nr))
    swap_g = Swap(place, stage_g, land_g, s_sg, r_sg)
    swap_g.start()
    total_up.collect()
    gather_s.forward()

    grads = dot(flip(tt[...]), gs16)
    put_blocks(time_mine, grads)
    time_one = []
    for k in range(1, nh):
        to = lax.rem(place.h + k, nh)
        made = remote(time_mine.at[to], time_part.at[k], s_t1.at[k], r_t1.at[k], (place.r, to))
        made.start()
        time_one.append(made)

    moment_tile(1, aux, coords, coef, dist, term, moments, heads, atoms)
    total_down.collect()
    total_qo.spread()

    swap_g.finish()
    full_g[place.h] = turn(take_blocks(land_g), shard // nr).astype(bf16)
    gather_g = Gather(place, full_g, s_gg, r_gg)
    gather_g.start()

    quarter = time_mine[place.h].astype(f32)
    for k in range(1, nh):
        time_one[k - 1].wait_recv()
        quarter = quarter + time_part[k].astype(f32)
    for made in time_one:
        made.wait_send()
    put_blocks(time_land.at[0], quarter)
    time_two = []
    for k in range(1, nr):
        to = lax.rem(place.r + k, nr)
        made = remote(time_land.at[0, to], time_land.at[1, k], s_t2.at[k], r_t2.at[k], (to, place.h))
        made.start()
        time_two.append(made)

    for tile in range(2, tiles):
        moment_tile(tile, aux, coords, coef, dist, term, moments, heads, atoms)

    mine = time_land[0, place.r]
    for k in range(1, nr):
        time_two[k - 1].wait_recv()
        mine = mine + time_land[1, k]
    for made in time_two:
        made.wait_send()
    time_full[place.h, place.r] = mine
    time_three = []
    for k in range(1, nr):
        to = lax.rem(place.r + k, nr)
        ref = time_full.at[place.h, place.r]
        made = remote(ref, ref, s_t3.at[k], r_t3.at[k], (to, place.h))
        made.start()
        time_three.append(made)
    total_up.back()

    own = full_s[place.h]
    cots = [cot_forces[pl.ds(j * nh + place.h, 1), :].astype(bf16).astype(f32) for j in range(3)]
    cots = jnp.concatenate(cots + [jnp.zeros((5, shard), f32)], axis=0).astype(bf16)
    force_grad = dot(cots, own)
    kernel_sums = kernel_grads(moments, means[...], widths[...], wk_t[...].astype(f32), heads)
    wide = jnp.concatenate([kernel_sums[1], kernel_sums[2], jnp.zeros((1, width - 2 * kernels), f32)], axis=1)
    small = jnp.concatenate([force_grad[0:3], sums[...], column_sum(grad_n * xhat), column_sum(grad_n), wide], axis=0)
    one_all[place.h] = small
    ones = []
    for k in range(1, nh):
        to = lax.rem(place.h + k, nh)
        ref = one_all.at[place.h]
        made = remote(ref, ref, s_m1.at[k], r_m1.at[k], (place.r, to))
        made.start()
        ones.append(made)
    gather_g.forward()
    total_down.back()
    for made in ones:
        made.wait_recv()
    for made in ones:
        made.wait_send()
    summed = one_all[0]
    for j in range(1, nh):
        summed = summed + one_all[j]
    row_all[place.r, :, 0:width] = summed
    row_all[place.r, :, width:] = jnp.concatenate([kernel_sums[0], jnp.zeros((8 - heads, kernels), f32)], axis=0) if heads < 8 else kernel_sums[0]
    rows = []
    for k in range(1, nr):
        to = lax.rem(place.r + k, nr)
        ref = row_all.at[place.r]
        made = remote(ref, ref, s_m2.at[k], r_m2.at[k], (to, place.h))
        made.start()
        rows.append(made)

    gather_s.near()
    gather_s.far()
    gather_s.done()
    states_out[...] = full_s[...].reshape(atoms, width)
    forces_out[...] = dot_nt(jnp.concatenate([w_force[...].astype(f32), jnp.zeros((5, width), f32)], axis=0).astype(bf16), states_out[...])
    total_qo.collect()
    gather_g.near()
    gather_g.far()
    gather_g.done()
    gs_out[...] = full_g[...].reshape(atoms, width)

    for made in time_three:
        made.wait_recv()
    for made in time_three:
        made.wait_send()
    time_four = []
    for k in range(1, nh):
        to = lax.rem(place.h + k, nh)
        ref = time_full.at[place.h]
        made = remote(ref, ref, s_t4.at[k], r_t4.at[k], (place.r, to))
        made.start()
        time_four.append(made)
    for made in rows:
        made.wait_recv()
    for made in rows:
        made.wait_send()
    total = row_all[0]
    for j in range(1, nr):
        total = total + row_all[j]
    small_out[...] = total[:, 0:width]
    wk_out[...] = total[:, width:]
    total_qo.back()
    for made in time_four:
        made.wait_recv()
    for made in time_four:
        made.wait_send()
    piece = time_full.shape[2]
    for j in range(nh):
        for i in range(nr):
            base = (j * nr + i) * piece
            time_out[base : base + piece, :] = time_full[j, i]
    total_up.finish()
    total_down.finish()
    total_qo.finish()


VM = pl.BlockSpec(memory_space=pltpu.VMEM)
ANY = pl.BlockSpec(memory_space=pl.ANY)


def sems(*counts):
    return [pltpu.SemaphoreType.DMA((n,)) for n in counts]


def S(shape, dtype):
    return jax.ShapeDtypeStruct(shape, dtype)


def V(shape, dtype):
    return pltpu.VMEM(shape, dtype)


def body(
    nr,
    nh,
    atom_states,
    time_steps,
    coords,
    item_ids,
    w_time,
    ln1_gain,
    ln1_bias,
    w_qkv,
    w_kernel,
    kernel_means,
    kernel_widths,
    w_out,
    ln2_gain,
    ln2_bias,
    w_up,
    w_down,
    w_force,
    cot_states,
    cot_forces,
):
    atoms, width = atom_states.shape
    heads, head_dim = w_qkv.shape[1], w_qkv.shape[3]
    kernels, freqs, units = w_kernel.shape[0], w_time.shape[0], w_up.shape[1]
    shard, tiles = atoms // nh, atoms // LANES
    chips, wide, group = nh // 2, heads * PAD, atoms // nr // nh
    line = 2 * chips - 1
    steps = time_steps.reshape(nh, shard)
    cot_rows = cot_forces.reshape(3 * nh, shard)
    gain1, bias1, gain2, bias2 = [x.reshape(1, width) for x in (ln1_gain, ln1_bias, ln2_gain, ln2_bias)]
    qkv_t = jnp.transpose(w_qkv, (1, 2, 3, 0))
    ids = item_ids.astype(f32)
    wk_t = w_kernel.T
    means, widths = kernel_means.reshape(1, kernels), kernel_widths.reshape(1, kernels)

    def params(collective, megabytes):
        return pltpu.CompilerParams(collective_id=collective, has_side_effects=True, vmem_limit_bytes=megabytes << 20)

    table = [V((atoms, LANES), f32), V((3, kernels, LANES), f32), V((8, atoms), f32)]
    big = V((tiles, atoms * heads, LANES), f32)
    square = V((atoms, atoms), f32)
    att, ctx_t, q, kt, v, n1, x0, gt, tt = pl.pallas_call(
        functools.partial(first_kernel, nr, nh),
        out_shape=(
            S((heads, atoms, atoms), bf16), S((wide, atoms), bf16), S((atoms, wide), bf16), S((wide, atoms), bf16), S((atoms, wide), bf16),
            S((nh, shard, width), bf16), S((shard, width), f32), S((nh, shard, width), bf16), S((shard, freqs), bf16),
        ),
        in_specs=[ANY, ANY] + [VM] * 12,
        out_specs=(VM,) * 9,
        scratch_shapes=[
            V((shard, width), f32), V((shard, width), f32),
            V((nr, group, width), bf16), V((nr, group, width), bf16), V((nr, group, width + freqs), bf16), V((nr, group, width + freqs), bf16),
            V((3, wide, width), bf16), V((wide, atoms), bf16), V((atoms, wide), bf16), V((wide, atoms), bf16),
        ] + table + [big, V((heads * 2, 2 * kernels), bf16), square, square]
        + sems(2, nr, nr, nr, nr, line, line, line, line),
        name="first",
        compiler_params=params(1, 56),
    )(atom_states, cot_states, steps, cot_rows, w_time, w_force, gain1, bias1, qkv_t, coords, ids, wk_t, means, widths)

    slabs = lambda rows: (2, nr // 2, rows // nr, width)
    block, three = V((nh, shard, width), bf16), (nh, shard, units)
    ring = [V((chips, shard, width), bf16), V((chips, shard, width), bf16), V((max(chips - 1, 1), shard, width), bf16), V((max(chips - 1, 1), shard, width), bf16)]
    up_shape, down_shape = (2, nr // 2, width // nr, units), (2, nr // 2, units // nr, width)
    dc, dct, up, down, wout, one, sums, two = pl.pallas_call(
        functools.partial(second_kernel, nr, nh),
        out_shape=(
            S((atoms, wide), bf16), S((wide, atoms), bf16), S((width, units), bf16), S((units, width), bf16), S((wide, width), bf16),
            S((shard, width), f32), S((2, width), f32), S((shard, width), bf16),
        ),
        in_specs=[VM] * 8,
        out_specs=(VM,) * 8,
        scratch_shapes=[V((nh, shard, wide), bf16), V((wide, width), bf16), V(three, f32), block, V(three, bf16), V(three, bf16), block]
        + ring * 3 + sems(*([line] * 10)),
        name="second",
        compiler_params=params(2, 56),
    )(ctx_t, x0, gt, w_out, w_up, w_down, gain2, bias2)

    rows_qo = heads * 4 * head_dim
    qo_shape = slabs(rows_qo)
    land = [V((nr, group, width), bf16)] * 2

    def total_buffers(shape):
        return [V(shape[1:], bf16), V(shape[1:], bf16), V(shape[1:], bf16)]

    quarter = freqs // nh
    piece = quarter // nr
    outs = pl.pallas_call(
        functools.partial(third_kernel, nr, nh),
        out_shape=(
            S(up_shape, bf16), S(down_shape, bf16), S(qo_shape, bf16), S((atoms, width), bf16), S((8, atoms), f32),
            S((atoms, width), bf16), S((freqs, width), f32), S((8, width), f32), S((8, kernels), f32),
        ),
        in_specs=[VM] * 24,
        out_specs=(VM,) * 9,
        scratch_shapes=[
            V((3, wide, width), bf16), V((wide, atoms), bf16), V((nh, shard, wide), bf16), V((nh, shard, wide), bf16), V((nh, shard, wide), bf16),
            V((rows_qo, width), f32),
        ] + table + [
            big, V((atoms, atoms), bf16), V((atoms, atoms), bf16), square, square,
            V((kernels, 8 * heads), f32), V((atoms, wide), f32), V((atoms, wide), f32),
        ] + ring + land + land + [block, block]
        + [
            V((nh, quarter, width), bf16), V((nh, quarter, width), bf16), V((2, nr, piece, width), f32), V((nh, nr, piece, width), f32),
            V((8, 128), f32), V((nr, 8, width + kernels), f32), V((8, 128), f32), V((nh, 8, width), f32),
        ]
        + total_buffers(up_shape) + total_buffers(down_shape) + total_buffers(qo_shape)
        + [V(qo_shape, bf16)]
        + sems(*([3 * (nr // 2) - 1] * 6), line, line, nr, nr, nr, nr, line, line, line, line)
        + sems(nh, nh, nr, nr, nr, nr, nh, nh, nh, nh, nr, nr),
        name="third",
        compiler_params=params(3, 60),
    )(
        att, q, kt, v, dc, dct, n1, x0, tt, one, two, up.reshape(up_shape), down.reshape(down_shape), wout, sums, gain1, qkv_t,
        w_force, cot_rows, coords, ids, wk_t, means, widths,
    )
    up_sum, down_sum, qo_sum, states, forces, grad_states, time_grad, small, wk_grad = outs
    qo = qo_sum.reshape(rows_qo, width).astype(f32)
    qkv_rows = heads * 3 * head_dim
    return (
        states.astype(f32),
        forces[:3],
        grad_states.astype(f32),
        time_grad,
        small[5],
        small[6],
        jnp.transpose(qo[:qkv_rows].reshape(heads, 3, head_dim, width), (3, 0, 1, 2)),
        wk_grad[:heads].T,
        small[7, :kernels],
        small[7, kernels : 2 * kernels],
        qo[qkv_rows:].reshape(heads, head_dim, width),
        small[3],
        small[4],
        up_sum.reshape(width, units).astype(f32),
        down_sum.reshape(units, width).astype(f32),
        small[0:3],
    )


def solution(mesh):
    in_specs = (
        P("rows", None),
        P("rows"),
        P(None, "rows"),
        P("rows", None),
        P(),
        P(),
        P(),
        P(None, "heads", None, None),
        P(None, "heads"),
        P(),
        P(),
        P("heads", None, None),
        P(),
        P(),
        P(None, "heads"),
        P("heads", None),
        P(),
        P("rows", None),
        P(None, "rows"),
    )
    out_specs = (
        P("rows", None),
        P(None, "rows"),
        P("rows", None),
        P(),
        P(),
        P(),
        P(None, "heads", None, None),
        P(None, "heads"),
        P(),
        P(),
        P("heads", None, None),
        P(),
        P(),
        P(None, "heads"),
        P("heads", None),
        P(),
    )
    step = functools.partial(body, mesh.shape["rows"], mesh.shape["heads"])
    return jax.shard_map(step, mesh=mesh, in_specs=in_specs, out_specs=out_specs, check_vma=False)
```

```python
import functools
import math
import types

import jax
import jax.numpy as jnp
from jax import lax
from jax.experimental import pallas as pl
from jax.experimental.pallas import tpu as pltpu
from jax.sharding import PartitionSpec as P

VMEM_MIB = 62
LOG2E = math.log2(math.e)
CENTRE = 4.0
LANES = 128
PAD = 32
bf16, f32 = jnp.bfloat16, jnp.float32
UNROLL_F = (2, 2, 4, 8)
UNROLL_B = (2, 2, 4, 8)


def dot(a, b):
    return lax.dot_general(a, b, (((1,), (0,)), ((), ())), preferred_element_type=f32)


def dot_nt(a, b):
    return lax.dot_general(a, b, (((1,), (1,)), ((), ())), preferred_element_type=f32)


def head_mask(h, width):
    lane = lax.broadcasted_iota(jnp.int32, (1, width), 1)
    return jnp.where(lane // PAD == h, 1.0, 0.0).astype(bf16)


def gauss_coefs(means, widths, coef):
    inv = 1.0 / (widths * widths)
    shift = means - CENTRE
    half = 0.5 * LOG2E * inv
    coef[0] = jnp.broadcast_to(-half, coef.shape[1:])
    coef[1] = jnp.broadcast_to(2.0 * half * shift, coef.shape[1:])
    norm = -jnp.log(widths * math.sqrt(2.0 * math.pi)) * LOG2E
    coef[2] = jnp.broadcast_to(norm - half * shift * shift, coef.shape[1:])


def distances(row0, aux, coords, first, width):
    total = None
    for axis in range(3):
        delta = aux[pl.ds(row0, 8), axis : axis + 1] - coords[axis : axis + 1, first : first + width]
        total = delta * delta if total is None else total + delta * delta
    return jnp.sqrt(total) - CENTRE


def gauss_value(dist, coef, row, cols):
    kernels = coef.shape[1]
    rows = []
    for piece in range(kernels // 16):
        ks = slice(piece * 16, piece * 16 + 16)
        c0, c1, c2 = coef[0, ks, :], coef[1, ks, :], coef[2, ks, :]
        line = []
        for lane in range(cols.start, cols.stop, LANES):
            d = dist[row : row + 1, lane : lane + LANES]
            line.append(jnp.exp2((d * c0 + c1) * d + c2).astype(bf16))
        rows.append(jnp.concatenate(line, axis=1) if len(line) > 1 else line[0])
    return jnp.concatenate(rows, axis=0)


def chunks(width, step):
    return [slice(at, min(at + step, width)) for at in range(0, width, step)]


def spread_weights(wk_t):
    zero = jnp.zeros_like(wk_t)
    return jnp.concatenate([jnp.concatenate([wk_t, zero], 1), jnp.concatenate([zero, wk_t], 1)], 0).astype(bf16)


def pair_tile(tile, aux, coords, ids, coef, dist, pair, spread, heads, atoms):
    first, width = tile * LANES, atoms - tile * LANES

    def unit(group, carry):
        row0 = pl.multiple_of(first + group * 8, 8)
        dist[:, :width] = distances(row0, aux, coords, first, width)
        same = aux[pl.ds(row0, 8), 3:4] == ids[0:1, first:]
        mask = jnp.where(same, 0.0, -1e30)
        for two in range(4):
            at = pl.ds(pl.multiple_of((row0 + 2 * two) * heads, 2 * heads), 2 * heads)
            for cols in chunks(width, 2 * LANES):
                g = jnp.concatenate([gauss_value(dist, coef, 2 * two + i, cols) for i in range(2)], 0)
                terms = dot(spread[...], g) * LOG2E
                for lane in range(cols.start, cols.stop, LANES):
                    bar = jnp.concatenate([jnp.broadcast_to(mask[2 * two + i : 2 * two + i + 1, lane : lane + LANES], (heads, LANES)) for i in range(2)], 0)
                    pair[tile + lane // LANES, at, :] = terms[:, lane - cols.start : lane - cols.start + LANES] + bar
        return carry

    lax.fori_loop(0, LANES // 8, unit, 0, unroll=UNROLL_F[tile % 4])


def mirror(ref, h, heads, tiles, add):
    for lo in range(tiles):
        for hi in range(lo + 1, tiles):
            near = pl.ds(lo * LANES * heads + h, LANES, stride=heads)
            far = pl.ds(hi * LANES * heads + h, LANES, stride=heads)
            if add:
                ref[hi, near, :] = ref[hi, near, :] + jnp.transpose(ref[lo, far, :])
            else:
                ref[lo, far, :] = jnp.transpose(ref[hi, near, :])


def soft_phase(pair, qt, k, vt, att_out, ctx_out, buf0, buf1, heads, atoms):
    tiles = atoms // LANES
    scale = LOG2E / math.sqrt(24)

    def raw(h, buf):
        buf[...] = dot(k[...] * head_mask(h, k.shape[1]), qt[...])

    def soften(h, buf):
        rows = pl.ds(pl.multiple_of(h * PAD, PAD), PAD)
        for tile in range(tiles):
            cols = slice(tile * LANES, (tile + 1) * LANES)
            logits = buf[:, cols] * scale + pair[tile, pl.ds(h, atoms, stride=heads), :]
            weights = jnp.exp2(logits - jnp.max(logits, axis=0, keepdims=True))
            soft = weights * (1.0 / jnp.sum(weights, axis=0, keepdims=True))
            att_out[h, :, cols] = soft.astype(bf16)
        ctx_out[rows, :] = dot(vt[rows, :], att_out[h]).astype(bf16)

    raw(0, buf0)

    def step(i, carry):
        h = 2 * i
        mirror(pair, h, heads, tiles, False)
        raw(h + 1, buf1)
        soften(h, buf0)
        mirror(pair, h + 1, heads, tiles, False)
        raw(jnp.minimum(h + 2, heads - 1), buf0)
        soften(h + 1, buf1)
        return carry

    lax.fori_loop(0, heads // 2, step, 0)


def pieces_of(x):
    a = x.astype(bf16).astype(f32)
    r = x - a
    b = r.astype(bf16).astype(f32)
    return a, b, r - b


def score_part(first, last, att, q, kt, v, dc, dct, term, score0, score1, buf0, buf1, dqt_out, dk_sum, dv_sum, heads, atoms):
    tiles = atoms // LANES
    scale = 1.0 / math.sqrt(24)

    def raw(h, buf):
        buf[...] = dot(v[...] * head_mask(h, v.shape[1]), dct[...])

    def grads(h, buf, score):
        mask = head_mask(h, v.shape[1])
        rows = pl.ds(pl.multiple_of(h * PAD, PAD), PAD)
        for tile in range(tiles):
            cols = slice(tile * LANES, (tile + 1) * LANES)
            soft = att[h, :, cols].astype(f32)
            part = soft * buf[:, cols]
            grad = part - soft * jnp.sum(part, axis=0, keepdims=True)
            score[:, cols] = (grad * scale).astype(bf16)
            term[tile, pl.ds(h, atoms, stride=heads), :] = grad.astype(bf16).astype(f32)
        dqt_out[rows, :] = dot(kt[rows, :], score[...]).astype(bf16)
        dv_sum[...] += dot(att[h], dc[...] * mask)
        dk_sum[...] += dot(score[...], q[...] * mask)
        mirror(term, h, heads, tiles, True)

    raw(first, buf0)

    def step(i, carry):
        h = first + 2 * i
        raw(h + 1, buf1)
        grads(h, buf0, score0)
        raw(jnp.minimum(h + 2, heads - 1), buf0)
        grads(h + 1, buf1, score1)
        return carry

    lax.fori_loop(0, (last - first) // 2, step, 0)


def moment_tile(tile, aux, coords, coef, dist, term, moments, heads, atoms):
    first, width = tile * LANES, atoms - tile * LANES

    def unit(group, carry):
        row0 = pl.multiple_of(first + group * 8, 8)
        dist[:, :width] = distances(row0, aux, coords, first, width)
        total = None
        for row in range(8):
            at = pl.ds(pl.multiple_of((row0 + row) * heads, heads), heads)
            for cols in chunks(width, 2 * LANES):
                lhs = []
                for lane in range(cols.start, cols.stop, LANES):
                    t = term[tile + lane // LANES, at, :].astype(bf16).astype(f32)
                    d = dist[row : row + 1, lane : lane + LANES]
                    x1 = t * d
                    parts = (t,) + pieces_of(x1) + pieces_of(x1 * d) + (jnp.zeros_like(t),)
                    lhs.append(jnp.concatenate(parts, axis=0).astype(bf16))
                lhs = jnp.concatenate(lhs, axis=1) if len(lhs) > 1 else lhs[0]
                out = dot_nt(gauss_value(dist, coef, row, cols), lhs)
                total = out if total is None else total + out
        moments[...] += total
        return carry

    lax.fori_loop(0, LANES // 8, unit, 0, unroll=UNROLL_B[tile % 4])


def kernel_grads(moments, means, widths, w, heads):
    kernels = means.shape[1]
    sums = moments[...]
    if sums.shape[1] < LANES:
        sums = jnp.concatenate([sums, jnp.zeros((kernels, LANES - sums.shape[1]), f32)], axis=1)
    flat = jnp.transpose(sums)
    m = [flat[i * heads : (i + 1) * heads] for i in range(7)]
    m0, m1, m2 = m[0], m[1] + m[2] + m[3], m[4] + m[5] + m[6]
    shift = means - CENTRE
    s1 = m1 - shift * m0
    s2 = m2 - 2.0 * shift * m1 + shift * shift * m0
    inv = 1.0 / widths
    mean_grad = jnp.sum(w * s1, axis=0, keepdims=True) * inv * inv
    width_grad = jnp.sum(w * (s2 * inv * inv - m0), axis=0, keepdims=True) * inv
    return m0, mean_grad, width_grad


MESH = pl.DeviceIdType.MESH
epsilon = 1e-05


def remote(src, dst, send, recv, device):
    return pltpu.make_async_remote_copy(
        src_ref=src, dst_ref=dst, send_sem=send, recv_sem=recv, device_id=device, device_id_type=MESH
    )


class Place:
    def __init__(self, nr, nh):
        self.nr, self.nh, self.chips = nr, nh, nh // 2
        self.r, self.h = lax.axis_index("rows"), lax.axis_index("heads")
        self.x, self.c = self.h // 2, lax.rem(self.h, 2)
        self.mate = self.h + 1 - 2 * self.c

    def chip(self, k):
        return lax.rem(self.x + k + self.chips, self.chips)

    def enter(self):
        barrier = pltpu.get_barrier_semaphore()
        for k in range(1, self.nr):
            pl.semaphore_signal(barrier, inc=1, device_id=(lax.rem(self.r + k, self.nr), self.h), device_id_type=MESH)
        for k in range(1, self.nh):
            pl.semaphore_signal(barrier, inc=1, device_id=(self.r, lax.rem(self.h + k, self.nh)), device_id_type=MESH)
        pl.semaphore_wait(barrier, self.nr + self.nh - 2)


class Gather:
    def __init__(self, place, full, send, recv):
        self.place, self.full, self.send, self.recv = place, full, send, recv

    def copy(self, block, to, slot):
        ref = self.full.at[block]
        made = remote(ref, ref, self.send.at[slot], self.recv.at[slot], (self.place.r, to))
        made.start()
        return made

    def start(self):
        p = self.place
        self.along = [self.copy(p.h, p.chip(k) * 2 + p.c, k) for k in range(1, p.chips)]
        self.across = [self.copy(p.h, p.mate, 0)]

    def forward(self):
        p = self.place
        for k in range(1, p.chips):
            self.along[k - 1].wait_recv()
            self.across.append(self.copy(p.chip(-k) * 2 + p.c, p.mate, p.chips - 1 + k))

    def near(self):
        self.across[0].wait_recv()

    def far(self):
        for made in self.across[1:]:
            made.wait_recv()

    def done(self):
        for made in self.along + self.across:
            made.wait_send()


class Scatter:
    def __init__(self, place, out1, in1, out2, in2, send, recv):
        self.place, self.out1, self.in1, self.out2, self.in2 = place, out1, in1, out2, in2
        self.send, self.recv = send, recv

    def start(self, block):
        p = self.place
        self.block = block
        self.pair, self.line = {}, []
        for k in list(range(1, p.chips)) + [0]:
            self.out1[k] = block(p.chip(k) * 2 + 1 - p.c).astype(bf16)
            self.pair[k] = remote(self.out1.at[k], self.in1.at[k], self.send.at[k], self.recv.at[k], (p.r, p.mate))
            self.pair[k].start()

    def middle(self):
        p = self.place
        for k in range(1, p.chips):
            mine = self.block(p.chip(k) * 2 + p.c)
            self.pair[k].wait_recv()
            self.out2[k - 1] = (mine + self.in1[k].astype(f32)).astype(bf16)
            slot = p.chips + k - 1
            made = remote(self.out2.at[k - 1], self.in2.at[k - 1], self.send.at[slot], self.recv.at[slot], (p.r, p.chip(k) * 2 + p.c))
            made.start()
            self.line.append(made)
        self.own = self.block(p.h)

    def finish(self):
        total = self.own
        self.pair[0].wait_recv()
        total = total + self.in1[0].astype(f32)
        for k, made in enumerate(self.line):
            made.wait_recv()
            total = total + self.in2[k].astype(f32)
        for made in list(self.pair.values()) + self.line:
            made.wait_send()
        return total


class Swap:
    def __init__(self, place, stage, land, send, recv):
        self.place, self.stage, self.land, self.send, self.recv = place, stage, land, send, recv

    def start(self):
        p = self.place
        self.made = []
        for k in range(1, p.nr):
            to = lax.rem(p.r + k, p.nr)
            made = remote(self.stage.at[to], self.land.at[p.r], self.send.at[k], self.recv.at[k], (to, p.h))
            made.start()
            self.made.append(made)
        self.land[p.r] = self.stage[p.r]

    def finish(self):
        for made in self.made:
            made.wait_recv()
        for made in self.made:
            made.wait_send()


def put_blocks(ref, value):
    count, size = ref.shape[0], ref.shape[1]
    for i in range(count):
        ref[i] = value[i * size : (i + 1) * size].astype(ref.dtype)


def take_blocks(ref):
    return jnp.concatenate([ref[i].astype(f32) for i in range(ref.shape[0])], axis=0)


def turn(value, inner):
    rows = value.shape[0]
    outer = rows // inner
    to = lax.broadcasted_iota(jnp.int32, (rows, rows), 0)
    at = lax.broadcasted_iota(jnp.int32, (rows, rows), 1)
    matrix = jnp.where(at == lax.rem(to, outer) * inner + to // outer, 1.0, 0.0).astype(bf16)
    return dot(matrix, value.astype(bf16))


def norm_parts(x):
    centred = x - jnp.mean(x, axis=1, keepdims=True)
    rstd = lax.rsqrt(jnp.mean(centred * centred, axis=1, keepdims=True) + epsilon)
    return centred * rstd, rstd


def norm_back(grad, xhat, rstd, gain):
    dy = grad * gain
    mean1 = jnp.mean(dy, axis=1, keepdims=True)
    mean2 = jnp.mean(dy * xhat, axis=1, keepdims=True)
    return rstd * (dy - mean1 - xhat * mean2)


def column_sum(x):
    return jnp.sum(x, axis=0, keepdims=True)


def flip(x):
    return jnp.transpose(x.astype(f32)).astype(x.dtype)


def pad_heads(parts):
    padded = []
    for part in parts:
        part = part.astype(f32)
        padded += [part, jnp.zeros((PAD - part.shape[0], part.shape[1]), f32)]
    return jnp.concatenate(padded, axis=0).astype(bf16)


class Total:
    def __init__(self, place, data, full, got, part, line, send, recv):
        self.place, self.data, self.full, self.got, self.part, self.line = place, data, full, got, part, line
        self.send, self.recv = send, recv
        self.a, self.b = place.r // 2, lax.rem(place.r, 2)
        self.count = place.nr // 2
        self.mate = (place.r + 1 - 2 * self.b, place.h)
        self.second, self.third, self.fourth = {}, {}, {}

    def peer(self, k):
        return lax.rem(self.a + k + self.count, self.count)

    def send_to(self, src, dst, slot, device):
        made = remote(src, dst, self.send.at[slot], self.recv.at[slot], device)
        made.start()
        return made

    def pair(self):
        self.first = {}
        for k in list(range(1, self.count)) + [0]:
            j = self.peer(k)
            self.first[k] = self.send_to(self.data.at[1 - self.b, j], self.got.at[j], k, self.mate)

    def spread(self, *ks):
        for k in ks:
            j = self.peer(k)
            self.first[k].wait_recv()
            self.part[j] = (self.data[self.b, j].astype(f32) + self.got[j].astype(f32)).astype(bf16)
            if k:
                self.second[k] = self.send_to(self.part.at[j], self.line.at[k], self.count + k, (j * 2 + self.b, self.place.h))

    def collect(self):
        total = self.part[self.a].astype(f32)
        for k in range(1, self.count):
            self.second[k].wait_recv()
            total = total + self.line[k].astype(f32)
        self.full[self.b, self.a] = total.astype(bf16)
        ref = self.full.at[self.b, self.a]
        for k in range(1, self.count):
            self.third[k] = self.send_to(ref, ref, 2 * self.count + k, (self.peer(k) * 2 + self.b, self.place.h))
        self.cross(self.a, 0)

    def cross(self, a, k):
        ref = self.full.at[self.b, a]
        self.fourth[k] = self.send_to(ref, ref, 3 * self.count + k, self.mate)

    def back(self, *ks):
        for k in ks:
            self.third[k].wait_recv()
            self.cross(self.peer(-k), k)

    def finish(self):
        for made in self.fourth.values():
            made.wait_recv()
        for group in (self.first, self.second, self.third, self.fourth):
            for made in group.values():
                made.wait_send()


def share(nh, h, value, shard):
    picked = value[:, :shard]
    for j in range(1, nh):
        picked = jnp.where(h == j, value[:, j * shard : (j + 1) * shard], picked)
    return picked


def widen(value):
    lanes = value.shape[1]
    return value if lanes == LANES else jnp.concatenate([value, jnp.zeros((value.shape[0], LANES - lanes), f32)], axis=1)


def row_of(ref):
    return ref[...].reshape(1, ref.shape[0])


def gelu_parts(x):
    below = 0.5 * (1.0 + lax.erf(x * math.sqrt(0.5)))
    return x * below, below + x * (jnp.exp(-0.5 * x * x) * (1.0 / math.sqrt(2.0 * math.pi)))


def layer_kernel(nr, nh, names, *refs):
    g = types.SimpleNamespace(**dict(zip(names, refs)))
    place = Place(nr, nh)
    shard, width = g.x_in.shape
    heads, atoms = g.att.shape[0], g.att.shape[1]
    tiles = atoms // LANES
    kernels, size = g.wk_t.shape[1], g.w_qkv.shape[2]
    units = g.w_up.shape[1]
    at = pl.ds(pl.multiple_of(place.h * shard, shard), shard)
    loads = [pltpu.make_async_copy(g.states.at[at], g.x_in, g.copy_sem.at[0]), pltpu.make_async_copy(g.cots.at[at], g.c_in, g.copy_sem.at[1])]
    for load in loads:
        load.start()
    place.enter()

    half = g.w_time.shape[0] // 2
    row = widen(share(nh, place.h, row_of(g.steps).astype(f32), shard))
    frequency = jnp.exp(lax.broadcasted_iota(jnp.int32, (half, 1), 0).astype(f32) * (-math.log(10000.0) / half))
    angles = frequency * row
    terms = jnp.transpose(jnp.concatenate([jnp.sin(angles), jnp.cos(angles)], axis=0))[:shard].astype(bf16)
    for load in loads:
        load.wait()
    zero = g.x_in[...] + dot(terms, g.w_time[...])
    put_blocks(g.stage_x, turn(zero, nr))
    swap_x = Swap(place, g.stage_x, g.land_x, g.s_x, g.r_x)
    swap_x.start()

    cots = share(nh, place.h, g.cot_forces[...], shard).astype(bf16).astype(f32)
    force = jnp.transpose(widen(jnp.concatenate([cots, jnp.zeros((LANES - 3, shard), f32)], axis=0)))[:shard]
    grad_two = g.c_in[...]
    for j in range(3):
        grad_two = grad_two + force[:, j : j + 1] * g.w_force[j : j + 1, :].astype(f32)
    put_blocks(g.stage_g, turn(jnp.concatenate([grad_two.astype(bf16), terms], axis=1), nr))
    swap_g = Swap(place, g.stage_g, g.land_g, g.s_g, g.r_g)
    swap_g.start()

    ids = g.item_ids[...].astype(f32)
    g.ids[...] = ids
    g.aux[...] = jnp.transpose(jnp.concatenate([g.coords[...], ids, jnp.zeros((LANES - 4, atoms), f32)], axis=0))
    means, widths = row_of(g.means), row_of(g.widths)
    columns = [jnp.transpose(jnp.broadcast_to(value, (LANES, kernels))) for value in (means, widths)]
    gauss_coefs(columns[0], columns[1], g.coef)
    g.spread[...] = spread_weights(g.wk_t[...].astype(f32))
    for part in range(3):
        g.weight[part] = pad_heads([g.w_qkv[h, part] for h in range(heads)])

    def pair_terms(tile):
        pair_tile(tile, g.aux, g.coords, g.ids, g.coef, g.dist, g.pair, g.spread, heads, atoms)

    pair_terms(0)
    swap_x.finish()
    x0 = turn(take_blocks(g.land_x), shard // nr)
    g.x0[...] = x0
    xhat, _ = norm_parts(x0)
    g.n1[place.h] = (xhat * row_of(g.gain1) + row_of(g.bias1)).astype(bf16)
    gather_n = Gather(place, g.n1, g.s_n1, g.r_n1)
    gather_n.start()
    swap_g.finish()
    both = turn(take_blocks(g.land_g), shard // nr).astype(bf16)
    g.gt[place.h] = both[:, :width]
    g.tt[...] = both[:, width:]
    pair_terms(1)
    gather_n.forward()
    gather_t = Gather(place, g.gt, g.s_gt, g.r_gt)
    gather_t.start()
    for tile in range(2, tiles):
        pair_terms(tile)
    gather_n.near()
    gather_n.far()
    gather_n.done()

    normed = g.n1[...].reshape(atoms, width)
    g.qt[...] = dot_nt(g.weight[0], normed).astype(bf16)
    g.kt[...] = dot_nt(g.weight[1], normed).astype(bf16)
    g.vt[...] = dot_nt(g.weight[2], normed).astype(bf16)
    g.q[...] = dot_nt(normed, g.weight[0]).astype(bf16)
    g.k[...] = dot_nt(normed, g.weight[1]).astype(bf16)
    g.v[...] = dot_nt(normed, g.weight[2]).astype(bf16)
    soft_phase(g.pair, g.qt, g.k, g.vt, g.att, g.ctx_t, g.buf0, g.buf1, heads, atoms)
    gather_t.forward()

    g.wo[...] = pad_heads([g.w_out[h] for h in range(heads)])
    g.ctx[...] = flip(g.ctx_t[...]).reshape(g.ctx.shape)
    sum_a = Scatter(place, g.o1a, g.i1a, g.o2a, g.i2a, g.s_a, g.r_a)
    sum_a.start(lambda s: dot(g.ctx[s], g.wo[...]))
    sum_a.middle()
    gather_t.near()
    gather_t.far()
    gather_t.done()
    for s in range(nh):
        g.back[s] = dot_nt(g.gt[s], g.w_down[...])
    one = g.x0[...] + sum_a.finish()
    g.one[...] = one
    xhat, rstd = norm_parts(one)
    g.n2[place.h] = (xhat * row_of(g.gain2) + row_of(g.bias2)).astype(bf16)
    gather_n = Gather(place, g.n2, g.s_n2, g.r_n2)
    gather_n.start()

    def forward(s):
        act, slope = gelu_parts(dot(g.n2[s], g.w_up[...]))
        g.hidden[s] = act.astype(bf16)
        g.pre_grad[s] = (g.back[s] * slope).astype(bf16)

    forward(place.h)
    gather_n.near()
    forward(place.mate)
    gather_n.forward()
    for k in range(1, place.chips):
        forward(place.chip(-k) * 2 + place.c)
    gather_n.far()
    for k in range(1, place.chips):
        forward(place.chip(-k) * 2 + 1 - place.c)
    gather_n.done()

    sum_b = Scatter(place, g.o1b, g.i1b, g.o2b, g.i2b, g.s_b, g.r_b)
    sum_b.start(lambda s: dot_nt(g.pre_grad[s], g.w_up[...]))
    total_down = Total(place, g.down, g.down_out, g.down_got, g.down_part, g.down_line, g.s_dn, g.r_dn)
    total_up = Total(place, g.up, g.up_out, g.up_got, g.up_part, g.up_line, g.s_up, g.r_up)
    total_qo = Total(place, g.qo, g.qo_out, g.qo_got, g.qo_part, g.qo_line, g.s_qo, g.r_qo)
    line = list(range(1, nr // 2))
    g.down[...] = dot(flip(g.hidden[...].reshape(atoms, units)), g.gt[...].reshape(atoms, width)).astype(bf16).reshape(g.down.shape)
    total_down.pair()
    sum_b.middle()
    normed_grad = sum_b.finish()
    one_grad = g.gt[place.h].astype(f32) + norm_back(normed_grad, xhat, rstd, row_of(g.gain2))
    g.one_grad[...] = one_grad
    g.og[place.h] = one_grad.astype(bf16)
    gather_o = Gather(place, g.og, g.s_og, g.r_og)
    gather_o.start()
    g.sums[0:1, :] = column_sum(normed_grad * xhat)
    g.sums[1:2, :] = column_sum(normed_grad)
    g.up[...] = dot(flip(g.n2[...].reshape(atoms, width)), g.pre_grad[...].reshape(atoms, units)).astype(bf16).reshape(g.up.shape)
    total_up.pair()
    total_down.spread(*line[:1])
    gather_o.forward()
    sum_c = Scatter(place, g.o1a, g.i1a, g.o2a, g.i2a, g.s_c, g.r_c)
    sum_c.start(lambda s: dot(g.hidden[s], g.w_down[...]))
    total_down.spread(*line[1:2])
    sum_c.middle()
    gather_o.near()
    gather_o.far()
    gather_o.done()
    grads = g.og[...].reshape(atoms, width)
    g.dc[...] = dot_nt(grads, g.wo[...]).astype(bf16)
    g.dct[...] = dot_nt(g.wo[...], grads).astype(bf16)
    wout = dot(g.ctx_t[...], grads)
    for h in range(heads):
        base = (heads * 3 + h) * size
        g.flat[base : base + size, :] = wout[h * PAD : h * PAD + size]
    total_down.spread(*line[2:], 0)
    two = (g.one[...] + sum_c.finish()).astype(bf16)
    put_blocks(g.stage_s, turn(two, nr))
    swap_s = Swap(place, g.stage_s, g.land_s, g.s_s, g.r_s)
    swap_s.start()

    g.dk_sum[...] = jnp.zeros_like(g.dk_sum)
    g.dv_sum[...] = jnp.zeros_like(g.dv_sum)

    def scores(first, last):
        score_part(first, last, g.att, g.q, g.kt, g.v, g.dc, g.dct, g.pair, g.score0, g.score1, g.buf0, g.buf1, g.dq_t, g.dk_sum, g.dv_sum, heads, atoms)

    scores(0, heads // 2)
    total_up.spread(*line[:2])
    scores(heads // 2, heads)
    total_up.spread(*line[2:], 0)
    total_down.collect()
    swap_s.finish()
    g.full_s[place.h] = turn(take_blocks(g.land_s), shard // nr).astype(bf16)
    gather_s = Gather(place, g.full_s, g.s_fs, g.r_fs)
    gather_s.start()

    g.dq[...] = flip(g.dq_t[...]).reshape(g.dq.shape)
    g.dk[...] = g.dk_sum[...].astype(bf16).reshape(g.dk.shape)
    g.dv[...] = g.dv_sum[...].astype(bf16).reshape(g.dv.shape)
    sum_n = Scatter(place, g.o1b, g.i1b, g.o2b, g.i2b, g.s_n, g.r_n)
    sum_n.start(lambda s: dot(g.dq[s], g.weight[0]) + dot(g.dk[s], g.weight[1]) + dot(g.dv[s], g.weight[2]))
    sum_n.middle()
    normed = g.n1[...].reshape(atoms, width)
    for i, grad in enumerate((g.dq_t[...], flip(g.dk[...].reshape(atoms, -1)), flip(g.dv[...].reshape(atoms, -1)))):
        part = dot(grad, normed)
        for h in range(heads):
            base = (h * 3 + i) * size
            g.flat[base : base + size, :] = part[h * PAD : h * PAD + size]
    slab = g.qo.shape[2]
    for b in range(2):
        for a in range(nr // 2):
            f = b * (nr // 2) + a
            g.qo[b, a] = g.flat[f * slab : (f + 1) * slab, :].astype(bf16)
    total_qo.pair()
    total_down.back(*line)
    total_up.collect()

    grad_n = sum_n.finish()
    xhat, rstd = norm_parts(g.x0[...])
    gs = (g.one_grad[...] + norm_back(grad_n, xhat, rstd, row_of(g.gain1))).astype(bf16)
    put_blocks(g.stage_d, turn(gs, nr))
    swap_d = Swap(place, g.stage_d, g.land_d, g.s_d, g.r_d)
    swap_d.start()
    gather_s.forward()

    put_blocks(g.time_mine, dot(flip(g.tt[...]), gs))
    time_one = []
    for k in range(1, nh):
        to = lax.rem(place.h + k, nh)
        made = remote(g.time_mine.at[to], g.time_part.at[k], g.s_t1.at[k], g.r_t1.at[k], (place.r, to))
        made.start()
        time_one.append(made)

    g.moments[...] = jnp.zeros_like(g.moments)

    def moments(tile):
        moment_tile(tile, g.aux, g.coords, g.coef, g.dist, g.pair, g.moments, heads, atoms)

    moments(0)
    total_qo.spread(*line, 0)
    swap_d.finish()
    g.full_d[place.h] = turn(take_blocks(g.land_d), shard // nr).astype(bf16)
    gather_d = Gather(place, g.full_d, g.s_fd, g.r_fd)
    gather_d.start()
    total_up.back(*line)

    quarter = g.time_mine[place.h].astype(f32)
    for k in range(1, nh):
        time_one[k - 1].wait_recv()
        quarter = quarter + g.time_part[k].astype(f32)
    put_blocks(g.time_land.at[0], quarter)
    time_two = []
    for k in range(1, nr):
        to = lax.rem(place.r + k, nr)
        made = remote(g.time_land.at[0, to], g.time_land.at[1, k], g.s_t2.at[k], g.r_t2.at[k], (to, place.h))
        made.start()
        time_two.append(made)
    moments(1)
    total_qo.collect()
    gather_d.forward()
    for tile in range(2, tiles):
        moments(tile)

    mine = g.time_land[0, place.r]
    for k in range(1, nr):
        time_two[k - 1].wait_recv()
        mine = mine + g.time_land[1, k]
    g.time_full[place.h, place.r] = mine
    time_three = []
    for k in range(1, nr):
        to = lax.rem(place.r + k, nr)
        ref = g.time_full.at[place.h, place.r]
        made = remote(ref, ref, g.s_t3.at[k], g.r_t3.at[k], (to, place.h))
        made.start()
        time_three.append(made)

    fields = jnp.concatenate([cots, jnp.zeros((5, shard), f32)], axis=0).astype(bf16)
    force_grad = dot(fields, g.full_s[place.h])
    kernel_sums = kernel_grads(g.moments, means, widths, g.wk_t[...].astype(f32), heads)
    wide = jnp.concatenate([kernel_sums[1], kernel_sums[2], jnp.zeros((1, width - 2 * kernels), f32)], axis=1)
    g.one_all[place.h] = jnp.concatenate([force_grad[0:3], g.sums[...], column_sum(grad_n * xhat), column_sum(grad_n), wide], axis=0)
    ones = []
    for k in range(1, nh):
        to = lax.rem(place.h + k, nh)
        ref = g.one_all.at[place.h]
        made = remote(ref, ref, g.s_m1.at[k], g.r_m1.at[k], (place.r, to))
        made.start()
        ones.append(made)
    total_qo.back(*line)
    for made in ones:
        made.wait_recv()
    summed = g.one_all[0]
    for j in range(1, nh):
        summed = summed + g.one_all[j]
    g.row_all[place.r, :, 0:width] = summed
    g.row_all[place.r, :, width:] = jnp.concatenate([kernel_sums[0], jnp.zeros((8 - heads, kernels), f32)], axis=0) if heads < 8 else kernel_sums[0]
    rows = []
    for k in range(1, nr):
        to = lax.rem(place.r + k, nr)
        ref = g.row_all.at[place.r]
        made = remote(ref, ref, g.s_m2.at[k], g.r_m2.at[k], (to, place.h))
        made.start()
        rows.append(made)

    gather_s.near()
    gather_s.far()
    gather_s.done()
    g.states_out[...] = g.full_s[...].reshape(atoms, width)
    fields = jnp.concatenate([g.w_force[...].astype(f32), jnp.zeros((5, width), f32)], axis=0).astype(bf16)
    g.forces_out[...] = dot_nt(fields, g.states_out[...])
    gather_d.near()
    gather_d.far()
    gather_d.done()
    g.gs_out[...] = g.full_d[...].reshape(atoms, width)

    for made in time_three:
        made.wait_recv()
    time_four = []
    for k in range(1, nh):
        to = lax.rem(place.h + k, nh)
        ref = g.time_full.at[place.h]
        made = remote(ref, ref, g.s_t4.at[k], g.r_t4.at[k], (place.r, to))
        made.start()
        time_four.append(made)
    for made in rows:
        made.wait_recv()
    total = g.row_all[0]
    for j in range(1, nr):
        total = total + g.row_all[j]
    g.small_out[...] = total
    for made in time_four:
        made.wait_recv()
    piece = g.time_full.shape[2]
    for j in range(nh):
        for i in range(nr):
            base = (j * nr + i) * piece
            g.time_out[base : base + piece, :] = g.time_full[j, i]
    for group in (time_one, time_two, time_three, time_four, ones, rows):
        for made in group:
            made.wait_send()
    total_down.finish()
    total_up.finish()
    total_qo.finish()


def last_kernel(
    up, down, qkv, wout, states, grads, time, small, forces,
    states_out, forces_out, grads_out, time_out, gain1_out, bias1_out, qkv_out, wk_out, means_out, widths_out, wout_out,
    gain2_out, bias2_out, up_out, down_out, force_out,
):
    kernels, width = means_out.shape[0], up.shape[0] * 0 + gain1_out.shape[0]
    up_out[...] = up[...].astype(f32)
    down_out[...] = down[...].astype(f32)
    states_out[...] = states[...].astype(f32)
    grads_out[...] = grads[...].astype(f32)
    time_out[...] = time[...]
    qkv_out[...] = qkv[...].astype(f32).reshape(qkv_out.shape)
    wout_out[...] = wout[...].astype(f32).reshape(wout_out.shape)

    @pl.when(pl.program_id(0) == 0)
    def _():
        forces_out[...] = forces[0:3, :]
        force_out[...] = small[0:3, 0:width]
        gain2_out[...] = small[3, 0:width]
        bias2_out[...] = small[4, 0:width]
        gain1_out[...] = small[5, 0:width]
        bias1_out[...] = small[6, 0:width]
        means_out[...] = small[7, 0:kernels]
        widths_out[...] = small[7, kernels : 2 * kernels]
        wk_out[...] = small[0 : wk_out.shape[0], width:]


VM = pl.BlockSpec(memory_space=pltpu.VMEM)
ANY = pl.BlockSpec(memory_space=pl.ANY)


def S(shape, dtype):
    return jax.ShapeDtypeStruct(shape, dtype)


def V(shape, dtype):
    return pltpu.VMEM(shape, dtype)


def body(
    nr,
    nh,
    atom_states,
    time_steps,
    coords,
    item_ids,
    w_time,
    ln1_gain,
    ln1_bias,
    w_qkv,
    w_kernel,
    kernel_means,
    kernel_widths,
    w_out,
    ln2_gain,
    ln2_bias,
    w_up,
    w_down,
    w_force,
    cot_states,
    cot_forces,
):
    atoms, width = atom_states.shape
    heads, head_dim = w_qkv.shape[1], w_qkv.shape[3]
    kernels, freqs, units = w_kernel.shape[0], w_time.shape[0], w_up.shape[1]
    shard, tiles = atoms // nh, atoms // LANES
    chips, wide, group = nh // 2, heads * PAD, atoms // nr // nh
    lanes, half = 2 * chips - 1, nr // 2
    rows_qo = heads * 4 * head_dim
    quarter = freqs // nh
    piece = quarter // nr
    inputs = dict(
        states=(atom_states, ANY), cots=(cot_states, ANY), steps=(time_steps, VM), cot_forces=(cot_forces, VM), w_time=(w_time, VM),
        w_force=(w_force, VM), gain1=(ln1_gain, VM), bias1=(ln1_bias, VM), gain2=(ln2_gain, VM), bias2=(ln2_bias, VM),
        w_qkv=(jnp.transpose(w_qkv, (1, 2, 3, 0)), VM), w_out=(w_out, VM), w_up=(w_up, VM), w_down=(w_down, VM),
        coords=(coords, VM), item_ids=(item_ids, VM), wk_t=(w_kernel.T, VM), means=(kernel_means, VM), widths=(kernel_widths, VM),
    )
    up_shape, down_shape, qo_shape = [(2, half, rows // nr, lanes_) for rows, lanes_ in ((width, units), (units, width), (rows_qo, width))]
    outputs = dict(
        up_out=S(up_shape, bf16), down_out=S(down_shape, bf16), qo_out=S(qo_shape, bf16), states_out=S((atoms, width), bf16),
        forces_out=S((8, atoms), f32), gs_out=S((atoms, width), bf16), time_out=S((freqs, width), f32),
        small_out=S((8, width + kernels), f32),
    )
    block, three = V((nh, shard, width), bf16), (nh, shard, units)
    rows_t, rows_s = V((wide, atoms), bf16), V((atoms, wide), bf16)
    square, split = V((atoms, atoms), f32), V((nh, shard, wide), bf16)
    land = V((nr, group, width), bf16)
    scratch = dict(
        x_in=V((shard, width), f32), c_in=V((shard, width), f32), x0=V((shard, width), f32), one=V((shard, width), f32),
        one_grad=V((shard, width), f32), stage_x=land, land_x=land, stage_s=land, land_s=land, stage_d=land, land_d=land,
        stage_g=V((nr, group, width + freqs), bf16), land_g=V((nr, group, width + freqs), bf16), tt=V((shard, freqs), bf16),
        ids=V((1, atoms), f32), aux=V((atoms, LANES), f32), coef=V((3, kernels, LANES), f32), dist=V((8, atoms), f32),
        pair=V((tiles, atoms * heads, LANES), f32), spread=V((heads * 2, 2 * kernels), bf16), buf0=square, buf1=square,
        weight=V((3, wide, width), bf16), wo=V((wide, width), bf16), att=V((heads, atoms, atoms), bf16),
        n1=block, gt=block, n2=block, og=block, full_s=block, full_d=block,
        qt=rows_t, kt=rows_t, vt=rows_t, ctx_t=rows_t, dct=rows_t, dq_t=rows_t, q=rows_s, k=rows_s, v=rows_s, dc=rows_s,
        ctx=split, dq=split, dk=split, dv=split, back=V(three, f32), hidden=V(three, bf16), pre_grad=V(three, bf16),
        score0=V((atoms, atoms), bf16), score1=V((atoms, atoms), bf16), dk_sum=V((atoms, wide), f32), dv_sum=V((atoms, wide), f32),
        moments=V((kernels, 8 * heads), f32), sums=V((2, width), f32), flat=V((rows_qo, width), f32),
        time_mine=V((nh, quarter, width), bf16), time_part=V((nh, quarter, width), bf16), time_land=V((2, nr, piece, width), f32),
        time_full=V((nh, nr, piece, width), f32), row_all=V((nr, 8, width + kernels), f32), one_all=V((nh, 8, width), f32),
        copy_sem=pltpu.SemaphoreType.DMA((2,)),
    )
    for letter in "ab":
        for name in ("o1", "i1"):
            scratch[name + letter] = V((chips, shard, width), bf16)
        for name in ("o2", "i2"):
            scratch[name + letter] = V((max(chips - 1, 1), shard, width), bf16)
    for name, shape in (("up", up_shape), ("down", down_shape), ("qo", qo_shape)):
        scratch[name] = V(shape, bf16)
        for suffix in ("_got", "_part", "_line"):
            scratch[name + suffix] = V(shape[1:], bf16)
    counts = dict(n1=lanes, gt=lanes, n2=lanes, og=lanes, fs=lanes, fd=lanes, a=lanes, b=lanes, c=lanes, n=lanes)
    counts.update(x=nr, g=nr, s=nr, d=nr, t1=nh, t2=nr, t3=nr, t4=nh, m1=nh, m2=nr, up=2 * nr, dn=2 * nr, qo=2 * nr)
    for name, count in counts.items():
        scratch["s_" + name] = pltpu.SemaphoreType.DMA((count,))
        scratch["r_" + name] = pltpu.SemaphoreType.DMA((count,))
    names = list(inputs) + list(outputs) + list(scratch)
    up, down, qo, states, forces, grads, time, small = pl.pallas_call(
        functools.partial(layer_kernel, nr, nh, names),
        out_shape=tuple(outputs.values()),
        in_specs=[spec for _, spec in inputs.values()],
        out_specs=(VM,) * len(outputs),
        scratch_shapes=list(scratch.values()),
        name="layer",
        compiler_params=pltpu.CompilerParams(collective_id=1, has_side_effects=True, vmem_limit_bytes=VMEM_MIB << 20),
    )(*[array for array, _ in inputs.values()])

    def rows(n, lanes_):
        return pl.BlockSpec((n, lanes_), lambda i: (i, 0))

    def whole(*shape):
        return pl.BlockSpec(shape, lambda i: (0,) * len(shape))

    qkv_rows = heads * 3 * head_dim
    flat = qo.reshape(rows_qo, width)
    steps = 4
    part = heads // steps
    results = pl.pallas_call(
        last_kernel,
        grid=(steps,),
        out_shape=(
            S((atoms, width), f32), S((3, atoms), f32), S((atoms, width), f32), S((freqs, width), f32), S((width,), f32), S((width,), f32),
            S((heads, 3, head_dim, width), f32), S((heads, kernels), f32), S((kernels,), f32), S((kernels,), f32),
            S((heads, head_dim, width), f32), S((width,), f32), S((width,), f32), S((width, units), f32), S((units, width), f32),
            S((3, width), f32),
        ),
        in_specs=[
            rows(width // steps, units), rows(units // steps, width), rows(qkv_rows // steps, width),
            pl.BlockSpec((heads * head_dim // steps, width), lambda i: (i + 3 * steps, 0)),
            rows(atoms // steps, width), rows(atoms // steps, width), rows(freqs // steps, width), whole(8, width + kernels), whole(8, atoms),
        ],
        out_specs=(
            rows(atoms // steps, width), whole(3, atoms), rows(atoms // steps, width), rows(freqs // steps, width), whole(width), whole(width),
            pl.BlockSpec((part, 3, head_dim, width), lambda i: (i, 0, 0, 0)), whole(heads, kernels), whole(kernels), whole(kernels),
            pl.BlockSpec((part, head_dim, width), lambda i: (i, 0, 0)), whole(width), whole(width),
            rows(width // steps, units), rows(units // steps, width), whole(3, width),
        ),
        name="last",
    )(up.reshape(width, units), down.reshape(units, width), flat, flat, states, grads, time, small, forces)
    results = list(results)
    results[6] = jnp.transpose(results[6], (3, 0, 1, 2))
    results[7] = results[7].T
    return tuple(results)


def solution(mesh):
    in_specs = (
        P("rows", None),
        P("rows"),
        P(None, "rows"),
        P("rows", None),
        P(),
        P(),
        P(),
        P(None, "heads", None, None),
        P(None, "heads"),
        P(),
        P(),
        P("heads", None, None),
        P(),
        P(),
        P(None, "heads"),
        P("heads", None),
        P(),
        P("rows", None),
        P(None, "rows"),
    )
    out_specs = (
        P("rows", None),
        P(None, "rows"),
        P("rows", None),
        P(),
        P(),
        P(),
        P(None, "heads", None, None),
        P(None, "heads"),
        P(),
        P(),
        P("heads", None, None),
        P(),
        P(),
        P(None, "heads"),
        P("heads", None),
        P(),
    )
    step = functools.partial(body, mesh.shape["rows"], mesh.shape["heads"])
    return jax.shard_map(step, mesh=mesh, in_specs=in_specs, out_specs=out_specs, check_vma=False)
```

```python
import functools
import math
import types

import jax
import jax.numpy as jnp
from jax import lax
from jax.experimental import pallas as pl
from jax.experimental.pallas import tpu as pltpu
from jax.sharding import PartitionSpec as P

VMEM_MIB = 62
LOG2E = math.log2(math.e)
CENTRE = 4.0
LANES = 128
PAD = 32
bf16, f32 = jnp.bfloat16, jnp.float32
UNROLL_F = (2, 2, 4, 8)
UNROLL_B = (2, 2, 4, 8)


def dot(a, b):
    return lax.dot_general(a, b, (((1,), (0,)), ((), ())), preferred_element_type=f32)


def dot_nt(a, b):
    return lax.dot_general(a, b, (((1,), (1,)), ((), ())), preferred_element_type=f32)


def head_mask(h, width):
    lane = lax.broadcasted_iota(jnp.int32, (1, width), 1)
    return jnp.where(lane // PAD == h, 1.0, 0.0).astype(bf16)


def gauss_coefs(means, widths, coef):
    inv = 1.0 / (widths * widths)
    shift = means - CENTRE
    half = 0.5 * LOG2E * inv
    coef[0] = jnp.broadcast_to(-half, coef.shape[1:])
    coef[1] = jnp.broadcast_to(2.0 * half * shift, coef.shape[1:])
    norm = -jnp.log(widths * math.sqrt(2.0 * math.pi)) * LOG2E
    coef[2] = jnp.broadcast_to(norm - half * shift * shift, coef.shape[1:])


def distances(row0, aux, coords, first, width):
    total = None
    for axis in range(3):
        delta = aux[pl.ds(row0, 8), axis : axis + 1] - coords[axis : axis + 1, first : first + width]
        total = delta * delta if total is None else total + delta * delta
    return jnp.sqrt(total) - CENTRE


def gauss_value(dist, coef, row, cols):
    kernels = coef.shape[1]
    rows = []
    for piece in range(kernels // 16):
        ks = slice(piece * 16, piece * 16 + 16)
        c0, c1, c2 = coef[0, ks, :], coef[1, ks, :], coef[2, ks, :]
        line = []
        for lane in range(cols.start, cols.stop, LANES):
            d = dist[row : row + 1, lane : lane + LANES]
            line.append(jnp.exp2((d * c0 + c1) * d + c2).astype(bf16))
        rows.append(jnp.concatenate(line, axis=1) if len(line) > 1 else line[0])
    return jnp.concatenate(rows, axis=0)


def chunks(width, step):
    return [slice(at, min(at + step, width)) for at in range(0, width, step)]


def spread_weights(wk_t):
    zero = jnp.zeros_like(wk_t)
    return jnp.concatenate([jnp.concatenate([wk_t, zero], 1), jnp.concatenate([zero, wk_t], 1)], 0).astype(bf16)


def pair_tile(tile, aux, coords, ids, coef, dist, pair, spread, heads, atoms):
    first, width = tile * LANES, atoms - tile * LANES

    def unit(group, carry):
        row0 = pl.multiple_of(first + group * 8, 8)
        dist[:, :width] = distances(row0, aux, coords, first, width)
        same = aux[pl.ds(row0, 8), 3:4] == ids[0:1, first:]
        mask = jnp.where(same, 0.0, -1e30)
        for two in range(4):
            at = pl.ds(pl.multiple_of((row0 + 2 * two) * heads, 2 * heads), 2 * heads)
            for cols in chunks(width, 2 * LANES):
                g = jnp.concatenate([gauss_value(dist, coef, 2 * two + i, cols) for i in range(2)], 0)
                terms = dot(spread[...], g) * LOG2E
                for lane in range(cols.start, cols.stop, LANES):
                    bar = jnp.concatenate([jnp.broadcast_to(mask[2 * two + i : 2 * two + i + 1, lane : lane + LANES], (heads, LANES)) for i in range(2)], 0)
                    pair[tile + lane // LANES, at, :] = terms[:, lane - cols.start : lane - cols.start + LANES] + bar
        return carry

    lax.fori_loop(0, LANES // 8, unit, 0, unroll=UNROLL_F[tile % 4])


def mirror(ref, h, lo, heads, tiles, add):
    for hi in range(lo + 1, tiles):
        near = pl.ds(lo * LANES * heads + h, LANES, stride=heads)
        far = pl.ds(hi * LANES * heads + h, LANES, stride=heads)
        if add:
            ref[hi, near, :] = ref[hi, near, :] + jnp.transpose(ref[lo, far, :])
        else:
            ref[lo, far, :] = jnp.transpose(ref[hi, near, :])


def soft_tile(tile, pair, qt, k, vt, att, ctx_t, bufs, heads, atoms):
    cols = slice(tile * LANES, (tile + 1) * LANES)
    scale = LOG2E / math.sqrt(24)
    together = min(4, heads)

    def step(i, carry):
        for j in range(together):
            h = i * together + j
            mirror(pair, h, tile, heads, atoms // LANES, False)
            bufs[j] = dot(k[...] * head_mask(h, k.shape[1]), qt[:, cols])
        for j in range(together):
            h = i * together + j
            rows = pl.ds(pl.multiple_of(h * PAD, PAD), PAD)
            logits = bufs[j] * scale + pair[tile, pl.ds(h, atoms, stride=heads), :]
            weights = jnp.exp2(logits - jnp.max(logits, axis=0, keepdims=True))
            soft = (weights * (1.0 / jnp.sum(weights, axis=0, keepdims=True))).astype(bf16)
            att[h, :, cols] = soft
            ctx_t[rows, cols] = dot(vt[rows, :], soft).astype(bf16)
        return carry

    lax.fori_loop(0, heads // together, step, 0)


def pieces_of(x):
    a = x.astype(bf16).astype(f32)
    r = x - a
    b = r.astype(bf16).astype(f32)
    return a, b, r - b


def score_part(chip, last, att, q, kt, v, dc, dct, term, bufs, scores, dq_t, dk_sum, dv_sum, heads, atoms):
    span = dc.shape[1]
    tiles = atoms // LANES
    scale = 1.0 / math.sqrt(24)
    start = pl.multiple_of(chip * span, LANES) if span % LANES == 0 else chip * span
    block = pl.ds(start, span)
    together = 2

    def step(i, carry):
        for j in range(together):
            h = i * together + j
            bufs[j] = dot(v[...] * head_mask(h, v.shape[1]), dct[chip])
        for j in range(together):
            h = i * together + j
            mask = head_mask(h, v.shape[1])
            rows = pl.ds(pl.multiple_of(h * PAD, PAD), PAD)
            for part in range(span // LANES):
                cols = slice(part * LANES, (part + 1) * LANES)
                soft = att[h, :, pl.ds(start + part * LANES, LANES)].astype(f32)
                part_sum = soft * bufs[j, :, cols]
                grad = part_sum - soft * jnp.sum(part_sum, axis=0, keepdims=True)
                scores[j, :, cols] = (grad * scale).astype(bf16)
                term[chip * (span // LANES) + part, pl.ds(h, atoms, stride=heads), :] = grad.astype(bf16).astype(f32)
            dq_t[chip, rows, :] = dot(kt[rows, :], scores[j]).astype(bf16)
            dv_sum[...] += dot(att[h, :, block], dc[chip] * mask)
            dk_sum[...] += dot(scores[j], q[block, :] * mask)
            if last:
                for lo in range(tiles):
                    mirror(term, h, lo, heads, tiles, True)
        return carry

    lax.fori_loop(0, heads // together, step, 0)


def moment_tile(tile, begin, end, aux, coords, coef, dist, term, moments, heads, atoms):
    first, width = tile * LANES, atoms - tile * LANES

    def unit(group, carry):
        row0 = pl.multiple_of(first + group * 8, 8)
        dist[:, :width] = distances(row0, aux, coords, first, width)
        total = None
        for row in range(8):
            at = pl.ds(pl.multiple_of((row0 + row) * heads, heads), heads)
            for cols in chunks(width, 2 * LANES):
                lhs = []
                for lane in range(cols.start, cols.stop, LANES):
                    t = term[tile + lane // LANES, at, :].astype(bf16).astype(f32)
                    d = dist[row : row + 1, lane : lane + LANES]
                    x1 = t * d
                    parts = (t,) + pieces_of(x1) + pieces_of(x1 * d) + (jnp.zeros_like(t),)
                    lhs.append(jnp.concatenate(parts, axis=0).astype(bf16))
                lhs = jnp.concatenate(lhs, axis=1) if len(lhs) > 1 else lhs[0]
                out = dot_nt(gauss_value(dist, coef, row, cols), lhs)
                total = out if total is None else total + out
        moments[...] += total
        return carry

    lax.fori_loop(begin, end, unit, 0, unroll=UNROLL_B[tile % 4])


def kernel_grads(moments, means, widths, w, heads):
    kernels = means.shape[1]
    sums = moments[...]
    if sums.shape[1] < LANES:
        sums = jnp.concatenate([sums, jnp.zeros((kernels, LANES - sums.shape[1]), f32)], axis=1)
    flat = jnp.transpose(sums)
    m = [flat[i * heads : (i + 1) * heads] for i in range(7)]
    m0, m1, m2 = m[0], m[1] + m[2] + m[3], m[4] + m[5] + m[6]
    shift = means - CENTRE
    s1 = m1 - shift * m0
    s2 = m2 - 2.0 * shift * m1 + shift * shift * m0
    inv = 1.0 / widths
    mean_grad = jnp.sum(w * s1, axis=0, keepdims=True) * inv * inv
    width_grad = jnp.sum(w * (s2 * inv * inv - m0), axis=0, keepdims=True) * inv
    return m0, mean_grad, width_grad


MESH = pl.DeviceIdType.MESH
epsilon = 1e-05


def remote(src, dst, send, recv, device):
    return pltpu.make_async_remote_copy(
        src_ref=src, dst_ref=dst, send_sem=send, recv_sem=recv, device_id=device, device_id_type=MESH
    )


class Place:
    def __init__(self, nr, nh):
        self.nr, self.nh, self.chips = nr, nh, nh // 2
        self.r, self.h = lax.axis_index("rows"), lax.axis_index("heads")
        self.x, self.c = self.h // 2, lax.rem(self.h, 2)
        self.mate = self.h + 1 - 2 * self.c

    def chip(self, k):
        return lax.rem(self.x + k + self.chips, self.chips)

    def enter(self):
        barrier = pltpu.get_barrier_semaphore()
        for k in range(1, self.nr):
            pl.semaphore_signal(barrier, inc=1, device_id=(lax.rem(self.r + k, self.nr), self.h), device_id_type=MESH)
        for k in range(1, self.nh):
            pl.semaphore_signal(barrier, inc=1, device_id=(self.r, lax.rem(self.h + k, self.nh)), device_id_type=MESH)
        pl.semaphore_wait(barrier, self.nr + self.nh - 2)


class Gather:
    def __init__(self, place, full, send, recv):
        self.place, self.full, self.send, self.recv = place, full, send, recv

    def copy(self, block, to, slot):
        ref = self.full.at[block]
        made = remote(ref, ref, self.send.at[slot], self.recv.at[slot], (self.place.r, to))
        made.start()
        return made

    def start(self):
        p = self.place
        self.along = [self.copy(p.h, p.chip(k) * 2 + p.c, k) for k in range(1, p.chips)]
        self.across = [self.copy(p.h, p.mate, 0)]

    def forward(self):
        p = self.place
        for k in range(1, p.chips):
            self.along[k - 1].wait_recv()
            self.across.append(self.copy(p.chip(-k) * 2 + p.c, p.mate, p.chips - 1 + k))

    def near(self):
        self.across[0].wait_recv()

    def far(self):
        for made in self.across[1:]:
            made.wait_recv()

    def done(self):
        for made in self.along + self.across:
            made.wait_send()


class Scatter:
    def __init__(self, place, out1, in1, keep, out2, in2, send, recv):
        self.place, self.out1, self.in1, self.keep, self.out2, self.in2 = place, out1, in1, keep, out2, in2
        self.send, self.recv = send, recv

    def near(self, xs):
        p = self.place
        return remote(self.out1.at[xs], self.in1.at[xs], self.send.at[xs], self.recv.at[xs], (p.r, p.mate))

    def far(self, xs, cs):
        p = self.place
        return remote(
            self.out2.at[xs], self.in2.at[p.x], self.send.at[p.chips + xs], self.recv.at[p.chips + p.x], (p.r, xs * 2 + cs)
        )

    def put(self, s, value):
        p = self.place
        xs, cs = s // 2, s % 2

        @pl.when(p.c != cs)
        def _():
            self.out1[xs] = value.astype(bf16)
            self.near(xs).start()

        @pl.when(p.c == cs)
        def _():
            self.keep[xs] = value.astype(self.keep.dtype)

    def send_on(self, s):
        p = self.place
        xs, cs = s // 2, s % 2

        @pl.when(jnp.logical_and(p.c == cs, p.x != xs))
        def _():
            self.near(xs).wait_recv()
            self.out2[xs] = (self.keep[xs].astype(f32) + self.in1[xs].astype(f32)).astype(bf16)
            self.far(xs, cs).start()

    def finish(self):
        p = self.place
        self.near(p.x).wait_recv()
        total = self.keep[p.x].astype(f32) + self.in1[p.x].astype(f32)
        for k in range(1, p.chips):
            at = p.chip(k)
            remote(self.out2.at[at], self.in2.at[at], self.send.at[p.chips + at], self.recv.at[p.chips + at], (p.r, p.mate)).wait_recv()
            total = total + self.in2[at].astype(f32)
        for xs in range(p.chips):
            self.near(xs).wait_send()
        for k in range(1, p.chips):
            self.far(p.chip(k), p.c).wait_send()
        return total


class Swap:
    def __init__(self, place, stage, land, send, recv):
        self.place, self.stage, self.land, self.send, self.recv = place, stage, land, send, recv

    def start(self):
        p = self.place
        self.made = []
        for k in range(1, p.nr):
            to = lax.rem(p.r + k, p.nr)
            made = remote(self.stage.at[to], self.land.at[p.r], self.send.at[k], self.recv.at[k], (to, p.h))
            made.start()
            self.made.append(made)
        self.land[p.r] = self.stage[p.r]

    def finish(self):
        for made in self.made:
            made.wait_recv()
        for made in self.made:
            made.wait_send()


def put_blocks(ref, value):
    count, size = ref.shape[0], ref.shape[1]
    for i in range(count):
        ref[i] = value[i * size : (i + 1) * size].astype(ref.dtype)


def take_blocks(ref):
    return jnp.concatenate([ref[i].astype(f32) for i in range(ref.shape[0])], axis=0)


def turn(value, inner):
    rows = value.shape[0]
    outer = rows // inner
    to = lax.broadcasted_iota(jnp.int32, (rows, rows), 0)
    at = lax.broadcasted_iota(jnp.int32, (rows, rows), 1)
    matrix = jnp.where(at == lax.rem(to, outer) * inner + to // outer, 1.0, 0.0).astype(bf16)
    return dot(matrix, value.astype(bf16))


def norm_parts(x):
    centred = x - jnp.mean(x, axis=1, keepdims=True)
    rstd = lax.rsqrt(jnp.mean(centred * centred, axis=1, keepdims=True) + epsilon)
    return centred * rstd, rstd


def norm_back(grad, xhat, rstd, gain):
    dy = grad * gain
    mean1 = jnp.mean(dy, axis=1, keepdims=True)
    mean2 = jnp.mean(dy * xhat, axis=1, keepdims=True)
    return rstd * (dy - mean1 - xhat * mean2)


def column_sum(x):
    return jnp.sum(x, axis=0, keepdims=True)


def flip(x):
    return jnp.transpose(x.astype(f32)).astype(x.dtype)


def pad_heads(parts):
    padded = []
    for part in parts:
        part = part.astype(f32)
        padded += [part, jnp.zeros((PAD - part.shape[0], part.shape[1]), f32)]
    return jnp.concatenate(padded, axis=0).astype(bf16)


class Halve:
    def __init__(self, place, order, data, full, got, send, recv):
        self.place, self.order, self.data, self.full, self.got, self.send, self.recv = place, order, data, full, got, send, recv
        self.n = len(order)
        self.bits = [lax.rem(place.r // 2**bit, 2) for bit in order]
        self.used, self.out = {}, {}

    def device(self, j):
        bit = self.order[j]
        return (self.place.r + 2**bit - 2 ** (bit + 1) * self.bits[j], self.place.h)

    def at(self, flips, length):
        start = 0
        for j in range(length):
            bit = 1 - self.bits[j] if j in flips else self.bits[j]
            start = start + bit * 2 ** (self.n - 1 - j)
        return pl.ds(start, 2 ** (self.n - length))

    def made(self, src, dst, key, j):
        slot = self.used.setdefault(key, len(self.used))
        return remote(src, dst, self.send.at[slot], self.recv.at[slot], self.device(j))

    def piece(self, j, part):
        size = 2 ** (self.n - 1 - j)
        base = 2**self.n - 2 * size
        if part == 2:
            src, land = self.at((j,), j + 1), pl.ds(base, size)
        else:
            src = self.at((j, j + 1) if part == 0 else (j,), j + 2)
            land = pl.ds(base + part * (size // 2), size // 2)
        return self.made(self.data.at[src], self.got.at[land], ("r", j, part), j), land

    def parts(self, j):
        return (2,) if j == self.n - 1 else (0, 1)

    def start(self, j=0):
        for part in self.parts(j):
            self.out[j, part] = self.piece(j, part)
            self.out[j, part][0].start()

    def add(self, j, part):
        copy, land = self.out[j, part]
        copy.wait_recv()
        mine = self.at((), j + 1) if part == 2 else self.at((j + 1,) if part == 0 else (), j + 2)
        self.data[mine] = (self.data[mine].astype(f32) + self.got[land].astype(f32)).astype(bf16)

    def reduce(self, *steps):
        for j in steps:
            if j:
                self.add(j - 1, 1)
            self.add(j, self.parts(j)[0])
            if j < self.n - 1:
                self.start(j + 1)

    def slab(self, flips):
        return self.full.at[self.at(flips, self.n)]

    def give(self, flips, j):
        ref = self.slab(flips)
        made = self.made(ref, ref, ("g", flips, j), j)
        made.start()
        self.out["g", flips, j] = made

    def hand(self):
        mine = self.at((), self.n)
        self.full[mine] = self.data[mine]
        self.have = [()]
        for j in range(self.n - 1, -1, -1):
            self.give((), j)

    def relay(self, *steps):
        for step in steps:
            j = self.n - 1 - step
            news = []
            for flips in self.have:
                self.out["g", flips, j].wait_recv()
                new = tuple(sorted(flips + (j,)))
                for i in range(j - 1, -1, -1):
                    self.give(new, i)
                news.append(new)
            self.have = self.have + news

    def finish(self):
        self.relay(self.n - 1)
        for key, made in self.out.items():
            (made if key[0] == "g" else made[0]).wait_send()


def share(nh, h, value, shard):
    picked = value[:, :shard]
    for j in range(1, nh):
        picked = jnp.where(h == j, value[:, j * shard : (j + 1) * shard], picked)
    return picked


def widen(value):
    lanes = value.shape[1]
    return value if lanes == LANES else jnp.concatenate([value, jnp.zeros((value.shape[0], LANES - lanes), f32)], axis=1)


def row_of(ref):
    return ref[...].reshape(1, ref.shape[0])


def gelu_parts(x):
    below = 0.5 * (1.0 + lax.erf(x * math.sqrt(0.5)))
    return x * below, below + x * (jnp.exp(-0.5 * x * x) * (1.0 / math.sqrt(2.0 * math.pi)))


def layer_kernel(nr, nh, names, *refs):
    g = types.SimpleNamespace(**dict(zip(names, refs)))
    place = Place(nr, nh)
    chips, shard, width = g.keep.shape
    heads, atoms = g.att.shape[0], g.att.shape[1]
    x_in, c_in = g.keep.at[0], g.keep.at[1]
    tiles = atoms // LANES
    kernels, size = g.wk_t.shape[1], g.w_qkv.shape[2]
    units = g.w_up.shape[1]
    at = pl.ds(pl.multiple_of(place.h * shard, shard), shard)
    loads = [pltpu.make_async_copy(g.states.at[at], x_in, g.copy_sem.at[0]), pltpu.make_async_copy(g.cots.at[at], c_in, g.copy_sem.at[1])]
    for load in loads:
        load.start()
    fills = {}
    for i, name in enumerate(("w_time", "w_out", "w_qkv", "w_up", "w_down")):
        fills[name] = pltpu.make_async_copy(getattr(g, name + "_hbm"), getattr(g, name), g.fill_sem.at[i])
        fills[name].start()
    place.enter()
    for name in ("w_time", "w_out", "w_qkv"):
        fills[name].wait()

    g.wo[place.h] = pad_heads([g.w_out[h] for h in range(heads)])
    gather_w = Gather(place, g.wo, g.s_wo, g.r_wo)
    gather_w.start()

    half = g.w_time.shape[0] // 2
    row = widen(share(nh, place.h, row_of(g.steps).astype(f32), shard))
    frequency = jnp.exp(lax.broadcasted_iota(jnp.int32, (half, 1), 0).astype(f32) * (-math.log(10000.0) / half))
    angles = frequency * row
    terms = jnp.transpose(jnp.concatenate([jnp.sin(angles), jnp.cos(angles)], axis=0))[:shard].astype(bf16)
    for load in loads:
        load.wait()
    zero = x_in[...] + dot(terms, g.w_time[...])
    put_blocks(g.stage_x, turn(zero, nr))
    swap_x = Swap(place, g.stage_x, g.land_x, g.s_x, g.r_x)
    swap_x.start()

    cots = share(nh, place.h, g.cot_forces[...], shard).astype(bf16).astype(f32)
    force = jnp.transpose(widen(jnp.concatenate([cots, jnp.zeros((LANES - 3, shard), f32)], axis=0)))[:shard]
    grad_two = c_in[...]
    for j in range(3):
        grad_two = grad_two + force[:, j : j + 1] * g.w_force[j : j + 1, :].astype(f32)
    put_blocks(g.stage_g, turn(jnp.concatenate([grad_two.astype(bf16), terms], axis=1), nr))
    swap_g = Swap(place, g.stage_g, g.land_g, g.s_g, g.r_g)
    swap_g.start()

    ids = g.item_ids[...].astype(f32)
    g.ids[...] = ids
    g.aux[...] = jnp.transpose(jnp.concatenate([g.coords[...], ids, jnp.zeros((LANES - 4, atoms), f32)], axis=0))
    means, widths = row_of(g.means), row_of(g.widths)
    columns = [jnp.transpose(jnp.broadcast_to(value, (LANES, kernels))) for value in (means, widths)]
    gauss_coefs(columns[0], columns[1], g.coef)
    g.spread[...] = spread_weights(g.wk_t[...].astype(f32))
    for part in range(3):
        g.weight[part] = pad_heads([g.w_qkv[h, part] for h in range(heads)])

    def pair_terms(tile):
        pair_tile(tile, g.aux, g.coords, g.ids, g.coef, g.dist, g.pair, g.spread, heads, atoms)

    pair_terms(0)
    swap_x.finish()
    g.x0[place.h] = turn(take_blocks(g.land_x), shard // nr).astype(bf16)
    gather_x = Gather(place, g.x0, g.s_x0, g.r_x0)
    gather_x.start()
    gather_w.forward()
    swap_g.finish()
    both = turn(take_blocks(g.land_g), shard // nr).astype(bf16)
    g.gt[place.h] = both[:, :width]
    g.tt[...] = both[:, width:]
    pair_terms(1)
    gather_x.forward()
    gather_t = Gather(place, g.gt, g.s_gt, g.r_gt)
    gather_t.start()
    for tile in range(2, tiles):
        pair_terms(tile)
    gather_x.near()
    gather_x.far()
    gather_x.done()
    for s in range(nh):
        xhat, _ = norm_parts(g.x0[s].astype(f32))
        g.n1[s] = (xhat * row_of(g.gain1) + row_of(g.bias1)).astype(bf16)
    normed = g.n1[...].reshape(atoms, width)
    g.qt[...] = dot_nt(g.weight[0], normed).astype(bf16)
    g.kt[...] = dot_nt(g.weight[1], normed).astype(bf16)
    g.vt[...] = dot_nt(g.weight[2], normed).astype(bf16)
    g.q[...] = dot_nt(normed, g.weight[0]).astype(bf16)
    g.k[...] = dot_nt(normed, g.weight[1]).astype(bf16)
    g.v[...] = dot_nt(normed, g.weight[2]).astype(bf16)
    gather_t.forward()
    gather_t.near()
    gather_t.far()
    gather_w.near()
    gather_w.far()

    gathers = []
    for tile in range(tiles):
        soft_tile(tile, g.pair, g.qt, g.k, g.vt, g.att, g.ctx_t, g.bufs, heads, atoms)
        g.ctx[tile, place.h] = flip(g.ctx_t[:, tile * LANES : (tile + 1) * LANES])
        gathers.append(Gather(place, g.ctx.at[tile], g.s_cx.at[tile], g.r_cx.at[tile]))
        gathers[-1].start()
        if tile:
            gathers[-2].forward()

    fills["w_up"].wait()
    fills["w_down"].wait()
    sum_b = Scatter(place, g.o1b, g.i1b, g.keep, g.o2b, g.i2b, g.s_b, g.r_b)
    each = LANES // shard
    for tile in range(tiles):
        pieces = [tile * each + i for i in range(each)]

        def rows_of(ref):
            return ref[tile] if each == 1 else jnp.concatenate([ref[s] for s in pieces], axis=0)

        def store(ref, value):
            for i, s in enumerate(pieces):
                ref[s] = value[i * shard : (i + 1) * shard].astype(ref.dtype)

        if tile == tiles - 1:
            gathers[-1].forward()
        back = dot_nt(rows_of(g.gt), g.w_down[...])
        gathers[tile].near()
        gathers[tile].far()
        one = rows_of(g.x0).astype(f32)
        for j in range(nh):
            one = one + dot(g.ctx[tile, j], g.wo[j])
        store(g.one, one)
        xhat, _ = norm_parts(one)
        normed = (xhat * row_of(g.gain2) + row_of(g.bias2)).astype(bf16)
        store(g.n2, normed)
        act, slope = gelu_parts(dot(normed, g.w_up[...]))
        store(g.hidden, act)
        pre_grad = (back * slope).astype(bf16)
        store(g.pre_grad, pre_grad)
        value = dot_nt(pre_grad, g.w_up[...])
        for i, s in enumerate(pieces):
            sum_b.put(s, value[i * shard : (i + 1) * shard])
        if tile:
            for s in range((tile - 1) * each, tile * each):
                sum_b.send_on(s)

    bits = list(range(nr.bit_length() - 1))
    total_down = Halve(place, [1, 0] + bits[2:], g.down, g.down_out, g.down_got, g.s_dn, g.r_dn)
    total_up = Halve(place, bits, g.up, g.up_out, g.up_got, g.s_up, g.r_up)
    total_qo = Halve(place, bits, g.qo, g.qo_out, g.qo_got, g.s_qo, g.r_qo)
    steps = bits
    g.down[...] = dot(flip(g.hidden[...].reshape(atoms, units)), g.gt[...].reshape(atoms, width)).astype(bf16).reshape(g.down.shape)
    total_down.start()
    for s in range((tiles - 1) * each, tiles * each):
        sum_b.send_on(s)
    g.up[...] = dot(flip(g.n2[...].reshape(atoms, width)), g.pre_grad[...].reshape(atoms, units)).astype(bf16).reshape(g.up.shape)
    total_up.start()
    normed_grad = sum_b.finish()
    xhat, rstd = norm_parts(g.one[place.h])
    one_grad = g.gt[place.h].astype(f32) + norm_back(normed_grad, xhat, rstd, row_of(g.gain2))
    g.one_grad[...] = one_grad
    g.og[place.h] = one_grad.astype(bf16)
    gather_o = Gather(place, g.og, g.s_og, g.r_og)
    gather_o.start()
    g.sums[0:1, :] = column_sum(normed_grad * xhat)
    g.sums[1:2, :] = column_sum(normed_grad)
    g.dk_sum[...] = jnp.zeros_like(g.dk_sum)
    g.dv_sum[...] = jnp.zeros_like(g.dv_sum)

    def out_grads(chip):
        for c in range(2):
            s = chip * 2 + c
            at = slice(c * shard, (c + 1) * shard)
            g.dc[chip, at, :] = dot_nt(g.og[s], g.wo[place.h]).astype(bf16)
        grads = jnp.concatenate([g.og[chip * 2], g.og[chip * 2 + 1]], axis=0)
        g.dct[chip] = dot_nt(g.wo[place.h], grads).astype(bf16)

    def scores(chip, last):
        score_part(chip, last, g.att, g.q, g.kt, g.v, g.dc, g.dct, g.pair, g.bufs2, g.scores, g.dq_t, g.dk_sum, g.dv_sum, heads, atoms)

    gather_o.near()
    out_grads(place.x)
    scores(place.x, False)
    gather_o.forward()
    total_down.reduce(0)
    total_up.reduce(0)
    gather_o.far()
    for k in range(1, chips):
        out_grads(place.chip(k))
        scores(place.chip(k), k == chips - 1)

    total_down.reduce(*steps[1:-1])
    total_up.reduce(*steps[1:-1])
    dq_t = jnp.concatenate([g.dq_t[x] for x in range(chips)], axis=1)
    g.dq[...] = flip(dq_t).reshape(g.dq.shape)
    g.dk[...] = g.dk_sum[...].astype(bf16).reshape(g.dk.shape)
    g.dv[...] = g.dv_sum[...].astype(bf16).reshape(g.dv.shape)
    normed = g.n1[...].reshape(atoms, width)
    for i, grad in enumerate((dq_t, flip(g.dk[...].reshape(atoms, -1)), flip(g.dv[...].reshape(atoms, -1)))):
        g.parts[i] = dot(grad, normed).astype(bf16)
    g.parts[3] = dot(g.ctx_t[...], g.og[...].reshape(atoms, width)).astype(bf16)
    chosen = [(i, h) for h in range(heads) for i in range(3)] + [(3, h) for h in range(heads)]
    flat = [g.parts[i, h * PAD : (h + 1) * PAD, :].astype(f32)[:size] for i, h in chosen]
    slab = g.qo.shape[1]
    for f in range(nr):
        first, last = f * slab // size, -(-(f + 1) * slab // size)
        rows = jnp.concatenate(flat[first:last], axis=0) if last - first > 1 else flat[first]
        begin = f * slab - first * size
        g.qo[f] = rows[begin : begin + slab].astype(bf16)

    total_qo.start()
    sum_n = Scatter(place, g.o1b, g.i1b, g.keep, g.o2b, g.i2b, g.s_n, g.r_n)
    for s in range(nh):
        sum_n.put(s, dot(g.dq[s], g.weight[0]) + dot(g.dk[s], g.weight[1]) + dot(g.dv[s], g.weight[2]))
    for s in range(nh):
        sum_n.send_on(s)

    sum_c = Scatter(place, g.o1a, g.i1a, g.keep_c, g.o2a, g.i2a, g.s_c, g.r_c)
    for s in range(nh):
        sum_c.put(s, dot(g.hidden[s], g.w_down[...]))
    for s in range(nh):
        sum_c.send_on(s)

    total_down.reduce(steps[-1])
    total_down.hand()
    total_up.reduce(steps[-1])
    total_up.hand()
    grad_n = sum_n.finish()
    xhat, rstd = norm_parts(g.x0[place.h].astype(f32))
    gs = (g.one_grad[...] + norm_back(grad_n, xhat, rstd, row_of(g.gain1))).astype(bf16)
    put_blocks(g.stage_d, turn(gs, nr))
    swap_d = Swap(place, g.stage_d, g.land_d, g.s_d, g.r_d)
    swap_d.start()
    put_blocks(g.time_mine, dot(flip(g.tt[...]), gs))
    time_one = []
    for k in range(1, nh):
        to = lax.rem(place.h + k, nh)
        made = remote(g.time_mine.at[to], g.time_part.at[k], g.s_t1.at[k], g.r_t1.at[k], (place.r, to))
        made.start()
        time_one.append(made)
    two = (g.one[place.h] + sum_c.finish()).astype(bf16)
    put_blocks(g.stage_x, turn(two, nr))
    swap_s = Swap(place, g.stage_x, g.land_s, g.s_s, g.r_s)
    swap_s.start()

    total_qo.reduce(0)
    total_down.relay(0)
    total_up.relay(0)
    g.moments[...] = jnp.zeros_like(g.moments)
    groups = LANES // 8

    def moments(tile, begin, end):
        moment_tile(tile, begin, end, g.aux, g.coords, g.coef, g.dist, g.pair, g.moments, heads, atoms)

    moments(0, 0, groups // 2)
    swap_d.finish()
    g.gs_out[place.h] = turn(take_blocks(g.land_d), shard // nr).astype(bf16)
    gather_d = Gather(place, g.gs_out, g.s_fd, g.r_fd)
    gather_d.start()
    total_qo.reduce(*steps[1:-1])
    total_down.relay(*steps[1:-1])
    total_up.relay(*steps[1:-1])
    quarter = g.time_mine[place.h].astype(f32)
    for k in range(1, nh):
        time_one[k - 1].wait_recv()
        quarter = quarter + g.time_part[k].astype(f32)
    put_blocks(g.time_land.at[0], quarter)
    time_two = []
    for k in range(1, nr):
        to = lax.rem(place.r + k, nr)
        made = remote(g.time_land.at[0, to], g.time_land.at[1, k], g.s_t2.at[k], g.r_t2.at[k], (to, place.h))
        made.start()
        time_two.append(made)

    moments(0, groups // 2, groups)
    swap_s.finish()
    g.states_out[place.h] = turn(take_blocks(g.land_s), shard // nr).astype(bf16)
    gather_s = Gather(place, g.states_out, g.s_fs, g.r_fs)
    gather_s.start()
    gather_d.forward()
    total_qo.reduce(steps[-1])
    total_qo.hand()

    moments(1, 0, groups // 2)
    total_qo.relay(0)
    mine = g.time_land[0, place.r]
    for k in range(1, nr):
        time_two[k - 1].wait_recv()
        mine = mine + g.time_land[1, k]
    g.time_full[place.h, place.r] = mine
    time_three = []
    for k in range(1, nr):
        to = lax.rem(place.r + k, nr)
        ref = g.time_full.at[place.h, place.r]
        made = remote(ref, ref, g.s_t3.at[k], g.r_t3.at[k], (to, place.h))
        made.start()
        time_three.append(made)

    moments(1, groups // 2, groups)
    gather_s.forward()
    for tile in range(2, tiles):
        moments(tile, 0, groups)
        if tile == 2:
            total_qo.relay(*steps[1:-1])

    fields = jnp.concatenate([cots, jnp.zeros((5, shard), f32)], axis=0).astype(bf16)
    force_grad = dot(fields, g.states_out[place.h])
    kernel_sums = kernel_grads(g.moments, means, widths, g.wk_t[...].astype(f32), heads)
    wide = jnp.concatenate([kernel_sums[1], kernel_sums[2], jnp.zeros((1, width - 2 * kernels), f32)], axis=1)
    g.one_all[place.h] = jnp.concatenate([force_grad[0:3], g.sums[...], column_sum(grad_n * xhat), column_sum(grad_n), wide], axis=0)
    ones = []
    for k in range(1, nh):
        to = lax.rem(place.h + k, nh)
        ref = g.one_all.at[place.h]
        made = remote(ref, ref, g.s_m1.at[k], g.r_m1.at[k], (place.r, to))
        made.start()
        ones.append(made)
    for made in time_three:
        made.wait_recv()
    time_four = []
    for k in range(1, nh):
        to = lax.rem(place.h + k, nh)
        ref = g.time_full.at[place.h]
        made = remote(ref, ref, g.s_t4.at[k], g.r_t4.at[k], (place.r, to))
        made.start()
        time_four.append(made)
    for made in ones:
        made.wait_recv()
    summed = g.one_all[0]
    for j in range(1, nh):
        summed = summed + g.one_all[j]
    g.row_all[place.r, :, 0:width] = summed
    g.row_all[place.r, :, width:] = jnp.concatenate([kernel_sums[0], jnp.zeros((8 - heads, kernels), f32)], axis=0) if heads < 8 else kernel_sums[0]
    rows = []
    for k in range(1, nr):
        to = lax.rem(place.r + k, nr)
        ref = g.row_all.at[place.r]
        made = remote(ref, ref, g.s_m2.at[k], g.r_m2.at[k], (to, place.h))
        made.start()
        rows.append(made)

    gather_s.near()
    gather_s.far()
    fields = jnp.concatenate([g.w_force[...].astype(f32), jnp.zeros((5, width), f32)], axis=0).astype(bf16)
    g.forces_out[...] = dot_nt(fields, g.states_out[...].reshape(atoms, width))
    gather_d.near()
    gather_d.far()
    for made in time_four:
        made.wait_recv()
    piece = g.time_full.shape[2]
    for j in range(nh):
        for i in range(nr):
            base = (j * nr + i) * piece
            g.time_out[base : base + piece, :] = g.time_full[j, i]
    for made in rows:
        made.wait_recv()
    total = g.row_all[0]
    for j in range(1, nr):
        total = total + g.row_all[j]
    g.small_out[...] = total
    for gather in gathers + [gather_t, gather_w, gather_o, gather_s, gather_d]:
        gather.done()
    for group in (time_one, time_two, time_three, time_four, ones, rows):
        for made in group:
            made.wait_send()
    total_down.finish()
    total_up.finish()
    total_qo.finish()


def last_kernel(
    up, down, qkv, wout, states, grads, time, small, forces,
    states_out, forces_out, grads_out, time_out, gain1_out, bias1_out, qkv_out, wk_out, means_out, widths_out, wout_out,
    gain2_out, bias2_out, up_out, down_out, force_out,
):
    kernels, width = means_out.shape[0], up.shape[0] * 0 + gain1_out.shape[0]
    up_out[...] = up[...].astype(f32)
    down_out[...] = down[...].astype(f32)
    states_out[...] = states[...].astype(f32)
    grads_out[...] = grads[...].astype(f32)
    time_out[...] = time[...]
    qkv_out[...] = qkv[...].astype(f32).reshape(qkv_out.shape)
    wout_out[...] = wout[...].astype(f32).reshape(wout_out.shape)

    @pl.when(pl.program_id(0) == 0)
    def _():
        forces_out[...] = forces[0:3, :]
        force_out[...] = small[0:3, 0:width]
        gain2_out[...] = small[3, 0:width]
        bias2_out[...] = small[4, 0:width]
        gain1_out[...] = small[5, 0:width]
        bias1_out[...] = small[6, 0:width]
        means_out[...] = small[7, 0:kernels]
        widths_out[...] = small[7, kernels : 2 * kernels]
        wk_out[...] = small[0 : wk_out.shape[0], width:]


VM = pl.BlockSpec(memory_space=pltpu.VMEM)
ANY = pl.BlockSpec(memory_space=pl.ANY)


def S(shape, dtype):
    return jax.ShapeDtypeStruct(shape, dtype)


def V(shape, dtype):
    return pltpu.VMEM(shape, dtype)


def body(
    nr,
    nh,
    atom_states,
    time_steps,
    coords,
    item_ids,
    w_time,
    ln1_gain,
    ln1_bias,
    w_qkv,
    w_kernel,
    kernel_means,
    kernel_widths,
    w_out,
    ln2_gain,
    ln2_bias,
    w_up,
    w_down,
    w_force,
    cot_states,
    cot_forces,
):
    atoms, width = atom_states.shape
    heads, head_dim = w_qkv.shape[1], w_qkv.shape[3]
    kernels, freqs, units = w_kernel.shape[0], w_time.shape[0], w_up.shape[1]
    shard, tiles = atoms // nh, atoms // LANES
    chips, wide, group = nh // 2, heads * PAD, atoms // nr // nh
    lanes = 2 * chips - 1
    rows_qo = heads * 4 * head_dim
    quarter = freqs // nh
    piece = quarter // nr
    inputs = dict(
        states=(atom_states, ANY), cots=(cot_states, ANY), steps=(time_steps, VM), cot_forces=(cot_forces, VM), w_time_hbm=(w_time, ANY),
        w_force=(w_force, VM), gain1=(ln1_gain, VM), bias1=(ln1_bias, VM), gain2=(ln2_gain, VM), bias2=(ln2_bias, VM),
        w_qkv_hbm=(jnp.transpose(w_qkv, (1, 2, 3, 0)), ANY), w_out_hbm=(w_out, ANY), w_up_hbm=(w_up, ANY), w_down_hbm=(w_down, ANY),
        coords=(coords, VM), item_ids=(item_ids, VM), wk_t=(w_kernel.T, VM), means=(kernel_means, VM), widths=(kernel_widths, VM),
    )
    up_shape, down_shape, qo_shape = (nr, width // nr, units), (nr, units // nr, width), (nr, rows_qo // nr, width)
    outputs = dict(
        up_out=S(up_shape, bf16), down_out=S(down_shape, bf16), qo_out=S(qo_shape, bf16), states_out=S((nh, shard, width), bf16),
        forces_out=S((8, atoms), f32), gs_out=S((nh, shard, width), bf16), time_out=S((freqs, width), f32),
        small_out=S((8, width + kernels), f32),
    )
    block, three = V((nh, shard, width), bf16), (nh, shard, units)
    rows_t, rows_s = V((wide, atoms), bf16), V((atoms, wide), bf16)
    split = V((nh, shard, wide), bf16)
    land = V((nr, group, width), bf16)
    scratch = dict(
        keep=V((chips, shard, width), f32), keep_c=V((chips, shard, width), bf16), x0=block, one=V((nh, shard, width), f32),
        one_grad=V((shard, width), f32), stage_x=land, land_x=land, land_s=land, stage_d=land, land_d=land,
        stage_g=V((nr, group, width + freqs), bf16), land_g=V((nr, group, width + freqs), bf16), tt=V((shard, freqs), bf16),
        ids=V((1, atoms), f32), aux=V((atoms, LANES), f32), coef=V((3, kernels, LANES), f32), dist=V((8, atoms), f32),
        pair=V((tiles, atoms * heads, LANES), f32), spread=V((heads * 2, 2 * kernels), bf16), bufs=V((min(4, heads), atoms, LANES), f32), bufs2=V((2, atoms, atoms // chips), f32), scores=V((2, atoms, atoms // chips), bf16),
        weight=V((3, wide, width), bf16), wo=V((nh, wide, width), bf16), att=V((heads, atoms, atoms), bf16),
        n1=block, gt=block, n2=block, og=block,
        qt=rows_t, kt=rows_t, vt=rows_t, ctx_t=rows_t, dct=V((chips, wide, atoms // chips), bf16), dq_t=V((chips, wide, atoms // chips), bf16), q=rows_s, k=rows_s, v=rows_s,
        dc=V((chips, atoms // chips, wide), bf16),
        ctx=V((tiles, nh, LANES, wide), bf16), dq=split, dk=split, dv=split, hidden=V(three, bf16), pre_grad=V(three, bf16),
        dk_sum=V((atoms, wide), f32), dv_sum=V((atoms, wide), f32),
        moments=V((kernels, 8 * heads), f32), sums=V((2, width), f32), parts=V((4, wide, width), bf16),
        time_mine=V((nh, quarter, width), bf16), time_part=V((nh, quarter, width), bf16), time_land=V((2, nr, piece, width), f32),
        time_full=V((nh, nr, piece, width), f32), row_all=V((nr, 8, width + kernels), f32), one_all=V((nh, 8, width), f32),
        w_time=V(w_time.shape, bf16), w_out=V(w_out.shape, bf16), w_up=V(w_up.shape, bf16), w_down=V(w_down.shape, bf16),
        w_qkv=V((heads, 3, head_dim, width), bf16), fill_sem=pltpu.SemaphoreType.DMA((5,)),
        copy_sem=pltpu.SemaphoreType.DMA((2,)),
    )
    for letter in "ab":
        for name in ("o1", "i1"):
            scratch[name + letter] = V((chips, shard, width), bf16)
        for name in ("o2", "i2"):
            scratch[name + letter] = V((chips, shard, width), bf16)
    for name, shape in (("up", up_shape), ("down", down_shape), ("qo", qo_shape)):
        scratch[name] = V(shape, bf16)
        scratch[name + "_got"] = V(shape, bf16)
    counts = dict(wo=lanes, x0=lanes, gt=lanes, og=lanes, fs=lanes, fd=lanes, b=2 * chips, c=2 * chips, n=2 * chips)
    counts.update(x=nr, g=nr, s=nr, d=nr, t1=nh, t2=nr, t3=nr, t4=nh, m1=nh, m2=nr, up=4 * nr, dn=4 * nr, qo=4 * nr)
    for name, count in counts.items():
        scratch["s_" + name] = pltpu.SemaphoreType.DMA((count,))
        scratch["r_" + name] = pltpu.SemaphoreType.DMA((count,))
    for letter in "sr":
        scratch[letter + "_cx"] = pltpu.SemaphoreType.DMA((tiles, lanes))
    names = list(inputs) + list(outputs) + list(scratch)
    up, down, qo, states, forces, grads, time, small = pl.pallas_call(
        functools.partial(layer_kernel, nr, nh, names),
        out_shape=tuple(outputs.values()),
        in_specs=[spec for _, spec in inputs.values()],
        out_specs=(VM,) * len(outputs),
        scratch_shapes=list(scratch.values()),
        name="layer",
        compiler_params=pltpu.CompilerParams(collective_id=1, has_side_effects=True, vmem_limit_bytes=VMEM_MIB << 20),
    )(*[array for array, _ in inputs.values()])

    def rows(n, lanes_):
        return pl.BlockSpec((n, lanes_), lambda i: (i, 0))

    def whole(*shape):
        return pl.BlockSpec(shape, lambda i: (0,) * len(shape))

    qkv_rows = heads * 3 * head_dim
    flat = qo.reshape(rows_qo, width)
    steps = 4
    part = heads // steps
    results = pl.pallas_call(
        last_kernel,
        grid=(steps,),
        out_shape=(
            S((atoms, width), f32), S((3, atoms), f32), S((atoms, width), f32), S((freqs, width), f32), S((width,), f32), S((width,), f32),
            S((heads, 3, head_dim, width), f32), S((heads, kernels), f32), S((kernels,), f32), S((kernels,), f32),
            S((heads, head_dim, width), f32), S((width,), f32), S((width,), f32), S((width, units), f32), S((units, width), f32),
            S((3, width), f32),
        ),
        in_specs=[
            rows(width // steps, units), rows(units // steps, width), rows(qkv_rows // steps, width),
            pl.BlockSpec((heads * head_dim // steps, width), lambda i: (i + 3 * steps, 0)),
            rows(atoms // steps, width), rows(atoms // steps, width), rows(freqs // steps, width), whole(8, width + kernels), whole(8, atoms),
        ],
        out_specs=(
            rows(atoms // steps, width), whole(3, atoms), rows(atoms // steps, width), rows(freqs // steps, width), whole(width), whole(width),
            pl.BlockSpec((part, 3, head_dim, width), lambda i: (i, 0, 0, 0)), whole(heads, kernels), whole(kernels), whole(kernels),
            pl.BlockSpec((part, head_dim, width), lambda i: (i, 0, 0)), whole(width), whole(width),
            rows(width // steps, units), rows(units // steps, width), whole(3, width),
        ),
        name="last",
    )(up.reshape(width, units), down.reshape(units, width), flat, flat, states.reshape(atoms, width), grads.reshape(atoms, width), time, small, forces)
    results = list(results)
    results[6] = jnp.transpose(results[6], (3, 0, 1, 2))
    results[7] = results[7].T
    return tuple(results)


def solution(mesh):
    in_specs = (
        P("rows", None),
        P("rows"),
        P(None, "rows"),
        P("rows", None),
        P(),
        P(),
        P(),
        P(None, "heads", None, None),
        P(None, "heads"),
        P(),
        P(),
        P("heads", None, None),
        P(),
        P(),
        P(None, "heads"),
        P("heads", None),
        P(),
        P("rows", None),
        P(None, "rows"),
    )
    out_specs = (
        P("rows", None),
        P(None, "rows"),
        P("rows", None),
        P(),
        P(),
        P(),
        P(None, "heads", None, None),
        P(None, "heads"),
        P(),
        P(),
        P("heads", None, None),
        P(),
        P(),
        P(None, "heads"),
        P("heads", None),
        P(),
    )
    step = functools.partial(body, mesh.shape["rows"], mesh.shape["heads"])
    return jax.shard_map(step, mesh=mesh, in_specs=in_specs, out_specs=out_specs, check_vma=False)
```

```python
import functools
import math
import types

import jax
import jax.numpy as jnp
from jax import lax
from jax.experimental import pallas as pl
from jax.experimental.pallas import tpu as pltpu
from jax.sharding import PartitionSpec as P

VMEM_MIB = 62
LOG2E = math.log2(math.e)
CENTRE = 4.0
LANES = 128
PAD = 32
bf16, f32 = jnp.bfloat16, jnp.float32
UNROLL_F = (2, 2, 4, 8)
UNROLL_B = (2, 2, 4, 8)


def dot(a, b):
    return lax.dot_general(a, b, (((1,), (0,)), ((), ())), preferred_element_type=f32)


def dot_nt(a, b):
    return lax.dot_general(a, b, (((1,), (1,)), ((), ())), preferred_element_type=f32)


def head_mask(h, width):
    lane = lax.broadcasted_iota(jnp.int32, (1, width), 1)
    return jnp.where(lane // PAD == h, 1.0, 0.0).astype(bf16)


def gauss_coefs(means, widths, coef):
    inv = 1.0 / (widths * widths)
    shift = means - CENTRE
    half = 0.5 * LOG2E * inv
    coef[0] = jnp.broadcast_to(-half, coef.shape[1:])
    coef[1] = jnp.broadcast_to(2.0 * half * shift, coef.shape[1:])
    norm = -jnp.log(widths * math.sqrt(2.0 * math.pi)) * LOG2E
    coef[2] = jnp.broadcast_to(norm - half * shift * shift, coef.shape[1:])


def distances(row0, aux, coords, first, width):
    total = None
    for axis in range(3):
        delta = aux[pl.ds(row0, 8), axis : axis + 1] - coords[axis : axis + 1, first : first + width]
        total = delta * delta if total is None else total + delta * delta
    return jnp.sqrt(total) - CENTRE


def gauss_value(dist, coef, row, cols):
    kernels = coef.shape[1]
    rows = []
    for piece in range(kernels // 16):
        ks = slice(piece * 16, piece * 16 + 16)
        c0, c1, c2 = coef[0, ks, :], coef[1, ks, :], coef[2, ks, :]
        line = []
        for lane in range(cols.start, cols.stop, LANES):
            d = dist[row : row + 1, lane : lane + LANES]
            line.append(jnp.exp2((d * c0 + c1) * d + c2).astype(bf16))
        rows.append(jnp.concatenate(line, axis=1) if len(line) > 1 else line[0])
    return jnp.concatenate(rows, axis=0)


def chunks(width, step):
    return [slice(at, min(at + step, width)) for at in range(0, width, step)]


def spread_weights(own, mate):
    blocks = []
    for w in (own, mate):
        zero = jnp.zeros_like(w)
        blocks += [jnp.concatenate([w, zero], 1), jnp.concatenate([zero, w], 1)]
    return jnp.concatenate(blocks, 0).astype(bf16)


def pair_tile(tile, core, aux, coords, ids, coef, dist, pair, stage, base, spread, heads, atoms):
    first, width = tile * LANES, atoms - tile * LANES
    part = LANES // 2

    def unit(group, carry):
        local = pl.multiple_of(group * 8, 8)
        row0 = pl.multiple_of(first + core * part + group * 8, 8)
        dist[:, :width] = distances(row0, aux, coords, first, width)
        same = aux[pl.ds(row0, 8), 3:4] == ids[0:1, first:]
        mask = jnp.where(same, 0.0, -1e30)
        for two in range(4):
            at = pl.ds(pl.multiple_of((row0 + 2 * two) * heads, 2 * heads), 2 * heads)
            to = pl.ds(pl.multiple_of((local + 2 * two) * heads, 2 * heads), 2 * heads)
            for cols in chunks(width, 2 * LANES):
                g = jnp.concatenate([gauss_value(dist, coef, 2 * two + i, cols) for i in range(2)], 0)
                terms = dot(spread[...], g) * LOG2E
                for lane in range(cols.start, cols.stop, LANES):
                    bar = jnp.concatenate([jnp.broadcast_to(mask[2 * two + i : 2 * two + i + 1, lane : lane + LANES], (heads, LANES)) for i in range(2)], 0)
                    here = slice(lane - cols.start, lane - cols.start + LANES)
                    pair[tile + lane // LANES, at, :] = terms[: 2 * heads, here] + bar
                    stage[base + lane // LANES, to, :] = terms[2 * heads :, here] + bar
        return carry

    lax.fori_loop(0, part // 8, unit, 0, unroll=UNROLL_F[tile % 4])


def mirror(ref, h, lo, heads, tiles, add):
    for hi in range(lo + 1, tiles):
        near = pl.ds(lo * LANES * heads + h, LANES, stride=heads)
        far = pl.ds(hi * LANES * heads + h, LANES, stride=heads)
        if add:
            ref[hi, near, :] = ref[hi, near, :] + jnp.transpose(ref[lo, far, :])
        else:
            ref[lo, far, :] = jnp.transpose(ref[hi, near, :])


def soft_tile(tile, pair, qt, k, vt, att, ctx_t, bufs, heads, atoms):
    cols = slice(tile * LANES, (tile + 1) * LANES)
    scale = LOG2E / math.sqrt(24)
    together = min(4, heads)

    def step(i, carry):
        for j in range(together):
            h = i * together + j
            mirror(pair, h, tile, heads, atoms // LANES, False)
            bufs[j] = dot(k[...] * head_mask(h, k.shape[1]), qt[:, cols])
        for j in range(together):
            h = i * together + j
            rows = pl.ds(pl.multiple_of(h * PAD, PAD), PAD)
            logits = bufs[j] * scale + pair[tile, pl.ds(h, atoms, stride=heads), :]
            weights = jnp.exp2(logits - jnp.max(logits, axis=0, keepdims=True))
            soft = (weights * (1.0 / jnp.sum(weights, axis=0, keepdims=True))).astype(bf16)
            att[h, :, cols] = soft
            ctx_t[rows, cols] = dot(vt[rows, :], soft).astype(bf16)
        return carry

    lax.fori_loop(0, heads // together, step, 0)


def pieces_of(x):
    a = x.astype(bf16).astype(f32)
    r = x - a
    b = r.astype(bf16).astype(f32)
    return a, b, r - b


def score_part(chip, last, att, q, kt, v, dc, dct, term, bufs, scores, dq_t, dk_sum, dv_sum, heads, atoms):
    span = dc.shape[1]
    tiles = atoms // LANES
    scale = 1.0 / math.sqrt(24)
    start = pl.multiple_of(chip * span, LANES) if span % LANES == 0 else chip * span
    block = pl.ds(start, span)
    together = 2

    def step(i, carry):
        for j in range(together):
            h = i * together + j
            bufs[j] = dot(v[...] * head_mask(h, v.shape[1]), dct[chip])
        for j in range(together):
            h = i * together + j
            mask = head_mask(h, v.shape[1])
            rows = pl.ds(pl.multiple_of(h * PAD, PAD), PAD)
            for part in range(span // LANES):
                cols = slice(part * LANES, (part + 1) * LANES)
                soft = att[h, :, pl.ds(start + part * LANES, LANES)].astype(f32)
                part_sum = soft * bufs[j, :, cols]
                grad = part_sum - soft * jnp.sum(part_sum, axis=0, keepdims=True)
                scores[j, :, cols] = (grad * scale).astype(bf16)
                term[chip * (span // LANES) + part, pl.ds(h, atoms, stride=heads), :] = grad.astype(bf16).astype(f32)
            dq_t[chip, rows, :] = dot(kt[rows, :], scores[j]).astype(bf16)
            dv_sum[...] += dot(att[h, :, block], dc[chip] * mask)
            dk_sum[...] += dot(scores[j], q[block, :] * mask)
            if last:
                for lo in range(tiles):
                    mirror(term, h, lo, heads, tiles, True)
        return carry

    lax.fori_loop(0, heads // together, step, 0)


def moment_tile(tile, begin, end, aux, coords, coef, dist, term, moments, heads, atoms):
    first, width = tile * LANES, atoms - tile * LANES

    def unit(group, carry):
        row0 = pl.multiple_of(first + group * 8, 8)
        dist[:, :width] = distances(row0, aux, coords, first, width)
        total = None
        for row in range(8):
            at = pl.ds(pl.multiple_of((row0 + row) * heads, heads), heads)
            for cols in chunks(width, 2 * LANES):
                lhs = []
                for lane in range(cols.start, cols.stop, LANES):
                    t = term[tile + lane // LANES, at, :].astype(bf16).astype(f32)
                    d = dist[row : row + 1, lane : lane + LANES]
                    x1 = t * d
                    parts = (t,) + pieces_of(x1) + pieces_of(x1 * d) + (jnp.zeros_like(t),)
                    lhs.append(jnp.concatenate(parts, axis=0).astype(bf16))
                lhs = jnp.concatenate(lhs, axis=1) if len(lhs) > 1 else lhs[0]
                out = dot_nt(gauss_value(dist, coef, row, cols), lhs)
                total = out if total is None else total + out
        moments[...] += total
        return carry

    lax.fori_loop(begin, end, unit, 0, unroll=UNROLL_B[tile % 4])


def kernel_grads(moments, means, widths, w, heads):
    kernels = means.shape[1]
    sums = moments[...]
    if sums.shape[1] < LANES:
        sums = jnp.concatenate([sums, jnp.zeros((kernels, LANES - sums.shape[1]), f32)], axis=1)
    flat = jnp.transpose(sums)
    m = [flat[i * heads : (i + 1) * heads] for i in range(7)]
    m0, m1, m2 = m[0], m[1] + m[2] + m[3], m[4] + m[5] + m[6]
    shift = means - CENTRE
    s1 = m1 - shift * m0
    s2 = m2 - 2.0 * shift * m1 + shift * shift * m0
    inv = 1.0 / widths
    mean_grad = jnp.sum(w * s1, axis=0, keepdims=True) * inv * inv
    width_grad = jnp.sum(w * (s2 * inv * inv - m0), axis=0, keepdims=True) * inv
    return m0, mean_grad, width_grad


MESH = pl.DeviceIdType.MESH
epsilon = 1e-05


def remote(src, dst, send, recv, device):
    return pltpu.make_async_remote_copy(
        src_ref=src, dst_ref=dst, send_sem=send, recv_sem=recv, device_id=device, device_id_type=MESH
    )


class Place:
    def __init__(self, nr, nh):
        self.nr, self.nh, self.chips = nr, nh, nh // 2
        self.r, self.h = lax.axis_index("rows"), lax.axis_index("heads")
        self.x, self.c = self.h // 2, lax.rem(self.h, 2)
        self.mate = self.h + 1 - 2 * self.c

    def chip(self, k):
        return lax.rem(self.x + k + self.chips, self.chips)

    def enter(self):
        barrier = pltpu.get_barrier_semaphore()
        for k in range(1, self.nr):
            pl.semaphore_signal(barrier, inc=1, device_id=(lax.rem(self.r + k, self.nr), self.h), device_id_type=MESH)
        for k in range(1, self.nh):
            pl.semaphore_signal(barrier, inc=1, device_id=(self.r, lax.rem(self.h + k, self.nh)), device_id_type=MESH)
        pl.semaphore_wait(barrier, self.nr + self.nh - 2)


class Gather:
    def __init__(self, place, full, send, recv):
        self.place, self.full, self.send, self.recv = place, full, send, recv

    def copy(self, block, to, slot):
        ref = self.full.at[block]
        made = remote(ref, ref, self.send.at[slot], self.recv.at[slot], (self.place.r, to))
        made.start()
        return made

    def start(self):
        p = self.place
        self.along = [self.copy(p.h, p.chip(k) * 2 + p.c, k) for k in range(1, p.chips)]
        self.across = [self.copy(p.h, p.mate, 0)]

    def forward(self):
        p = self.place
        for k in range(1, p.chips):
            self.along[k - 1].wait_recv()
            self.across.append(self.copy(p.chip(-k) * 2 + p.c, p.mate, p.chips - 1 + k))

    def near(self):
        self.across[0].wait_recv()

    def far(self):
        for made in self.across[1:]:
            made.wait_recv()

    def done(self):
        for made in self.along + self.across:
            made.wait_send()


class Scatter:
    def __init__(self, place, out1, in1, keep, out2, in2, send, recv):
        self.place, self.out1, self.in1, self.keep, self.out2, self.in2 = place, out1, in1, keep, out2, in2
        self.send, self.recv = send, recv

    def near(self, xs):
        p = self.place
        return remote(self.out1.at[xs], self.in1.at[xs], self.send.at[xs], self.recv.at[xs], (p.r, p.mate))

    def far(self, xs, cs):
        p = self.place
        return remote(
            self.out2.at[xs], self.in2.at[p.x], self.send.at[p.chips + xs], self.recv.at[p.chips + p.x], (p.r, xs * 2 + cs)
        )

    def put(self, s, value):
        p = self.place
        xs, cs = s // 2, s % 2

        @pl.when(p.c != cs)
        def _():
            self.out1[xs] = value.astype(bf16)
            self.near(xs).start()

        @pl.when(p.c == cs)
        def _():
            self.keep[xs] = value.astype(self.keep.dtype)

    def send_on(self, s):
        p = self.place
        xs, cs = s // 2, s % 2

        @pl.when(jnp.logical_and(p.c == cs, p.x != xs))
        def _():
            self.near(xs).wait_recv()
            self.out2[xs] = (self.keep[xs].astype(f32) + self.in1[xs].astype(f32)).astype(bf16)
            self.far(xs, cs).start()

    def finish(self):
        p = self.place
        self.near(p.x).wait_recv()
        total = self.keep[p.x].astype(f32) + self.in1[p.x].astype(f32)
        for k in range(1, p.chips):
            at = p.chip(k)
            remote(self.out2.at[at], self.in2.at[at], self.send.at[p.chips + at], self.recv.at[p.chips + at], (p.r, p.mate)).wait_recv()
            total = total + self.in2[at].astype(f32)
        for xs in range(p.chips):
            self.near(xs).wait_send()
        for k in range(1, p.chips):
            self.far(p.chip(k), p.c).wait_send()
        return total


class Swap:
    def __init__(self, place, stage, land, send, recv):
        self.place, self.stage, self.land, self.send, self.recv = place, stage, land, send, recv

    def start(self):
        p = self.place
        self.made = []
        for k in range(1, p.nr):
            to = lax.rem(p.r + k, p.nr)
            made = remote(self.stage.at[to], self.land.at[p.r], self.send.at[k], self.recv.at[k], (to, p.h))
            made.start()
            self.made.append(made)
        self.land[p.r] = self.stage[p.r]

    def finish(self):
        for made in self.made:
            made.wait_recv()
        for made in self.made:
            made.wait_send()


def put_blocks(ref, value):
    count, size = ref.shape[0], ref.shape[1]
    for i in range(count):
        ref[i] = value[i * size : (i + 1) * size].astype(ref.dtype)


def take_blocks(ref):
    return jnp.concatenate([ref[i].astype(f32) for i in range(ref.shape[0])], axis=0)


def turn(value, inner):
    rows = value.shape[0]
    outer = rows // inner
    to = lax.broadcasted_iota(jnp.int32, (rows, rows), 0)
    at = lax.broadcasted_iota(jnp.int32, (rows, rows), 1)
    matrix = jnp.where(at == lax.rem(to, outer) * inner + to // outer, 1.0, 0.0).astype(bf16)
    return dot(matrix, value.astype(bf16))


def norm_parts(x):
    centred = x - jnp.mean(x, axis=1, keepdims=True)
    rstd = lax.rsqrt(jnp.mean(centred * centred, axis=1, keepdims=True) + epsilon)
    return centred * rstd, rstd


def norm_back(grad, xhat, rstd, gain):
    dy = grad * gain
    mean1 = jnp.mean(dy, axis=1, keepdims=True)
    mean2 = jnp.mean(dy * xhat, axis=1, keepdims=True)
    return rstd * (dy - mean1 - xhat * mean2)


def column_sum(x):
    return jnp.sum(x, axis=0, keepdims=True)


def flip(x):
    return jnp.transpose(x.astype(f32)).astype(x.dtype)


def pad_heads(parts):
    padded = []
    for part in parts:
        part = part.astype(f32)
        padded += [part, jnp.zeros((PAD - part.shape[0], part.shape[1]), f32)]
    return jnp.concatenate(padded, axis=0).astype(bf16)


class Halve:
    def __init__(self, place, order, data, full, got, send, recv):
        self.place, self.order, self.data, self.full, self.got, self.send, self.recv = place, order, data, full, got, send, recv
        self.n = len(order)
        self.bits = [lax.rem(place.r // 2**bit, 2) for bit in order]
        self.used, self.out = {}, {}

    def device(self, j):
        bit = self.order[j]
        return (self.place.r + 2**bit - 2 ** (bit + 1) * self.bits[j], self.place.h)

    def at(self, flips, length):
        start = 0
        for j in range(length):
            bit = 1 - self.bits[j] if j in flips else self.bits[j]
            start = start + bit * 2 ** (self.n - 1 - j)
        return pl.ds(start, 2 ** (self.n - length))

    def made(self, src, dst, key, j):
        slot = self.used.setdefault(key, len(self.used))
        return remote(src, dst, self.send.at[slot], self.recv.at[slot], self.device(j))

    def piece(self, j, part):
        size = 2 ** (self.n - 1 - j)
        base = 2**self.n - 2 * size
        if part == 2:
            src, land = self.at((j,), j + 1), pl.ds(base, size)
        else:
            src = self.at((j, j + 1) if part == 0 else (j,), j + 2)
            land = pl.ds(base + part * (size // 2), size // 2)
        return self.made(self.data.at[src], self.got.at[land], ("r", j, part), j), land

    def parts(self, j):
        return (2,) if j == self.n - 1 else (0, 1)

    def start(self, j=0):
        for part in self.parts(j):
            self.out[j, part] = self.piece(j, part)
            self.out[j, part][0].start()

    def add(self, j, part):
        copy, land = self.out[j, part]
        copy.wait_recv()
        mine = self.at((), j + 1) if part == 2 else self.at((j + 1,) if part == 0 else (), j + 2)
        self.data[mine] = (self.data[mine].astype(f32) + self.got[land].astype(f32)).astype(bf16)

    def reduce(self, *steps):
        for j in steps:
            if j:
                self.add(j - 1, 1)
            self.add(j, self.parts(j)[0])
            if j < self.n - 1:
                self.start(j + 1)

    def slab(self, flips):
        return self.full.at[self.at(flips, self.n)]

    def give(self, flips, j):
        ref = self.slab(flips)
        made = self.made(ref, ref, ("g", flips, j), j)
        made.start()
        self.out["g", flips, j] = made

    def hand(self):
        mine = self.at((), self.n)
        self.full[mine] = self.data[mine]
        self.have = [()]
        for j in range(self.n - 1, -1, -1):
            self.give((), j)

    def relay(self, *steps):
        for step in steps:
            j = self.n - 1 - step
            news = []
            for flips in self.have:
                self.out["g", flips, j].wait_recv()
                new = tuple(sorted(flips + (j,)))
                for i in range(j - 1, -1, -1):
                    self.give(new, i)
                news.append(new)
            self.have = self.have + news

    def finish(self):
        self.relay(self.n - 1)
        for key, made in self.out.items():
            (made if key[0] == "g" else made[0]).wait_send()


def share(nh, h, value, shard):
    picked = value[:, :shard]
    for j in range(1, nh):
        picked = jnp.where(h == j, value[:, j * shard : (j + 1) * shard], picked)
    return picked


def widen(value):
    lanes = value.shape[1]
    return value if lanes == LANES else jnp.concatenate([value, jnp.zeros((value.shape[0], LANES - lanes), f32)], axis=1)


def row_of(ref):
    return ref[...].reshape(1, ref.shape[0])


def fold(value, rows):
    half = value.shape[1] // 2
    return value if value.shape[0] == rows else jnp.concatenate([value[:, :half], value[:, half:]], axis=0)


def unfold(value, rows):
    return value if value.shape[0] == rows else jnp.concatenate([value[:rows], value[rows:]], axis=1)


def gelu_parts(x):
    below = 0.5 * (1.0 + lax.erf(x * math.sqrt(0.5)))
    return x * below, below + x * (jnp.exp(-0.5 * x * x) * (1.0 / math.sqrt(2.0 * math.pi)))


def layer_kernel(nr, nh, names, *refs):
    g = types.SimpleNamespace(**dict(zip(names, refs)))
    place = Place(nr, nh)
    chips, shard, width = g.keep.shape
    heads, atoms = g.att.shape[0], g.att.shape[1]
    x_in, c_in = g.keep.at[0], g.keep.at[1]
    tiles = atoms // LANES
    kernels, size = g.wk_t.shape[1], g.w_qkv.shape[2]
    units = g.w_up.shape[1]
    at = pl.ds(pl.multiple_of(place.h * shard, shard), shard)
    loads = [pltpu.make_async_copy(g.states.at[at], x_in, g.copy_sem.at[0]), pltpu.make_async_copy(g.cots.at[at], c_in, g.copy_sem.at[1])]
    for load in loads:
        load.start()
    fills = {}
    for i, name in enumerate(("w_time", "w_out", "w_qkv", "w_up", "w_down")):
        fills[name] = pltpu.make_async_copy(getattr(g, name + "_hbm"), getattr(g, name), g.fill_sem.at[i])
        fills[name].start()
    place.enter()
    for name in ("w_time", "w_out", "w_qkv"):
        fills[name].wait()

    g.wk_own[...] = g.wk_t[...].astype(f32)
    swap_w = remote(g.wk_own, g.wk_mate, g.s_wk.at[0], g.r_wk.at[0], (place.r, place.mate))
    swap_w.start()
    g.wo[place.h] = pad_heads([g.w_out[h] for h in range(heads)])
    gather_w = Gather(place, g.wo, g.s_wo, g.r_wo)
    gather_w.start()

    half = g.w_time.shape[0] // 2
    row = widen(share(nh, place.h, row_of(g.steps).astype(f32), shard))
    frequency = jnp.exp(lax.broadcasted_iota(jnp.int32, (half, 1), 0).astype(f32) * (-math.log(10000.0) / half))
    angles = frequency * row
    terms = jnp.transpose(jnp.concatenate([jnp.sin(angles), jnp.cos(angles)], axis=0))[:shard].astype(bf16)
    for load in loads:
        load.wait()
    zero = x_in[...] + dot(terms, g.w_time[...])
    put_blocks(g.stage_x, turn(zero, nr))
    swap_x = Swap(place, g.stage_x, g.land_x, g.s_x, g.r_x)
    swap_x.start()

    cots = share(nh, place.h, g.cot_forces[...], shard).astype(bf16).astype(f32)
    force = jnp.transpose(widen(jnp.concatenate([cots, jnp.zeros((LANES - 3, shard), f32)], axis=0)))[:shard]
    grad_two = c_in[...]
    for j in range(3):
        grad_two = grad_two + force[:, j : j + 1] * g.w_force[j : j + 1, :].astype(f32)
    put_blocks(g.stage_g, turn(jnp.concatenate([grad_two.astype(bf16), terms], axis=1), nr))
    swap_g = Swap(place, g.stage_g, g.land_g, g.s_g, g.r_g)
    swap_g.start()

    ids = g.item_ids[...].astype(f32)
    g.ids[...] = ids
    g.aux[...] = jnp.transpose(jnp.concatenate([g.coords[...], ids, jnp.zeros((LANES - 4, atoms), f32)], axis=0))
    means, widths = row_of(g.means), row_of(g.widths)
    columns = [jnp.transpose(jnp.broadcast_to(value, (LANES, kernels))) for value in (means, widths)]
    gauss_coefs(columns[0], columns[1], g.coef)
    swap_w.wait_recv()
    g.spread[...] = spread_weights(g.wk_own[...], g.wk_mate[...])
    for part in range(3):
        g.weight[part] = pad_heads([g.w_qkv[h, part] for h in range(heads)])

    bases = [sum(tiles - i for i in range(tile)) for tile in range(tiles + 1)]
    crossed = []

    def pair_terms(tile):
        pair_tile(tile, place.c, g.aux, g.coords, g.ids, g.coef, g.dist, g.pair, g.stage, bases[tile], g.spread, heads, atoms)
        rows = pl.ds(pl.multiple_of((tile * LANES + place.c * (LANES // 2)) * heads, LANES // 2), (LANES // 2) * heads)
        src = g.stage.at[bases[tile] : bases[tile + 1]]
        made = remote(src, g.pair.at[tile:tiles, rows], g.s_pr.at[tile], g.r_pr.at[tile], (place.r, place.mate))
        made.start()
        crossed.append(made)

    pair_terms(0)
    swap_x.finish()
    g.x0[place.h] = turn(take_blocks(g.land_x), shard // nr).astype(bf16)
    gather_x = Gather(place, g.x0, g.s_x0, g.r_x0)
    gather_x.start()
    gather_w.forward()
    swap_g.finish()
    both = turn(take_blocks(g.land_g), shard // nr).astype(bf16)
    g.gt[place.h] = both[:, :width]
    g.tt[...] = both[:, width:]
    pair_terms(1)
    gather_x.forward()
    gather_t = Gather(place, g.gt, g.s_gt, g.r_gt)
    gather_t.start()
    for tile in range(2, tiles):
        pair_terms(tile)
    gather_x.near()
    gather_x.far()
    gather_x.done()
    for s in range(nh):
        xhat, _ = norm_parts(g.x0[s].astype(f32))
        g.n1[s] = (xhat * row_of(g.gain1) + row_of(g.bias1)).astype(bf16)
    normed = g.n1[...].reshape(atoms, width)
    g.qt[...] = dot_nt(g.weight[0], normed).astype(bf16)
    g.kt[...] = dot_nt(g.weight[1], normed).astype(bf16)
    g.vt[...] = dot_nt(g.weight[2], normed).astype(bf16)
    g.q[...] = dot_nt(normed, g.weight[0]).astype(bf16)
    g.k[...] = dot_nt(normed, g.weight[1]).astype(bf16)
    g.v[...] = dot_nt(normed, g.weight[2]).astype(bf16)
    gather_t.forward()
    gather_t.near()
    gather_t.far()
    gather_w.near()
    gather_w.far()

    for made in crossed:
        made.wait_recv()
    gathers = []
    for tile in range(tiles):
        soft_tile(tile, g.pair, g.qt, g.k, g.vt, g.att, g.ctx_t, g.bufs, heads, atoms)
        g.ctx[tile, place.h] = flip(g.ctx_t[:, tile * LANES : (tile + 1) * LANES])
        gathers.append(Gather(place, g.ctx.at[tile], g.s_cx.at[tile], g.r_cx.at[tile]))
        gathers[-1].start()
        if tile:
            gathers[-2].forward()

    fills["w_up"].wait()
    fills["w_down"].wait()
    sum_b = Scatter(place, g.o1b, g.i1b, g.keep, g.o2b, g.i2b, g.s_b, g.r_b)
    each = LANES // shard
    for tile in range(tiles):
        pieces = [tile * each + i for i in range(each)]

        def rows_of(ref):
            return ref[tile] if each == 1 else jnp.concatenate([ref[s] for s in pieces], axis=0)

        def store(ref, value):
            for i, s in enumerate(pieces):
                ref[s] = value[i * shard : (i + 1) * shard].astype(ref.dtype)

        if tile == tiles - 1:
            gathers[-1].forward()
        back = dot_nt(rows_of(g.gt), g.w_down[...])
        gathers[tile].near()
        gathers[tile].far()
        one = rows_of(g.x0).astype(f32)
        for j in range(nh):
            one = one + dot(g.ctx[tile, j], g.wo[j])
        store(g.one, one)
        xhat, _ = norm_parts(one)
        normed = (xhat * row_of(g.gain2) + row_of(g.bias2)).astype(bf16)
        store(g.n2, normed)
        act, slope = gelu_parts(dot(normed, g.w_up[...]))
        store(g.hidden, act)
        pre_grad = (back * slope).astype(bf16)
        store(g.pre_grad, pre_grad)
        value = dot_nt(pre_grad, g.w_up[...])
        for i, s in enumerate(pieces):
            sum_b.put(s, value[i * shard : (i + 1) * shard])
        if tile:
            for s in range((tile - 1) * each, tile * each):
                sum_b.send_on(s)

    bits = list(range(nr.bit_length() - 1))
    total_down = Halve(place, [1, 0] + bits[2:], g.down, g.down_out, g.down_got, g.s_dn, g.r_dn)
    total_up = Halve(place, bits, g.up, g.up_out, g.up_got, g.s_up, g.r_up)
    total_qo = Halve(place, [1, 0] + bits[2:], g.qo, g.qo_out, g.qo_got, g.s_qo, g.r_qo)
    steps = bits
    g.down[...] = dot(flip(g.hidden[...].reshape(atoms, units)), g.gt[...].reshape(atoms, width)).astype(bf16).reshape(g.down.shape)
    total_down.start()
    for s in range((tiles - 1) * each, tiles * each):
        sum_b.send_on(s)
    g.up[...] = dot(flip(g.n2[...].reshape(atoms, width)), g.pre_grad[...].reshape(atoms, units)).astype(bf16).reshape(g.up.shape)
    total_up.start()
    normed_grad = sum_b.finish()
    xhat, rstd = norm_parts(g.one[place.h])
    one_grad = g.gt[place.h].astype(f32) + norm_back(normed_grad, xhat, rstd, row_of(g.gain2))
    g.one_grad[...] = one_grad
    g.og[place.h] = one_grad.astype(bf16)
    gather_o = Gather(place, g.og, g.s_og, g.r_og)
    gather_o.start()
    g.sums[0:1, :] = column_sum(normed_grad * xhat)
    g.sums[1:2, :] = column_sum(normed_grad)
    g.dk_sum[...] = jnp.zeros_like(g.dk_sum)
    g.dv_sum[...] = jnp.zeros_like(g.dv_sum)

    def out_grads(chip):
        for c in range(2):
            s = chip * 2 + c
            at = slice(c * shard, (c + 1) * shard)
            g.dc[chip, at, :] = dot_nt(g.og[s], g.wo[place.h]).astype(bf16)
        grads = jnp.concatenate([g.og[chip * 2], g.og[chip * 2 + 1]], axis=0)
        g.dct[chip] = dot_nt(g.wo[place.h], grads).astype(bf16)

    def scores(chip, last):
        score_part(chip, last, g.att, g.q, g.kt, g.v, g.dc, g.dct, g.pair, g.bufs2, g.scores, g.dq_t, g.dk_sum, g.dv_sum, heads, atoms)

    gather_o.near()
    out_grads(place.x)
    scores(place.x, False)
    gather_o.forward()
    total_down.reduce(0)
    total_up.reduce(0)
    gather_o.far()
    for k in range(1, chips):
        out_grads(place.chip(k))
        scores(place.chip(k), k == chips - 1)

    total_down.reduce(*steps[1:-1])
    total_up.reduce(*steps[1:-1])
    dq_t = jnp.concatenate([g.dq_t[x] for x in range(chips)], axis=1)
    g.dq[...] = flip(dq_t).reshape(g.dq.shape)
    g.dk[...] = g.dk_sum[...].astype(bf16).reshape(g.dk.shape)
    g.dv[...] = g.dv_sum[...].astype(bf16).reshape(g.dv.shape)
    normed = g.n1[...].reshape(atoms, width)
    for i, grad in enumerate((dq_t, flip(g.dk[...].reshape(atoms, -1)), flip(g.dv[...].reshape(atoms, -1)))):
        g.parts[i] = dot(grad, normed).astype(bf16)
    g.parts[3] = dot(g.ctx_t[...], g.og[...].reshape(atoms, width)).astype(bf16)
    chosen = [(i, h) for h in range(heads) for i in range(3)] + [(3, h) for h in range(heads)]
    flat = [g.parts[i, h * PAD : (h + 1) * PAD, :].astype(f32)[:size] for i, h in chosen]
    slab = g.qo.shape[1]
    for f in range(nr):
        first, last = f * slab // size, -(-(f + 1) * slab // size)
        rows = jnp.concatenate(flat[first:last], axis=0) if last - first > 1 else flat[first]
        begin = f * slab - first * size
        g.qo[f] = rows[begin : begin + slab].astype(bf16)

    total_qo.start()
    sum_n = Scatter(place, g.o1b, g.i1b, g.keep, g.o2b, g.i2b, g.s_n, g.r_n)
    for s in range(nh):
        sum_n.put(s, dot(g.dq[s], g.weight[0]) + dot(g.dk[s], g.weight[1]) + dot(g.dv[s], g.weight[2]))

    g.moments[...] = jnp.zeros_like(g.moments)
    groups = LANES // 8

    def moments(tile, begin, end):
        moment_tile(tile, begin, end, g.aux, g.coords, g.coef, g.dist, g.pair, g.moments, heads, atoms)

    moments(0, 0, groups // 2)
    for s in range(nh):
        sum_n.send_on(s)
    for total in (total_down, total_up):
        total.reduce(steps[-1])
        total.hand()
    moments(0, groups // 2, groups)
    total_qo.reduce(0)

    grad_n = sum_n.finish()
    xhat, rstd = norm_parts(g.x0[place.h].astype(f32))
    gs = (g.one_grad[...] + norm_back(grad_n, xhat, rstd, row_of(g.gain1))).astype(bf16)
    put_blocks(g.stage_d, turn(gs, nr))
    swap_d = Swap(place, g.stage_d, g.land_d, g.s_d, g.r_d)
    swap_d.start()
    put_blocks(g.time_mine, dot(flip(g.tt[...]), gs))
    time_one = []
    for k in range(1, nh):
        to = lax.rem(place.h + k, nh)
        made = remote(g.time_mine.at[to], g.time_part.at[k], g.s_t1.at[k], g.r_t1.at[k], (place.r, to))
        made.start()
        time_one.append(made)
    total_down.relay(0)
    total_up.relay(0)
    moments(1, 0, groups // 2)

    sum_c = Scatter(place, g.o1a, g.i1a, g.keep_c, g.o2a, g.i2a, g.s_c, g.r_c)
    for s in range(nh):
        sum_c.put(s, dot(g.hidden[s], g.w_down[...]))
    total_qo.reduce(*steps[1:-1])
    for s in range(nh):
        sum_c.send_on(s)
    moments(1, groups // 2, groups)
    total_down.relay(*steps[1:-1])
    total_up.relay(*steps[1:-1])
    swap_d.finish()
    g.gs_out[place.h] = turn(take_blocks(g.land_d), shard // nr).astype(bf16)
    gather_d = Gather(place, g.gs_out, g.s_fd, g.r_fd)
    gather_d.start()
    piece = g.time_mine.shape[1] // nr
    quarter = g.time_mine[place.h].astype(f32)
    for k in range(1, nh):
        time_one[k - 1].wait_recv()
        quarter = quarter + g.time_part[k].astype(f32)
    for i in range(nr):
        g.time_land[0, i] = fold(quarter[i * piece : (i + 1) * piece], g.time_land.shape[2]).astype(bf16)
    time_two = []
    for k in range(1, nr):
        to = lax.rem(place.r + k, nr)
        made = remote(g.time_land.at[0, to], g.time_land.at[1, k], g.s_t2.at[k], g.r_t2.at[k], (to, place.h))
        made.start()
        time_two.append(made)
    two = (g.one[place.h] + sum_c.finish()).astype(bf16)
    put_blocks(g.stage_x, turn(two, nr))
    swap_s = Swap(place, g.stage_x, g.land_s, g.s_s, g.r_s)
    swap_s.start()
    moments(2, 0, groups)
    total_qo.reduce(steps[-1])
    total_qo.hand()
    for tile in range(3, tiles):
        moments(tile, 0, groups)
    gather_d.forward()
    mine = g.time_land[0, place.r].astype(f32)
    for k in range(1, nr):
        time_two[k - 1].wait_recv()
        mine = mine + g.time_land[1, k].astype(f32)
    g.time_full[place.h, place.r] = mine.astype(bf16)
    time_three = []
    for k in range(1, nr):
        to = lax.rem(place.r + k, nr)
        ref = g.time_full.at[place.h, place.r]
        made = remote(ref, ref, g.s_t3.at[k], g.r_t3.at[k], (to, place.h))
        made.start()
        time_three.append(made)
    swap_s.finish()
    g.states_out[place.h] = turn(take_blocks(g.land_s), shard // nr).astype(bf16)
    gather_s = Gather(place, g.states_out, g.s_fs, g.r_fs)
    gather_s.start()

    fields = jnp.concatenate([cots, jnp.zeros((5, shard), f32)], axis=0).astype(bf16)
    force_grad = dot(fields, g.states_out[place.h])
    kernel_sums = kernel_grads(g.moments, means, widths, g.wk_t[...].astype(f32), heads)
    wide = jnp.concatenate([kernel_sums[1], kernel_sums[2], jnp.zeros((1, width - 2 * kernels), f32)], axis=1)
    g.one_all[place.h] = jnp.concatenate([force_grad[0:3], g.sums[...], column_sum(grad_n * xhat), column_sum(grad_n), wide], axis=0)
    ones = []
    for k in range(1, nh):
        to = lax.rem(place.h + k, nh)
        ref = g.one_all.at[place.h]
        made = remote(ref, ref, g.s_m1.at[k], g.r_m1.at[k], (place.r, to))
        made.start()
        ones.append(made)
    total_qo.relay(0)
    for made in ones:
        made.wait_recv()
    summed = g.one_all[0]
    for j in range(1, nh):
        summed = summed + g.one_all[j]
    g.row_all[place.r, :, 0:width] = summed
    g.row_all[place.r, :, width:] = jnp.concatenate([kernel_sums[0], jnp.zeros((8 - heads, kernels), f32)], axis=0) if heads < 8 else kernel_sums[0]
    rows = []
    for k in range(1, nr):
        to = lax.rem(place.r + k, nr)
        ref = g.row_all.at[place.r]
        made = remote(ref, ref, g.s_m2.at[k], g.r_m2.at[k], (to, place.h))
        made.start()
        rows.append(made)
    gather_s.forward()
    total_qo.relay(*steps[1:-1])
    for made in time_three:
        made.wait_recv()
    time_four = []
    for k in range(1, nh):
        to = lax.rem(place.h + k, nh)
        ref = g.time_full.at[place.h]
        made = remote(ref, ref, g.s_t4.at[k], g.r_t4.at[k], (place.r, to))
        made.start()
        time_four.append(made)

    stores = []

    def keep_result(name):
        made = pltpu.make_async_copy(getattr(g, name), getattr(g, name + "_hbm"), g.out_sem.at[len(stores)])
        made.start()
        stores.append(made)

    gather_s.near()
    gather_s.far()
    keep_result("states_out")
    fields = jnp.concatenate([g.w_force[...].astype(f32), jnp.zeros((5, width), f32)], axis=0).astype(bf16)
    g.forces_out[...] = dot_nt(fields, g.states_out[...].reshape(atoms, width))
    gather_d.near()
    gather_d.far()
    keep_result("gs_out")
    for made in time_four:
        made.wait_recv()
    for j in range(nh):
        for i in range(nr):
            base = (j * nr + i) * piece
            g.time_out[base : base + piece, :] = unfold(g.time_full[j, i].astype(f32), piece)
    for made in rows:
        made.wait_recv()
    total = g.row_all[0]
    for j in range(1, nr):
        total = total + g.row_all[j]
    g.small_out[...] = total
    for gather in gathers + [gather_t, gather_w, gather_o, gather_s, gather_d]:
        gather.done()
    for group in ([swap_w], crossed, time_one, time_two, time_three, time_four, ones, rows):
        for made in group:
            made.wait_send()
    total_down.finish()
    keep_result("down_out")
    total_up.finish()
    keep_result("up_out")
    total_qo.finish()
    keep_result("qo_out")
    for made in stores:
        made.wait()


def last_kernel(
    up, down, qkv, wout, states, grads, time, small, forces,
    states_out, forces_out, grads_out, time_out, gain1_out, bias1_out, qkv_out, wk_out, means_out, widths_out, wout_out,
    gain2_out, bias2_out, up_out, down_out, force_out,
):
    kernels, width = means_out.shape[0], up.shape[0] * 0 + gain1_out.shape[0]
    up_out[...] = up[...].astype(f32)
    down_out[...] = down[...].astype(f32)
    states_out[...] = states[...].astype(f32)
    grads_out[...] = grads[...].astype(f32)
    time_out[...] = time[...]
    qkv_out[...] = qkv[...].astype(f32).reshape(qkv_out.shape)
    wout_out[...] = wout[...].astype(f32).reshape(wout_out.shape)

    @pl.when(pl.program_id(0) == 0)
    def _():
        forces_out[...] = forces[0:3, :]
        force_out[...] = small[0:3, 0:width]
        gain2_out[...] = small[3, 0:width]
        bias2_out[...] = small[4, 0:width]
        gain1_out[...] = small[5, 0:width]
        bias1_out[...] = small[6, 0:width]
        means_out[...] = small[7, 0:kernels]
        widths_out[...] = small[7, kernels : 2 * kernels]
        wk_out[...] = small[0 : wk_out.shape[0], width:]


VM = pl.BlockSpec(memory_space=pltpu.VMEM)
ANY = pl.BlockSpec(memory_space=pl.ANY)


def S(shape, dtype):
    return jax.ShapeDtypeStruct(shape, dtype)


def V(shape, dtype):
    return pltpu.VMEM(shape, dtype)


def body(
    nr,
    nh,
    atom_states,
    time_steps,
    coords,
    item_ids,
    w_time,
    ln1_gain,
    ln1_bias,
    w_qkv,
    w_kernel,
    kernel_means,
    kernel_widths,
    w_out,
    ln2_gain,
    ln2_bias,
    w_up,
    w_down,
    w_force,
    cot_states,
    cot_forces,
):
    atoms, width = atom_states.shape
    heads, head_dim = w_qkv.shape[1], w_qkv.shape[3]
    kernels, freqs, units = w_kernel.shape[0], w_time.shape[0], w_up.shape[1]
    shard, tiles = atoms // nh, atoms // LANES
    chips, wide, group = nh // 2, heads * PAD, atoms // nr // nh
    lanes = 2 * chips - 1
    rows_qo = heads * 4 * head_dim
    quarter = freqs // nh
    piece = quarter // nr
    folded = (2 * piece, width // 2) if piece % 8 == 0 else (piece, width)
    inputs = dict(
        states=(atom_states, ANY), cots=(cot_states, ANY), steps=(time_steps, VM), cot_forces=(cot_forces, VM), w_time_hbm=(w_time, ANY),
        w_force=(w_force, VM), gain1=(ln1_gain, VM), bias1=(ln1_bias, VM), gain2=(ln2_gain, VM), bias2=(ln2_bias, VM),
        w_qkv_hbm=(jnp.transpose(w_qkv, (1, 2, 3, 0)), ANY), w_out_hbm=(w_out, ANY), w_up_hbm=(w_up, ANY), w_down_hbm=(w_down, ANY),
        coords=(coords, VM), item_ids=(item_ids, VM), wk_t=(w_kernel.T, VM), means=(kernel_means, VM), widths=(kernel_widths, VM),
    )
    up_shape, down_shape, qo_shape = (nr, width // nr, units), (nr, units // nr, width), (nr, rows_qo // nr, width)
    outputs = dict(
        up_out_hbm=S(up_shape, bf16), down_out_hbm=S(down_shape, bf16), qo_out_hbm=S(qo_shape, bf16), states_out_hbm=S((nh, shard, width), bf16),
        forces_out=S((8, atoms), f32), gs_out_hbm=S((nh, shard, width), bf16), time_out=S((freqs, width), f32),
        small_out=S((8, width + kernels), f32),
    )
    block, three = V((nh, shard, width), bf16), (nh, shard, units)
    rows_t, rows_s = V((wide, atoms), bf16), V((atoms, wide), bf16)
    split = V((nh, shard, wide), bf16)
    land = V((nr, group, width), bf16)
    scratch = dict(
        keep=V((chips, shard, width), f32), keep_c=V((chips, shard, width), bf16), x0=block, one=V((nh, shard, width), f32),
        one_grad=V((shard, width), f32), stage_x=land, land_x=land, land_s=land, stage_d=land, land_d=land,
        stage_g=V((nr, group, width + freqs), bf16), land_g=V((nr, group, width + freqs), bf16), tt=V((shard, freqs), bf16),
        ids=V((1, atoms), f32), aux=V((atoms, LANES), f32), coef=V((3, kernels, LANES), f32), dist=V((8, atoms), f32),
        pair=V((tiles, atoms * heads, LANES), f32), spread=V((heads * 4, 2 * kernels), bf16), wk_own=V((heads, kernels), f32), wk_mate=V((heads, kernels), f32),
        stage=V((tiles * (tiles + 1) // 2, LANES // 2 * heads, LANES), f32), bufs=V((min(4, heads), atoms, LANES), f32), bufs2=V((2, atoms, atoms // chips), f32), scores=V((2, atoms, atoms // chips), bf16),
        weight=V((3, wide, width), bf16), wo=V((nh, wide, width), bf16), att=V((heads, atoms, atoms), bf16),
        n1=block, gt=block, n2=block, og=block,
        qt=rows_t, kt=rows_t, vt=rows_t, ctx_t=rows_t, dct=V((chips, wide, atoms // chips), bf16), dq_t=V((chips, wide, atoms // chips), bf16), q=rows_s, k=rows_s, v=rows_s,
        dc=V((chips, atoms // chips, wide), bf16),
        ctx=V((tiles, nh, LANES, wide), bf16), dq=split, dk=split, dv=split, hidden=V(three, bf16), pre_grad=V(three, bf16),
        dk_sum=V((atoms, wide), f32), dv_sum=V((atoms, wide), f32),
        moments=V((kernels, 8 * heads), f32), sums=V((2, width), f32), parts=V((4, wide, width), bf16),
        time_mine=V((nh, quarter, width), bf16), time_part=V((nh, quarter, width), bf16), time_land=V((2, nr) + folded, bf16),
        time_full=V((nh, nr) + folded, bf16), row_all=V((nr, 8, width + kernels), f32), one_all=V((nh, 8, width), f32),
        w_time=V(w_time.shape, bf16), w_out=V(w_out.shape, bf16), w_up=V(w_up.shape, bf16), w_down=V(w_down.shape, bf16),
        w_qkv=V((heads, 3, head_dim, width), bf16), fill_sem=pltpu.SemaphoreType.DMA((5,)),
        up_out=V(up_shape, bf16), down_out=V(down_shape, bf16), qo_out=V(qo_shape, bf16), states_out=block, gs_out=block,
        out_sem=pltpu.SemaphoreType.DMA((5,)),
        copy_sem=pltpu.SemaphoreType.DMA((2,)),
    )
    for letter in "ab":
        for name in ("o1", "i1"):
            scratch[name + letter] = V((chips, shard, width), bf16)
        for name in ("o2", "i2"):
            scratch[name + letter] = V((chips, shard, width), bf16)
    for name, shape in (("up", up_shape), ("down", down_shape), ("qo", qo_shape)):
        scratch[name] = V(shape, bf16)
        scratch[name + "_got"] = V(shape, bf16)
    counts = dict(wo=lanes, x0=lanes, gt=lanes, og=lanes, fs=lanes, fd=lanes, b=2 * chips, c=2 * chips, n=2 * chips)
    counts.update(wk=1, pr=tiles, x=nr, g=nr, s=nr, d=nr, t1=nh, t2=nr, t3=nr, t4=nh, m1=nh, m2=nr, up=4 * nr, dn=4 * nr, qo=4 * nr)
    for name, count in counts.items():
        scratch["s_" + name] = pltpu.SemaphoreType.DMA((count,))
        scratch["r_" + name] = pltpu.SemaphoreType.DMA((count,))
    for letter in "sr":
        scratch[letter + "_cx"] = pltpu.SemaphoreType.DMA((tiles, lanes))
    names = list(inputs) + list(outputs) + list(scratch)
    up, down, qo, states, forces, grads, time, small = pl.pallas_call(
        functools.partial(layer_kernel, nr, nh, names),
        out_shape=tuple(outputs.values()),
        in_specs=[spec for _, spec in inputs.values()],
        out_specs=tuple(ANY if name.endswith("_hbm") else VM for name in outputs),
        scratch_shapes=list(scratch.values()),
        name="layer",
        compiler_params=pltpu.CompilerParams(collective_id=1, has_side_effects=True, vmem_limit_bytes=VMEM_MIB << 20),
    )(*[array for array, _ in inputs.values()])

    def rows(n, lanes_):
        return pl.BlockSpec((n, lanes_), lambda i: (i, 0))

    def whole(*shape):
        return pl.BlockSpec(shape, lambda i: (0,) * len(shape))

    qkv_rows = heads * 3 * head_dim
    flat = qo.reshape(rows_qo, width)
    steps = 4
    part = heads // steps
    results = pl.pallas_call(
        last_kernel,
        grid=(steps,),
        out_shape=(
            S((atoms, width), f32), S((3, atoms), f32), S((atoms, width), f32), S((freqs, width), f32), S((width,), f32), S((width,), f32),
            S((heads, 3, head_dim, width), f32), S((heads, kernels), f32), S((kernels,), f32), S((kernels,), f32),
            S((heads, head_dim, width), f32), S((width,), f32), S((width,), f32), S((width, units), f32), S((units, width), f32),
            S((3, width), f32),
        ),
        in_specs=[
            rows(width // steps, units), rows(units // steps, width), rows(qkv_rows // steps, width),
            pl.BlockSpec((heads * head_dim // steps, width), lambda i: (i + 3 * steps, 0)),
            rows(atoms // steps, width), rows(atoms // steps, width), rows(freqs // steps, width), whole(8, width + kernels), whole(8, atoms),
        ],
        out_specs=(
            rows(atoms // steps, width), whole(3, atoms), rows(atoms // steps, width), rows(freqs // steps, width), whole(width), whole(width),
            pl.BlockSpec((part, 3, head_dim, width), lambda i: (i, 0, 0, 0)), whole(heads, kernels), whole(kernels), whole(kernels),
            pl.BlockSpec((part, head_dim, width), lambda i: (i, 0, 0)), whole(width), whole(width),
            rows(width // steps, units), rows(units // steps, width), whole(3, width),
        ),
        name="last",
    )(up.reshape(width, units), down.reshape(units, width), flat, flat, states.reshape(atoms, width), grads.reshape(atoms, width), time, small, forces)
    results = list(results)
    results[6] = jnp.transpose(results[6], (3, 0, 1, 2))
    results[7] = results[7].T
    return tuple(results)


def solution(mesh):
    in_specs = (
        P("rows", None),
        P("rows"),
        P(None, "rows"),
        P("rows", None),
        P(),
        P(),
        P(),
        P(None, "heads", None, None),
        P(None, "heads"),
        P(),
        P(),
        P("heads", None, None),
        P(),
        P(),
        P(None, "heads"),
        P("heads", None),
        P(),
        P("rows", None),
        P(None, "rows"),
    )
    out_specs = (
        P("rows", None),
        P(None, "rows"),
        P("rows", None),
        P(),
        P(),
        P(),
        P(None, "heads", None, None),
        P(None, "heads"),
        P(),
        P(),
        P("heads", None, None),
        P(),
        P(),
        P(None, "heads"),
        P("heads", None),
        P(),
    )
    step = functools.partial(body, mesh.shape["rows"], mesh.shape["heads"])
    return jax.shard_map(step, mesh=mesh, in_specs=in_specs, out_specs=out_specs, check_vma=False)
```
